128 devices in a mesh: dp: 4 (over z), expert: 32 (over x, y, core).
Axes of the slice: x: 4, y: 4, z: 4, core: 2. Of those that a mesh axis runs over, the one named last changes fastest.
Arguments:
- tokens: bfloat16 [16384, 2048], P(('dp', 'expert')), may hold values from -24 to 24
- routes: int32 [16384, 4], P(('dp', 'expert')), may hold values from 0 to 31, all different within a row; in each aligned block of 128 rows (0 to 127, 128 to 255, ...) at most 20 rows name the same one
- gates: float32 [16384, 4], P(('dp', 'expert')), may hold values from 0.05 to 0.5
- gate_up: bfloat16 [32, 2048, 2816], P('expert'), may hold values from -0.125 to 0.125
- down_proj: bfloat16 [32, 1408, 2048], P('expert'), may hold values from -0.15625 to 0.15625
- projection: bfloat16 [2048, 512], replicated, may hold values from -0.125 to 0.125
- matches: int32 [128, 128], P(('dp', 'expert')), may hold values from 0 to 127, each once within a row
Outputs:
- grad_tokens: bfloat16 [16384, 2048], P(('dp', 'expert'))
- grad_projection: float32 [2048, 512], P(('dp', 'expert'))
- row_loss: float32 [16384], P(('dp', 'expert'))
The draws below stay inside these ranges and needn't reach their ends.
Inputs may be any that keep to these rules, and one draw needn't show every extreme that they name: `routes`: each row names 4 different experts; within the rows of one device no expert is named more than 20 times, a bound that some block reaches. `matches`: within each patch the entries are a permutation of 0 to 127.
All inputs are finite; a program needn't handle non-finite values.
Results may differ from the reference program's by a relative error of at most 0.011.
Values may be sent and summed in bfloat16 or wider, within the bound.
No kernel may reach another device: no remote copies, remote signals or barrier semaphores. Data moves between devices by JAX's collectives and lax.ppermute only.
A program may use at most 128 MiB of HBM per device.

```python
import math
import jax
import jax.numpy as jnp
import numpy as np
from jax import lax

D = 2048
FFH = 1408
EMB = 512
TOP = 4
PATCH = 128
TOK_DEV = 128
EXPERTS = 32
CAP = 20
TOKENS = 16384
PATCHES = 128
N_DP = 4
N_EXPERT = 32


def spiked(drawn, stream_key, source, target, blocks, factor):
    owner, partner = [(jnp.arange(drawn.shape[dim]) // (drawn.shape[dim] // blocks)).reshape([-1 if axis == dim else 1 for axis in range(drawn.ndim)]) for dim in (source, target)]
    chosen = jax.random.permutation(stream_key, blocks)[partner]
    strong = (owner == chosen) | (owner == (partner + blocks // 2) % blocks)
    return jnp.where(strong, factor * drawn, drawn)


def levels(own_key, shape, split, smallest, high):
    gain = 1.0
    for axis_at, blocks in split:
        draws = jax.random.uniform(jax.random.fold_in(jax.random.fold_in(own_key, 6), axis_at), (blocks,), jnp.float32, smallest / len(split), high / len(split))
        gain = gain * jnp.repeat(jnp.exp(draws), shape[axis_at] // blocks).reshape((-1,) + (1,) * (len(shape) - 1 - axis_at))
    return gain


def shared_out(rng, own, number, rows, count, top, limit, slope):
    order = jax.random.permutation(rng, count)
    packed, usual = load_shares(count, rows * top, limit, slope, True), load_shares(count, rows * top, limit, slope, False)
    places = jnp.arange(count)

    def named(lengths, rotation):
        used = int((lengths > 0).sum())
        fixed = max(1, used // 4)
        shifted = fixed + (places - fixed + rotation * (used - fixed)) % max(1, count - fixed)
        return jnp.zeros((count,), jnp.int32).at[order[jnp.where(places < fixed, places, shifted)]].set(jnp.asarray(lengths, jnp.int32))

    lengths = jnp.where(number % 4 == 0, named(packed, number // 4), named(usual, number - number // 4 - 1))
    mixed = jax.random.permutation(jax.random.fold_in(own, 3), count)
    source_of, receiver = mixed[0:count // 2 * 2:2], mixed[1:count // 2 * 2:2]
    margin = jnp.minimum(lengths[source_of] - 1, limit - lengths[receiver]) // 2
    margin = jnp.where((source_of == order[0]) | (receiver == order[0]) | (lengths[receiver] == 0), 0, jnp.maximum(margin, 0))
    shifted = jax.random.randint(jax.random.fold_in(own, 4), (count // 2,), 0, 1 << 20) % (margin + 1)
    lengths = lengths.at[source_of].add(-shifted).at[receiver].add(shifted)
    items = jnp.searchsorted(jnp.cumsum(lengths), jnp.arange(rows * top), side="right").astype(jnp.int32)
    listing = items.reshape(top, rows).T
    listing = listing[jax.random.permutation(jax.random.fold_in(own, 1), rows)]
    rotation = jax.random.randint(jax.random.fold_in(own, 2), (rows, 1), 0, top)
    return jnp.take_along_axis(listing, (jnp.arange(top)[None, :] + rotation) % top, axis=1)


def load_shares(count, total, limit, slope, full):
    loads = [(1 << 20) // math.isqrt(rank ** slope) + 1 for rank in range(1, count + 1)]
    largest = limit if full else min(limit, max(-(-total // count), total * loads[0] // sum(loads)))
    least = 1 if total - largest >= count - 1 else 0
    holding, rest = [largest] + [least] * (count - 1), total - largest - least * (count - 1)
    while rest > 0:
        free = [i for i in range(1, count) if holding[i] < largest] or [i for i in range(1, count) if holding[i] < limit]
        whole, left = sum([loads[i] for i in free]), rest
        for i in free:
            extra = min(limit - holding[i], max(1, left * loads[i] // whole), rest)
            holding[i] = holding[i] + extra
            rest = rest - extra
    return np.array(holding)


def noise(own_key, extent, scale, limit, split=(), kind=jnp.bfloat16):
    factor_of = levels(own_key, extent, split, -0.22, 0.18) if split else 1.0
    drawn = jax.random.normal(own_key, extent, jnp.float32) * scale * factor_of
    return jnp.minimum(jnp.maximum(drawn, -limit), limit).astype(kind)


def heavy_noise(key, shape, width, bound, pieces, heavy, kind=jnp.bfloat16):
    values = width * jax.random.normal(key, shape, jnp.float32)
    if pieces:
        values = values * levels(key, shape, pieces, -0.22, 0.18)
    return jnp.clip(spiked(values, jax.random.fold_in(key, 3), *heavy), -bound, bound).astype(kind)


def setup_inputs(seed: int = 0) -> dict:
    key_list = jax.random.split(jax.random.key(seed), 8)
    tokens = heavy_noise(key_list[0], (TOKENS, D), 1.0, 24.0, ((0, 128),), (0, 1, 128, 5.5))
    routes_keys = jax.random.split(jax.random.fold_in(key_list[1], 1), TOKENS // TOK_DEV)
    routes_turns = jax.random.permutation(jax.random.fold_in(key_list[1], 3), TOKENS // TOK_DEV)
    routes = jax.vmap(lambda own, number: shared_out(jax.random.fold_in(key_list[1], 2), own, number, TOK_DEV, EXPERTS, TOP, CAP, 2))(routes_keys, routes_turns).reshape((TOKENS, TOP))
    gates = jnp.clip(jnp.exp(math.log(0.5) - 2.3025851 * jax.random.uniform(key_list[2], (TOKENS, TOP), jnp.float32) ** levels(key_list[2], (TOKENS, TOP), ((0, 128),), -0.2, 0.2)), 0.05, 0.5)
    gate_up = noise(key_list[3], (EXPERTS, D, 2 * FFH), D ** -0.5, 0.125, ((0, 32),))
    down_proj = noise(key_list[4], (EXPERTS, FFH, D), FFH ** -0.5, 0.15625, ((0, 32),))
    projection = noise(key_list[5], (D, EMB), D ** -0.5, 0.125)
    matches = jax.vmap(lambda own: jax.random.permutation(own, PATCH))(jax.random.split(key_list[6], PATCHES)).reshape((PATCHES, PATCH)).astype(jnp.int32)
    return dict(tokens=tokens, routes=routes, gates=gates, gate_up=gate_up, down_proj=down_proj, projection=projection, matches=matches)


TEMPER = 0.1
EPSILON = 1e-06

def scores_of(queries, key_rows, matches, coefficient):
    logits = jnp.einsum('pie,pje->pij', queries.astype(jnp.float32), key_rows.astype(jnp.float32)) * coefficient
    totals = jnp.log(lax.optimization_barrier(jnp.sum(jnp.exp(logits), axis=2)))
    target = matches[:, :, None] == jnp.arange(PATCH, dtype=jnp.int32)[None, None, :]
    chosen = lax.optimization_barrier(jnp.sum(jnp.where(target, logits, jnp.zeros_like(logits)), axis=2))
    weights = (jnp.exp(logits - totals[:, :, None]) - target.astype(jnp.float32)).astype(jnp.bfloat16)
    return (totals - chosen, weights)

def reference(tokens, routes, gates, gate_up, down_proj, projection, matches):
    block_count = N_DP * N_EXPERT
    pair_count = TOK_DEV * TOP
    expert_ids = routes.reshape(block_count, pair_count)
    member = (expert_ids[:, :, None] == jnp.arange(EXPERTS, dtype=jnp.int32)[None, None, :]).astype(jnp.int32)
    before = jnp.cumsum(member, axis=1) - member
    position = lax.optimization_barrier(jnp.sum(before * member, axis=2)).astype(jnp.int32)
    block_ids = jnp.broadcast_to(jnp.arange(block_count, dtype=jnp.int32)[:, None], (block_count, pair_count))
    pair_rows = jnp.broadcast_to((jnp.arange(pair_count, dtype=jnp.int32) // TOP)[None, :], (block_count, pair_count))
    row_ids = block_ids * TOK_DEV + pair_rows
    slot_ids = block_ids * CAP + position
    row_table = jnp.full((EXPERTS, block_count * CAP), -1, jnp.int32).at[expert_ids, slot_ids].set(row_ids)
    gate_table = jnp.zeros((EXPERTS, block_count * CAP), jnp.float32).at[expert_ids, slot_ids].set(gates.reshape(block_count, pair_count))

    def forward_slots(joined_w, down_w, row_slots):
        present = row_slots >= 0
        picked = jnp.where(present[:, None], tokens[jnp.maximum(row_slots, 0)], jnp.zeros((), tokens.dtype))
        joined = jnp.dot(picked, joined_w, preferred_element_type=jnp.float32)
        hidden = (jax.nn.silu(joined[:, :FFH]) * joined[:, FFH:]).astype(jnp.bfloat16)
        outputs = jnp.dot(hidden, down_w, preferred_element_type=jnp.float32).astype(jnp.bfloat16)
        return (joined, outputs, present)

    def project_slots(inputs):
        joined, outputs, present = forward_slots(inputs[0], inputs[1], inputs[2])
        return jnp.dot(outputs, projection, preferred_element_type=jnp.float32).astype(jnp.bfloat16)
    projected_table = lax.map(project_slots, (gate_up, down_proj, row_table))
    slot_flat = slot_ids.reshape(TOKENS, TOP)
    mixture = jnp.zeros((TOKENS, EMB), jnp.float32)
    for choice_index in range(TOP):
        picked_proj = projected_table[routes[:, choice_index], slot_flat[:, choice_index]].astype(jnp.float32)
        mixture = mixture + gates[:, choice_index:choice_index + 1] * picked_proj
    embedding = jnp.dot(tokens, projection, preferred_element_type=jnp.float32) + mixture
    inverse = lax.rsqrt(lax.optimization_barrier(jnp.mean(embedding * embedding, axis=1, keepdims=True)) + EPSILON)
    unit_rows = embedding * inverse
    unit_b = unit_rows.astype(jnp.bfloat16)
    coefficient = 1.0 / (EMB * TEMPER)
    partner_index = jnp.bitwise_xor(jnp.arange(N_EXPERT, dtype=jnp.int32), jnp.int32(N_EXPERT // 2))
    patch_shape = (N_DP, N_EXPERT, TOK_DEV // PATCH, PATCH, EMB)
    queries_all = unit_b.reshape(patch_shape)
    queries = queries_all.reshape(PATCHES, PATCH, EMB)
    key_rows = queries_all[:, partner_index].reshape(PATCHES, PATCH, EMB)
    row_loss, weights = scores_of(queries, key_rows, matches, coefficient)
    query_part = jnp.einsum('pij,pje->pie', weights.astype(jnp.float32), key_rows.astype(jnp.float32)) * coefficient
    outgoing = jnp.einsum('pij,pie->pje', weights.astype(jnp.float32), queries.astype(jnp.float32)) * coefficient
    key_part = outgoing.reshape(patch_shape)[:, partner_index].reshape(TOKENS, EMB)
    upstream = query_part.reshape(TOKENS, EMB) + key_part
    embed_grad = inverse * (upstream - unit_rows * lax.optimization_barrier(jnp.mean(upstream * unit_rows, axis=1, keepdims=True)))
    embed_grad_b = embed_grad.astype(jnp.bfloat16)
    direct_grad = jnp.dot(embed_grad_b, projection.T, preferred_element_type=jnp.float32)

    def backward_step(carry, inputs):
        grad_acc, proj_acc = carry
        joined_w, down_w, row_slots, gate_slots = inputs
        joined, outputs, present = forward_slots(joined_w, down_w, row_slots)
        picked_grad = jnp.where(present[:, None], embed_grad_b[jnp.maximum(row_slots, 0)], jnp.zeros((), embed_grad_b.dtype))
        slot_grads = (gate_slots[:, None] * picked_grad.astype(jnp.float32)).astype(jnp.bfloat16)
        output_grads = jnp.dot(slot_grads, projection.T, preferred_element_type=jnp.float32).astype(jnp.bfloat16)
        hidden_grad = jnp.dot(output_grads, down_w.T, preferred_element_type=jnp.float32)
        gate_act = joined[:, :FFH]
        up_act = joined[:, FFH:]
        sigmoid = jax.nn.sigmoid(gate_act)
        joined_grad = jnp.concatenate([hidden_grad * up_act * sigmoid * (1.0 + gate_act * (1.0 - sigmoid)), hidden_grad * gate_act * sigmoid], axis=1).astype(jnp.bfloat16)
        input_grads = jnp.dot(joined_grad, joined_w.T, preferred_element_type=jnp.float32).astype(jnp.bfloat16)
        masked = jnp.where(present[:, None], input_grads.astype(jnp.float32), jnp.zeros((), jnp.float32))
        grad_acc = grad_acc.at[jnp.maximum(row_slots, 0)].add(masked)
        proj_acc = proj_acc + jnp.dot(outputs.T, slot_grads, preferred_element_type=jnp.float32)
        return ((grad_acc, proj_acc), None)
    start_carry = (jnp.zeros((TOKENS, D), jnp.float32), jnp.zeros((D, EMB), jnp.float32))
    final_carry, unused = lax.scan(backward_step, start_carry, (gate_up, down_proj, row_table, gate_table))
    grad_tokens = (direct_grad + final_carry[0]).astype(jnp.bfloat16)
    grad_projection = (jnp.dot(tokens.T, embed_grad_b, preferred_element_type=jnp.float32) + final_carry[1]) * (1.0 / math.sqrt(TOKENS))
    return (grad_tokens, grad_projection, row_loss.reshape(TOKENS))
```

```python
import math

import jax
import jax.numpy as jnp
from jax import lax
from jax.experimental import pallas as pl
from jax.experimental.pallas import tpu as pltpu
from jax.sharding import Mesh
from jax.sharding import PartitionSpec as P

EXPERT = ("expert_0", "expert_1", "expert_2")
DP_EXPERT = ("dp", "expert_0", "expert_1", "expert_2")

TEMPER = 0.1
EPSILON = 1e-06
ROWS = 128
TOP = 4
WIDTH = 2048
HIDDEN = 1408
EMBED = 512
EXPERTS = 32
MAIN = 16
EXTRA = 4
SLOTS = EXPERTS * MAIN
SPARE = EXPERTS * EXTRA
TOTAL = SLOTS + SPARE
CHUNKS = tuple((lo, min(lo + 256, HIDDEN)) for lo in range(0, HIDDEN, 256))
TILE = 256
F32 = jnp.float32
BF16 = jnp.bfloat16
VMEM_LIMIT = 48 * 1024 * 1024


def dot(left, right):
    return jnp.dot(left, right, preferred_element_type=F32)


def dot_rows(left, right):
    return lax.dot_general(left, right, (((0,), (0,)), ((), ())), preferred_element_type=F32)


def dot_cols(left, right):
    return lax.dot_general(left, right, (((1,), (1,)), ((), ())), preferred_element_type=F32)


def iota(shape, dim):
    return lax.broadcasted_iota(jnp.int32, shape, dim)


def expanded(table):
    spread = jnp.broadcast_to(table[:, None, :], (EXPERTS, MAIN, ROWS))
    return spread.reshape(SLOTS, ROWS)


def ranks(routes):
    experts = iota((EXPERTS, ROWS), 0)
    member = jnp.zeros((EXPERTS, ROWS), F32)
    for k in range(TOP):
        member = member + jnp.where(routes[k : k + 1, :] == experts, 1.0, 0.0)
    earlier = jnp.where(iota((ROWS, ROWS), 0) < iota((ROWS, ROWS), 1), 1.0, 0.0)
    rank = dot(member.astype(BF16), earlier.astype(BF16))
    return jnp.where(member > 0.0, rank, -1.0)


def pair_gates(routes, gates):
    experts = iota((EXPERTS, ROWS), 0)
    total = jnp.zeros((EXPERTS, ROWS), F32)
    for k in range(TOP):
        total = total + jnp.where(routes[k : k + 1, :] == experts, gates[k : k + 1, :], 0.0)
    return total


def choosers(routes):
    rank = expanded(ranks(routes))
    place = iota((SLOTS, ROWS), 0) % MAIN
    main = rank == place.astype(F32)
    extra = rank == (MAIN + place % EXTRA).astype(F32)
    quarters = [extra & (place // EXTRA == j) for j in range(MAIN // EXTRA)]
    return main, quarters


def one_hot(chosen):
    return jnp.where(chosen, 1.0, 0.0).astype(BF16)


def unpacker():
    row = iota((SLOTS, SLOTS), 0)
    wanted = (row % SPARE) // EXTRA * MAIN + row // SPARE * EXTRA + row % EXTRA
    return one_hot(iota((SLOTS, SLOTS), 1) == wanted)


def packer():
    row = iota((SLOTS, SLOTS), 0)
    wanted = (row % MAIN) // EXTRA * SPARE + row // MAIN * EXTRA + row % EXTRA
    return one_hot(iota((SLOTS, SLOTS), 1) == wanted)


def dispatch_kernel(routes_ref, tokens_ref, out_ref):
    main, quarters = choosers(routes_ref[...])
    out_ref[:, :WIDTH] = dot(one_hot(main), tokens_ref[...]).astype(BF16)
    quarter = WIDTH // 4
    total = jnp.zeros((SLOTS, quarter), F32)
    for j in range(4):
        total = total + dot(one_hot(quarters[j]), tokens_ref[:, j * quarter : (j + 1) * quarter])
    out_ref[:, WIDTH:] = total.astype(BF16)


def forward_kernel(
    recv_hbm, joined_hbm, mixed_hbm, out_ref, hidden_hbm, slopes_hbm,
    x_ref, extra_ref, w_ref, mixed_ref, act_ref, hidden_ref, slopes_ref, sems, out_sems,
):
    def start(source, target, index):
        copy = pltpu.make_async_copy(source, target, sems.at[index])
        copy.start()
        return copy

    extra_copy = start(recv_hbm.at[:, pl.ds(WIDTH, WIDTH // 4)], extra_ref, 0)
    main_copy = start(recv_hbm.at[:, pl.ds(0, WIDTH)], x_ref.at[pl.ds(0, SLOTS), :], 1)
    weight_copies = []
    for c, (lo, hi) in enumerate(CHUNKS):
        pair = []
        for h in range(2):
            cols = pl.ds(h * HIDDEN + lo, hi - lo)
            pair.append(start(joined_hbm.at[:, cols], w_ref.at[:, cols], 3 + 2 * c + h))
        weight_copies.append(pair)
    mixed_copy = start(mixed_hbm, mixed_ref, 2)
    turned = unpacker()
    extra_copy.wait()
    quarter = WIDTH // 4
    spread = dot(turned, extra_ref[...]).astype(BF16)
    for j in range(4):
        x_ref[SLOTS:, j * quarter : (j + 1) * quarter] = spread[j * SPARE : (j + 1) * SPARE]
    main_copy.wait()
    outgoing = []
    for c, (lo, hi) in enumerate(CHUNKS):
        slot = c % 2
        wide = hi - lo
        for copy in weight_copies[c]:
            copy.wait()
        act_ref[slot, 0, :, :wide] = dot(x_ref[...], w_ref[:, lo:hi])
        act_ref[slot, 1, :, :wide] = dot(x_ref[...], w_ref[:, HIDDEN + lo : HIDDEN + hi])
        for m in range(0, TOTAL, 64):
            gate = act_ref[slot, 0, m : m + 64, :wide]
            up = act_ref[slot, 1, m : m + 64, :wide]
            sigmoid = jax.nn.sigmoid(gate)
            silu = gate * sigmoid
            hidden_ref[m : m + 64, lo:hi] = (silu * up).astype(BF16)
            slopes_ref[m : m + 64, HIDDEN + lo : HIDDEN + hi] = silu.astype(BF16)
            slopes_ref[m : m + 64, lo:hi] = (up * sigmoid * (1.0 + gate * (1.0 - sigmoid))).astype(BF16)
        for n, (source, target, offset) in enumerate(
            ((hidden_ref, hidden_hbm, 0), (slopes_ref, slopes_hbm, 0), (slopes_ref, slopes_hbm, HIDDEN))
        ):
            cols = pl.ds(offset + lo, wide)
            copy = pltpu.make_async_copy(source.at[:, cols], target.at[:, cols], out_sems.at[3 * c + n])
            copy.start()
            outgoing.append(copy)
    mixed_copy.wait()
    projected = dot(hidden_ref[...], mixed_ref[...]).astype(BF16)
    out_ref[:, :EMBED] = projected[:SLOTS]
    quarter = EMBED // 4
    stacked = jnp.concatenate(
        [projected[SLOTS:, j * quarter : (j + 1) * quarter] for j in range(4)], axis=0
    )
    out_ref[:, EMBED:] = dot(packer(), stacked).astype(BF16)
    for copy in outgoing:
        copy.wait()


def weighted(chosen, gates):
    return jnp.where(chosen, gates, 0.0)


def split_product(chosen, gates, values):
    whole = weighted(chosen, gates)
    high = whole.astype(BF16)
    low = (whole - high.astype(F32)).astype(BF16)
    return dot_rows(high, values) + dot_rows(low, values)


def embed_kernel(routes_ref, gates_ref, answer_ref, base_ref, embedding_ref, unit_ref):
    main, quarters = choosers(routes_ref[...])
    gates = expanded(pair_gates(routes_ref[...], gates_ref[...]))
    mixture = split_product(main, gates, answer_ref[:, :EMBED])
    extra = jnp.concatenate(
        [split_product(quarters[j], gates, answer_ref[:, EMBED:]) for j in range(4)], axis=1
    )
    embedding = base_ref[...] + mixture + extra
    inverse = lax.rsqrt(jnp.mean(embedding * embedding, axis=1, keepdims=True) + EPSILON)
    embedding_ref[...] = embedding
    unit_ref[...] = (embedding * inverse).astype(BF16)


def loss_kernel(
    routes_ref, gates_ref, matches_ref, partner_ref, embedding_ref, unit_ref, key_ref,
    loss_ref, grad_ref, out_ref,
):
    embedding = embedding_ref[...]
    unit = unit_ref[...]
    keys = key_ref[...]
    coefficient = 1.0 / (EMBED * TEMPER)
    inverse = lax.rsqrt(jnp.mean(embedding * embedding, axis=1, keepdims=True) + EPSILON)
    unit_rows = embedding * inverse
    entry = iota((ROWS, ROWS), 0)

    def scores(rows, columns, matches):
        logits = dot_cols(rows, columns) * coefficient
        totals = jnp.log(jnp.sum(jnp.exp(logits), axis=0, keepdims=True))
        target = matches == entry
        chosen = jnp.sum(jnp.where(target, logits, 0.0), axis=0, keepdims=True)
        weights = jnp.exp(logits - totals) - jnp.where(target, 1.0, 0.0)
        return totals - chosen, weights.astype(BF16)

    loss, own = scores(keys, unit, matches_ref[...])
    loss_ref[...] = loss
    partner = scores(unit, keys, partner_ref[...].astype(jnp.int32))[1]
    upstream = (dot_rows(own, keys) + dot(partner, keys)) * coefficient
    grad = inverse * (upstream - unit_rows * jnp.mean(upstream * unit_rows, axis=1, keepdims=True))
    grad = grad.astype(BF16)
    grad_ref[...] = grad
    main, quarters = choosers(routes_ref[...])
    gates = expanded(pair_gates(routes_ref[...], gates_ref[...]))
    slot_gates = jnp.sum(weighted(main, gates), axis=1, keepdims=True)
    out_ref[:, :EMBED] = (slot_gates * dot(one_hot(main), grad)).astype(BF16)
    quarter = EMBED // 4
    total = jnp.zeros((SLOTS, quarter), F32)
    extra_gates = jnp.zeros((SLOTS, 1), F32)
    for j in range(4):
        total = total + dot(one_hot(quarters[j]), grad[:, j * quarter : (j + 1) * quarter])
        extra_gates = extra_gates + jnp.sum(weighted(quarters[j], gates), axis=1, keepdims=True)
    out_ref[:, EMBED:] = (extra_gates * total).astype(BF16)


def backward_kernel(
    arrived_ref, mixed_hbm, slopes_hbm, joined_hbm, out_hbm, grads_ref,
    mixed_ref, slopes_ref, w_ref, act_ref, joined_ref, extra_ref, out_ref, sems, out_sems,
):
    def start(source, target, index):
        copy = pltpu.make_async_copy(source, target, sems.at[index])
        copy.start()
        return copy

    mixed_copy = start(mixed_hbm, mixed_ref, 0)
    slopes_copy = start(slopes_hbm, slopes_ref, 1)
    weight_copies = [
        start(joined_hbm.at[pl.ds(n, TILE), :], w_ref.at[pl.ds(n, TILE), :], 2 + n // TILE)
        for n in range(0, WIDTH, TILE)
    ]
    quarter = EMBED // 4
    grads_ref[:SLOTS, :] = arrived_ref[:, :EMBED]
    spread = dot(unpacker(), arrived_ref[:, EMBED:]).astype(BF16)
    for j in range(4):
        grads_ref[SLOTS:, j * quarter : (j + 1) * quarter] = spread[j * SPARE : (j + 1) * SPARE]
    mixed_copy.wait()
    slopes_copy.wait()
    for c, (lo, hi) in enumerate(CHUNKS):
        slot = c % 2
        wide = hi - lo
        act_ref[slot, :, :wide] = dot_cols(grads_ref[...], mixed_ref[lo:hi, :])
        for m in range(0, TOTAL, 64):
            hidden_grad = act_ref[slot, m : m + 64, :wide]
            for offset in (0, HIDDEN):
                slope = slopes_ref[m : m + 64, offset + lo : offset + hi].astype(F32)
                joined_ref[m : m + 64, offset + lo : offset + hi] = (hidden_grad * slope).astype(BF16)
    outgoing = []
    quarter = WIDTH // 4
    for n in range(0, WIDTH, TILE):
        weight_copies[n // TILE].wait()
        result = dot_cols(joined_ref[...], w_ref[n : n + TILE, :]).astype(BF16)
        out_ref[:, n : n + TILE] = result[:SLOTS]
        j, within = n // quarter, n % quarter
        extra_ref[j * SPARE : (j + 1) * SPARE, within : within + TILE] = result[SLOTS:]
        cols = pl.ds(n, TILE)
        copy = pltpu.make_async_copy(out_ref.at[:, cols], out_hbm.at[:, cols], out_sems.at[n // TILE])
        copy.start()
        outgoing.append(copy)
    out_ref[:, WIDTH:] = dot(packer(), extra_ref[...]).astype(BF16)
    cols = pl.ds(WIDTH, quarter)
    copy = pltpu.make_async_copy(out_ref.at[:, cols], out_hbm.at[:, cols], out_sems.at[WIDTH // TILE])
    copy.start()
    outgoing.append(copy)
    for copy in outgoing:
        copy.wait()


def head_kernel(hidden_ref, grads_ref, tokens_ref, embed_grad_ref, down_ref, out_ref):
    inner = dot_rows(hidden_ref[...], grads_ref[...]).astype(BF16)
    for n in range(0, WIDTH, TILE):
        part = dot_rows(down_ref[:, n : n + TILE], inner)
        part = part + dot_rows(tokens_ref[:, n : n + TILE], embed_grad_ref[...])
        part = part.astype(BF16)
        for b in range(TILE // 32):
            row = n // 2 + 16 * b
            for core in range(2):
                out_ref[core, row : row + 16, :] = part[32 * b + 16 * core : 32 * b + 16 * core + 16]


def combine_kernel(routes_ref, back_ref, direct_ref, out_ref):
    main, quarters = choosers(routes_ref[...])
    main = one_hot(main)
    quarter = WIDTH // 4
    for j in range(4):
        cols = slice(j * quarter, (j + 1) * quarter)
        total = dot_rows(main, back_ref[:, cols]) + dot_rows(one_hot(quarters[j]), back_ref[:, WIDTH:])
        out_ref[:, cols] = (direct_ref[:, cols] + total).astype(BF16)


def call(kernel, outs, ins, scratch=(), flops=0, moved=0):
    def spec(space):
        return pl.BlockSpec(memory_space=space)

    return pl.pallas_call(
        kernel,
        out_shape=tuple(jax.ShapeDtypeStruct(shape, dtype) for shape, dtype, _ in outs),
        in_specs=[spec(space) for _, space in ins],
        out_specs=tuple(spec(space) for _, _, space in outs),
        scratch_shapes=scratch,
        compiler_params=pltpu.CompilerParams(vmem_limit_bytes=VMEM_LIMIT),
        cost_estimate=pl.CostEstimate(flops=flops, bytes_accessed=moved, transcendentals=0),
    )(*[value for value, _ in ins])


def exchanged(value, axes, parts):
    rows, width = value.shape
    blocks = value.reshape(parts, rows // parts, width)
    return lax.all_to_all(blocks, axes, 0, 0, tiled=True).reshape(rows, width)


def body(tokens, routes, gates, gate_up, down_proj, projection, matches):
    vmem, hbm = pltpu.VMEM, pl.ANY
    routes, gates = routes.T, gates.T
    weights_joined, weights_down = gate_up[0], down_proj[0]
    partner = [(i, i ^ EXPERTS // 2) for i in range(EXPERTS)]
    dma = pltpu.SemaphoreType.DMA

    (dispatch,) = call(
        dispatch_kernel, [((SLOTS, WIDTH * 5 // 4), BF16, vmem)], [(routes, vmem), (tokens, vmem)],
        flops=2 * SLOTS * ROWS * WIDTH * 2, moved=3 << 20,
    )
    received = exchanged(dispatch, EXPERT, EXPERTS)
    partner_matches = lax.ppermute(matches.astype(BF16), EXPERT, partner)
    mixed = dot(weights_down, projection).astype(BF16)
    base = dot(tokens, projection)

    packed_embed = ((SLOTS, EMBED * 5 // 4), BF16, vmem)
    packed, hidden, slopes = call(
        forward_kernel,
        [packed_embed, ((TOTAL, HIDDEN), BF16, hbm), ((TOTAL, 2 * HIDDEN), BF16, hbm)],
        [(received, hbm), (weights_joined, hbm), (mixed, hbm)],
        scratch=[
            pltpu.VMEM((TOTAL, WIDTH), BF16),
            pltpu.VMEM((SLOTS, WIDTH // 4), BF16),
            pltpu.VMEM((WIDTH, 2 * HIDDEN), BF16),
            pltpu.VMEM((HIDDEN, EMBED), BF16),
            pltpu.VMEM((2, 2, TOTAL, 256), F32),
            pltpu.VMEM((TOTAL, HIDDEN), BF16),
            pltpu.VMEM((TOTAL, 2 * HIDDEN), BF16),
            dma((3 + 2 * len(CHUNKS),)),
            dma((3 * len(CHUNKS),)),
        ],
        flops=2 * TOTAL * HIDDEN * (2 * WIDTH + EMBED), moved=22 << 20,
    )
    answer = exchanged(packed, EXPERT, EXPERTS)
    embedding, unit = call(
        embed_kernel,
        [((ROWS, EMBED), F32, vmem), ((ROWS, EMBED), BF16, vmem)],
        [(routes, vmem), (gates, vmem), (answer, vmem), (base, vmem)],
        flops=4 * SLOTS * ROWS * EMBED * 2, moved=2 << 20,
    )
    keys = lax.ppermute(unit, EXPERT, partner)
    row_loss, embed_grad, slot_grads = call(
        loss_kernel,
        [((1, ROWS), F32, vmem), ((ROWS, EMBED), BF16, vmem), packed_embed],
        [(routes, vmem), (gates, vmem), (matches, vmem), (partner_matches, vmem),
         (embedding, vmem), (unit, vmem), (keys, vmem)],
        flops=2 * SLOTS * ROWS * EMBED * 2, moved=2 << 20,
    )
    arrived = exchanged(slot_grads, EXPERT, EXPERTS)
    direct = dot_cols(embed_grad, projection)
    input_grads, grads = call(
        backward_kernel,
        [((SLOTS, WIDTH * 5 // 4), BF16, hbm), ((TOTAL, EMBED), BF16, vmem)],
        [(arrived, vmem), (mixed, hbm), (slopes, hbm), (weights_joined, hbm)],
        scratch=[
            pltpu.VMEM((HIDDEN, EMBED), BF16),
            pltpu.VMEM((TOTAL, 2 * HIDDEN), BF16),
            pltpu.VMEM((WIDTH, 2 * HIDDEN), BF16),
            pltpu.VMEM((2, TOTAL, 256), F32),
            pltpu.VMEM((TOTAL, 2 * HIDDEN), BF16),
            pltpu.VMEM((SLOTS, WIDTH // 4), BF16),
            pltpu.VMEM((SLOTS, WIDTH * 5 // 4), BF16),
            dma((2 + WIDTH // TILE,)),
            dma((1 + WIDTH // TILE,)),
        ],
        flops=2 * TOTAL * HIDDEN * (2 * WIDTH + EMBED), moved=22 << 20,
    )
    back = exchanged(input_grads, EXPERT, EXPERTS)
    (head,) = call(
        head_kernel,
        [((2, WIDTH // 2, EMBED), BF16, vmem)],
        [(hidden, vmem), (grads, vmem), (tokens, vmem), (embed_grad, vmem), (weights_down, vmem)],
        flops=2 * HIDDEN * EMBED * (TOTAL + WIDTH), moved=12 << 20,
    )
    halves = lax.all_to_all(head, "expert_2", 0, 0, tiled=True)
    half = (halves[0].astype(F32) + halves[1].astype(F32)).astype(BF16)
    parts = lax.all_to_all(
        half.reshape(64, 16, EMBED), ("dp", "expert_0", "expert_1"), 0, 0, tiled=True
    )
    summed = jnp.sum(parts.astype(F32), axis=0)
    device_count = lax.axis_size("dp") * EXPERTS
    grad_projection = summed * (1.0 / math.sqrt(ROWS * device_count))
    (grad_tokens,) = call(
        combine_kernel, [((ROWS, WIDTH), BF16, vmem)], [(routes, vmem), (back, vmem), (direct, vmem)],
        flops=2 * SLOTS * ROWS * WIDTH * 2, moved=4 << 20,
    )
    return grad_tokens, grad_projection, row_loss.reshape(ROWS)


def solution(mesh):
    torus = Mesh(
        mesh.devices.reshape(mesh.shape["dp"], 4, 4, 2), ("dp", "expert_0", "expert_1", "expert_2")
    )
    return jax.shard_map(
        body,
        mesh=torus,
        in_specs=(
            P(DP_EXPERT, None),
            P(DP_EXPERT, None),
            P(DP_EXPERT, None),
            P(EXPERT, None, None),
            P(EXPERT, None, None),
            P(),
            P(DP_EXPERT, None),
        ),
        out_specs=(P(DP_EXPERT, None), P(DP_EXPERT, None), P(DP_EXPERT)),
        check_vma=False,
    )
```

```python
import math

import jax
import jax.numpy as jnp
from jax import lax
from jax.experimental import pallas as pl
from jax.experimental.pallas import tpu as pltpu
from jax.sharding import Mesh
from jax.sharding import PartitionSpec as P

EXPERT = ("expert_0", "expert_1", "expert_2")
DP_EXPERT = ("dp", "expert_0", "expert_1", "expert_2")

TEMPER = 0.1
EPSILON = 1e-06
ROWS = 128
TOP = 4
WIDTH = 2048
HIDDEN = 1408
EMBED = 512
EXPERTS = 32
MAIN = 16
EXTRA = 4
SLOTS = EXPERTS * MAIN
SPARE = EXPERTS * EXTRA
TOTAL = SLOTS + SPARE
CHUNKS = tuple((lo, min(lo + 256, HIDDEN)) for lo in range(0, HIDDEN, 256))
TILE = 256
F32 = jnp.float32
BF16 = jnp.bfloat16
VMEM_LIMIT = 24 * 1024 * 1024


def dot(left, right):
    return jnp.dot(left, right, preferred_element_type=F32)


def dot_rows(left, right):
    return lax.dot_general(left, right, (((0,), (0,)), ((), ())), preferred_element_type=F32)


def dot_cols(left, right):
    return lax.dot_general(left, right, (((1,), (1,)), ((), ())), preferred_element_type=F32)


def iota(shape, dim):
    return lax.broadcasted_iota(jnp.int32, shape, dim)


def expanded(table):
    spread = jnp.broadcast_to(table[:, None, :], (EXPERTS, MAIN, ROWS))
    return spread.reshape(SLOTS, ROWS)


def ranks(routes):
    experts = iota((EXPERTS, ROWS), 0)
    member = jnp.zeros((EXPERTS, ROWS), F32)
    for k in range(TOP):
        member = member + jnp.where(routes[k : k + 1, :] == experts, 1.0, 0.0)
    earlier = jnp.where(iota((ROWS, ROWS), 0) < iota((ROWS, ROWS), 1), 1.0, 0.0)
    rank = dot(member.astype(BF16), earlier.astype(BF16))
    return jnp.where(member > 0.0, rank, -1.0)


def pair_gates(routes, gates):
    experts = iota((EXPERTS, ROWS), 0)
    total = jnp.zeros((EXPERTS, ROWS), F32)
    for k in range(TOP):
        total = total + jnp.where(routes[k : k + 1, :] == experts, gates[k : k + 1, :], 0.0)
    return total


def choosers(routes):
    rank = expanded(ranks(routes))
    place = iota((SLOTS, ROWS), 0) % MAIN
    main = rank == place.astype(F32)
    extra = rank == (MAIN + place % EXTRA).astype(F32)
    quarters = [extra & (place // EXTRA == j) for j in range(MAIN // EXTRA)]
    return main, quarters


def one_hot(chosen):
    return jnp.where(chosen, 1.0, 0.0).astype(BF16)


def unpacker():
    row = iota((SLOTS, SLOTS), 0)
    wanted = (row % SPARE) // EXTRA * MAIN + row // SPARE * EXTRA + row % EXTRA
    return one_hot(iota((SLOTS, SLOTS), 1) == wanted)


def packer():
    row = iota((SLOTS, SLOTS), 0)
    wanted = (row % MAIN) // EXTRA * SPARE + row // MAIN * EXTRA + row % EXTRA
    return one_hot(iota((SLOTS, SLOTS), 1) == wanted)


def dispatch_kernel(routes_hbm, tokens_hbm, out_hbm, routes_ref, tokens_ref, out_ref, sems, out_sems):
    routes_copy = pltpu.make_async_copy(routes_hbm, routes_ref, sems.at[0])
    tokens_copy = pltpu.make_async_copy(tokens_hbm, tokens_ref, sems.at[1])
    routes_copy.start()
    tokens_copy.start()
    routes_copy.wait()
    main, quarters = choosers(routes_ref[...])
    main = one_hot(main)
    quarter = WIDTH // 4
    total = jnp.zeros((SLOTS, quarter), F32)
    tokens_copy.wait()
    outgoing = []
    for j in range(5):
        cols = slice(j * quarter, (j + 1) * quarter)
        if j < 4:
            out_ref[:, cols] = dot(main, tokens_ref[:, cols]).astype(BF16)
            total = total + dot(one_hot(quarters[j]), tokens_ref[:, cols])
        else:
            out_ref[:, cols] = total.astype(BF16)
        part = pl.ds(j * quarter, quarter)
        copy = pltpu.make_async_copy(out_ref.at[:, part], out_hbm.at[:, part], out_sems.at[j])
        copy.start()
        outgoing.append(copy)
    for copy in outgoing:
        copy.wait()


def forward_kernel(
    recv_hbm, w_ref, mixed_ref, out_hbm, hidden_ref, slopes_ref,
    x_ref, extra_ref, act_ref, out_ref, sems, out_sems,
):
    quarter = WIDTH // 4
    extra_copy = pltpu.make_async_copy(recv_hbm.at[:, pl.ds(WIDTH, quarter)], extra_ref, sems.at[0])
    extra_copy.start()
    main_copy = pltpu.make_async_copy(
        recv_hbm.at[:, pl.ds(0, WIDTH)], x_ref.at[pl.ds(0, SLOTS), :], sems.at[1]
    )
    main_copy.start()
    turned = unpacker()
    extra_copy.wait()
    spread = dot(turned, extra_ref[...]).astype(BF16)
    for j in range(4):
        x_ref[SLOTS:, j * quarter : (j + 1) * quarter] = spread[j * SPARE : (j + 1) * SPARE]
    main_copy.wait()
    for c, (lo, hi) in enumerate(CHUNKS):
        slot = c % 2
        wide = hi - lo
        act_ref[slot, 0, :, :wide] = dot(x_ref[...], w_ref[:, lo:hi])
        act_ref[slot, 1, :, :wide] = dot(x_ref[...], w_ref[:, HIDDEN + lo : HIDDEN + hi])
        for m in range(0, TOTAL, 64):
            gate = act_ref[slot, 0, m : m + 64, :wide]
            up = act_ref[slot, 1, m : m + 64, :wide]
            sigmoid = 0.5 + 0.5 * jnp.tanh(0.5 * gate)
            silu = gate * sigmoid
            hidden_ref[m : m + 64, lo:hi] = (silu * up).astype(BF16)
            slopes_ref[m : m + 64, HIDDEN + lo : HIDDEN + hi] = silu.astype(BF16)
            slopes_ref[m : m + 64, lo:hi] = (up * sigmoid * (1.0 + gate * (1.0 - sigmoid))).astype(BF16)
    projected = dot(hidden_ref[...], mixed_ref[...]).astype(BF16)
    out_ref[:, :EMBED] = projected[:SLOTS]
    cols = pl.ds(0, EMBED)
    first = pltpu.make_async_copy(out_ref.at[:, cols], out_hbm.at[:, cols], out_sems.at[0])
    first.start()
    quarter = EMBED // 4
    stacked = jnp.concatenate(
        [projected[SLOTS:, j * quarter : (j + 1) * quarter] for j in range(4)], axis=0
    )
    out_ref[:, EMBED:] = dot(packer(), stacked).astype(BF16)
    cols = pl.ds(EMBED, quarter)
    second = pltpu.make_async_copy(out_ref.at[:, cols], out_hbm.at[:, cols], out_sems.at[1])
    second.start()
    first.wait()
    second.wait()


def weighted(chosen, gates):
    return jnp.where(chosen, gates, 0.0)


def split_product(chosen, gates, values):
    whole = weighted(chosen, gates)
    high = whole.astype(BF16)
    low = (whole - high.astype(F32)).astype(BF16)
    return dot_rows(high, values) + dot_rows(low, values)


def embed_kernel(routes_ref, gates_ref, answer_ref, base_ref, embedding_ref, unit_ref):
    main, quarters = choosers(routes_ref[...])
    gates = expanded(pair_gates(routes_ref[...], gates_ref[...]))
    mixture = split_product(main, gates, answer_ref[:, :EMBED])
    extra = jnp.concatenate(
        [split_product(quarters[j], gates, answer_ref[:, EMBED:]) for j in range(4)], axis=1
    )
    embedding = base_ref[...] + mixture + extra
    inverse = lax.rsqrt(jnp.mean(embedding * embedding, axis=1, keepdims=True) + EPSILON)
    embedding_ref[...] = embedding
    unit_ref[...] = (embedding * inverse).astype(BF16)


def loss_kernel(
    routes_ref, gates_ref, matches_ref, partner_ref, embedding_ref, unit_ref, key_ref,
    loss_ref, grad_ref, out_ref,
):
    embedding = embedding_ref[...]
    unit = unit_ref[...]
    keys = key_ref[...]
    coefficient = 1.0 / (EMBED * TEMPER)
    inverse = lax.rsqrt(jnp.mean(embedding * embedding, axis=1, keepdims=True) + EPSILON)
    unit_rows = embedding * inverse
    entry = iota((ROWS, ROWS), 0)

    def scores(rows, columns, matches):
        logits = dot_cols(rows, columns) * coefficient
        totals = jnp.log(jnp.sum(jnp.exp(logits), axis=0, keepdims=True))
        target = matches == entry
        chosen = jnp.sum(jnp.where(target, logits, 0.0), axis=0, keepdims=True)
        weights = jnp.exp(logits - totals) - jnp.where(target, 1.0, 0.0)
        return totals - chosen, weights.astype(BF16)

    loss, own = scores(keys, unit, matches_ref[...])
    loss_ref[...] = loss
    partner = scores(unit, keys, partner_ref[...].astype(jnp.int32))[1]
    upstream = (dot_rows(own, keys) + dot(partner, keys)) * coefficient
    grad = inverse * (upstream - unit_rows * jnp.mean(upstream * unit_rows, axis=1, keepdims=True))
    grad = grad.astype(BF16)
    grad_ref[...] = grad
    main, quarters = choosers(routes_ref[...])
    gates = expanded(pair_gates(routes_ref[...], gates_ref[...]))
    slot_gates = jnp.sum(weighted(main, gates), axis=1, keepdims=True)
    out_ref[:, :EMBED] = (slot_gates * dot(one_hot(main), grad)).astype(BF16)
    quarter = EMBED // 4
    total = jnp.zeros((SLOTS, quarter), F32)
    extra_gates = jnp.zeros((SLOTS, 1), F32)
    for j in range(4):
        total = total + dot(one_hot(quarters[j]), grad[:, j * quarter : (j + 1) * quarter])
        extra_gates = extra_gates + jnp.sum(weighted(quarters[j], gates), axis=1, keepdims=True)
    out_ref[:, EMBED:] = (extra_gates * total).astype(BF16)


def backward_kernel(
    arrived_ref, mixed_ref, slopes_ref, w_ref, out_hbm, grads_ref,
    act_ref, joined_ref, extra_ref, out_ref, out_sems,
):
    quarter = EMBED // 4
    grads_ref[:SLOTS, :] = arrived_ref[:, :EMBED]
    spread = dot(unpacker(), arrived_ref[:, EMBED:]).astype(BF16)
    for j in range(4):
        grads_ref[SLOTS:, j * quarter : (j + 1) * quarter] = spread[j * SPARE : (j + 1) * SPARE]
    for c, (lo, hi) in enumerate(CHUNKS):
        slot = c % 2
        wide = hi - lo
        act_ref[slot, :, :wide] = dot_cols(grads_ref[...], mixed_ref[lo:hi, :])
        for m in range(0, TOTAL, 64):
            hidden_grad = act_ref[slot, m : m + 64, :wide]
            for offset in (0, HIDDEN):
                slope = slopes_ref[m : m + 64, offset + lo : offset + hi].astype(F32)
                joined_ref[m : m + 64, offset + lo : offset + hi] = (hidden_grad * slope).astype(BF16)
    outgoing = []
    quarter = WIDTH // 4

    def send(start, wide, index):
        cols = pl.ds(start, wide)
        copy = pltpu.make_async_copy(out_ref.at[:, cols], out_hbm.at[:, cols], out_sems.at[index])
        copy.start()
        outgoing.append(copy)

    for n in range(0, WIDTH, TILE):
        result = dot_cols(joined_ref[...], w_ref[n : n + TILE, :]).astype(BF16)
        out_ref[:, n : n + TILE] = result[:SLOTS]
        j, within = n // quarter, n % quarter
        extra_ref[j * SPARE : (j + 1) * SPARE, within : within + TILE] = result[SLOTS:]
        if n % quarter:
            send(j * quarter, quarter, j)
    out_ref[:, WIDTH:] = dot(packer(), extra_ref[...]).astype(BF16)
    send(WIDTH, quarter, 4)
    for copy in outgoing:
        copy.wait()


def head_kernel(
    core_ref, hidden_ref, grads_ref, tokens_ref, embed_grad_ref, down_ref, own_ref, other_ref
):
    first = core_ref[0] == 0
    inner = dot_rows(hidden_ref[...], grads_ref[...]).astype(BF16)
    for n in range(0, WIDTH, TILE):
        part = dot_rows(down_ref[:, n : n + TILE], inner)
        part = part + dot_rows(tokens_ref[:, n : n + TILE], embed_grad_ref[...])
        for b in range(TILE // 32):
            row = n // 2 + 16 * b
            even, odd = part[32 * b : 32 * b + 16], part[32 * b + 16 : 32 * b + 32]
            own_ref[row : row + 16, :] = jnp.where(first, even, odd)
            other_ref[row : row + 16, :] = jnp.where(first, odd, even).astype(BF16)


def share_kernel(place_ref, own_ref, *refs):
    received, (kept_ref, *sent_refs) = refs[: len(refs) - 4], refs[len(refs) - 4 :]
    place = place_ref[0]
    for k in range(4):
        quarter = jnp.bitwise_xor(place, k)
        total = own_ref[quarter]
        for ref in received:
            total = total + ref[quarter].astype(F32)
        if k == 0:
            kept_ref[...] = total
        else:
            sent_refs[k - 1][...] = total.astype(BF16)


def combine_kernel(routes_ref, back_ref, direct_ref, out_ref):
    main, quarters = choosers(routes_ref[...])
    main = one_hot(main)
    quarter = WIDTH // 4
    for j in range(4):
        cols = slice(j * quarter, (j + 1) * quarter)
        total = dot_rows(main, back_ref[:, cols]) + dot_rows(one_hot(quarters[j]), back_ref[:, WIDTH:])
        out_ref[:, cols] = (direct_ref[:, cols] + total).astype(BF16)


def call(kernel, outs, ins, scratch=(), flops=0, moved=0):
    def spec(space):
        return pl.BlockSpec(memory_space=space)

    return pl.pallas_call(
        kernel,
        out_shape=tuple(jax.ShapeDtypeStruct(shape, dtype) for shape, dtype, _ in outs),
        in_specs=[spec(space) for _, space in ins],
        out_specs=tuple(spec(space) for _, _, space in outs),
        scratch_shapes=scratch,
        compiler_params=pltpu.CompilerParams(vmem_limit_bytes=VMEM_LIMIT),
        cost_estimate=pl.CostEstimate(flops=flops, bytes_accessed=moved, transcendentals=0),
    )(*[value for value, _ in ins])


def exchanged(value, axes, parts):
    rows, width = value.shape
    blocks = value.reshape(parts, rows // parts, width)
    return lax.all_to_all(blocks, axes, 0, 0, tiled=True).reshape(rows, width)


def body(tokens, routes, gates, gate_up, down_proj, projection, matches):
    vmem, hbm, smem = pltpu.VMEM, pltpu.HBM, pltpu.SMEM
    routes, gates = routes.T, gates.T
    weights_joined, weights_down = gate_up[0], down_proj[0]
    partner = [(i, i ^ EXPERTS // 2) for i in range(EXPERTS)]
    dma = pltpu.SemaphoreType.DMA

    (dispatch,) = call(
        dispatch_kernel, [((SLOTS, WIDTH * 5 // 4), BF16, hbm)], [(routes, hbm), (tokens, hbm)],
        scratch=[
            pltpu.VMEM((TOP, ROWS), jnp.int32),
            pltpu.VMEM((ROWS, WIDTH), BF16),
            pltpu.VMEM((SLOTS, WIDTH * 5 // 4), BF16),
            dma((2,)),
            dma((5,)),
        ],
        flops=2 * SLOTS * ROWS * WIDTH * 2, moved=3 << 20,
    )
    partner_matches = lax.ppermute(matches.astype(BF16), EXPERT, partner)
    received = exchanged(dispatch, EXPERT, EXPERTS)
    mixed = dot(weights_down, projection).astype(BF16)
    base = dot(tokens, projection)
    received, partner_matches = lax.optimization_barrier((received, partner_matches))

    packed_shape = (SLOTS, EMBED * 5 // 4)
    packed, hidden, slopes = call(
        forward_kernel,
        [(packed_shape, BF16, hbm), ((TOTAL, HIDDEN), BF16, vmem), ((TOTAL, 2 * HIDDEN), BF16, vmem)],
        [(received, hbm), (weights_joined, vmem), (mixed, vmem)],
        scratch=[
            pltpu.VMEM((TOTAL, WIDTH), BF16),
            pltpu.VMEM((SLOTS, WIDTH // 4), BF16),
            pltpu.VMEM((2, 2, TOTAL, 256), F32),
            pltpu.VMEM(packed_shape, BF16),
            dma((2,)),
            dma((2,)),
        ],
        flops=2 * TOTAL * HIDDEN * (2 * WIDTH + EMBED), moved=22 << 20,
    )
    answer = exchanged(packed, EXPERT, EXPERTS)
    embedding, unit = call(
        embed_kernel,
        [((ROWS, EMBED), F32, vmem), ((ROWS, EMBED), BF16, vmem)],
        [(routes, vmem), (gates, vmem), (answer, vmem), (base, vmem)],
        flops=4 * SLOTS * ROWS * EMBED * 2, moved=2 << 20,
    )
    keys = lax.ppermute(unit, EXPERT, partner)
    row_loss, embed_grad, slot_grads = call(
        loss_kernel,
        [((1, ROWS), F32, vmem), ((ROWS, EMBED), BF16, vmem), (packed_shape, BF16, vmem)],
        [(routes, vmem), (gates, vmem), (matches, vmem), (partner_matches, vmem),
         (embedding, vmem), (unit, vmem), (keys, vmem)],
        flops=2 * SLOTS * ROWS * EMBED * 2, moved=2 << 20,
    )
    arrived = exchanged(slot_grads, EXPERT, EXPERTS)
    direct = dot_cols(embed_grad, projection)
    input_grads, grads = call(
        backward_kernel,
        [((SLOTS, WIDTH * 5 // 4), BF16, hbm), ((TOTAL, EMBED), BF16, vmem)],
        [(arrived, vmem), (mixed, vmem), (slopes, vmem), (weights_joined, vmem)],
        scratch=[
            pltpu.VMEM((2, TOTAL, 256), F32),
            pltpu.VMEM((TOTAL, 2 * HIDDEN), BF16),
            pltpu.VMEM((SLOTS, WIDTH // 4), BF16),
            pltpu.VMEM((SLOTS, WIDTH * 5 // 4), BF16),
            dma((5,)),
        ],
        flops=2 * TOTAL * HIDDEN * (2 * WIDTH + EMBED), moved=22 << 20,
    )
    back = exchanged(input_grads, EXPERT, EXPERTS)

    def place(axis):
        return lax.axis_index(axis).astype(jnp.int32).reshape(1), smem

    own, other = call(
        head_kernel,
        [((WIDTH // 2, EMBED), F32, vmem), ((WIDTH // 2, EMBED), BF16, vmem)],
        [place("expert_2"), (hidden, vmem), (grads, vmem), (tokens, vmem), (embed_grad, vmem),
         (weights_down, vmem)],
    )
    arrivals = [lax.ppermute(other, "expert_2", [(0, 1), (1, 0)])]
    for axis in ("dp", "expert_0", "expert_1"):
        rows = own.shape[0] // 4
        own, *sent = call(
            share_kernel,
            [((rows, EMBED), F32, vmem)] + [((rows, EMBED), BF16, vmem)] * 3,
            [place(axis), (own.reshape(4, rows, EMBED), vmem)]
            + [(value.reshape(4, rows, EMBED), vmem) for value in arrivals],
        )
        arrivals = [
            lax.ppermute(value, axis, [(i, i ^ (k + 1)) for i in range(4)])
            for k, value in enumerate(sent)
        ]
    summed = own
    for value in arrivals:
        summed = summed + value.astype(F32)
    device_count = lax.axis_size("dp") * EXPERTS
    grad_projection = summed * (1.0 / math.sqrt(ROWS * device_count))
    (grad_tokens,) = call(
        combine_kernel, [((ROWS, WIDTH), BF16, vmem)], [(routes, vmem), (back, vmem), (direct, vmem)],
        flops=2 * SLOTS * ROWS * WIDTH * 2, moved=4 << 20,
    )
    return grad_tokens, grad_projection, row_loss.reshape(ROWS)


def solution(mesh):
    torus = Mesh(
        mesh.devices.reshape(mesh.shape["dp"], 4, 4, 2), ("dp", "expert_0", "expert_1", "expert_2")
    )
    return jax.shard_map(
        body,
        mesh=torus,
        in_specs=(
            P(DP_EXPERT, None),
            P(DP_EXPERT, None),
            P(DP_EXPERT, None),
            P(EXPERT, None, None),
            P(EXPERT, None, None),
            P(),
            P(DP_EXPERT, None),
        ),
        out_specs=(P(DP_EXPERT, None), P(DP_EXPERT, None), P(DP_EXPERT)),
        check_vma=False,
    )
```

```python
import functools
import math

import jax
import jax.numpy as jnp
from jax import lax
from jax.experimental import pallas as pl
from jax.experimental.pallas import tpu as pltpu
from jax.sharding import Mesh
from jax.sharding import PartitionSpec as P

EXPERT = ("expert_0", "expert_1", "expert_2")
DP_EXPERT = ("dp", "expert_0", "expert_1", "expert_2")

TEMPER = 0.1
EPSILON = 1e-06
ROWS = 128
TOP = 4
WIDTH = 2048
HIDDEN = 1408
EMBED = 512
EXPERTS = 32
MAIN = 16
EXTRA = 4
SLOTS = EXPERTS * MAIN
SPARE = EXPERTS * EXTRA
TOTAL = SLOTS + SPARE
CHUNKS = tuple((lo, min(lo + 256, HIDDEN)) for lo in range(0, HIDDEN, 256))
TILE = 256
F32 = jnp.float32
BF16 = jnp.bfloat16
WHOLE = 60


def dot(left, right):
    return jnp.dot(left, right, preferred_element_type=F32)


def dot_rows(left, right):
    return lax.dot_general(left, right, (((0,), (0,)), ((), ())), preferred_element_type=F32)


def dot_cols(left, right):
    return lax.dot_general(left, right, (((1,), (1,)), ((), ())), preferred_element_type=F32)


def iota(shape, dim):
    return lax.broadcasted_iota(jnp.int32, shape, dim)


def expanded(table):
    spread = jnp.broadcast_to(table[:, None, :], (EXPERTS, MAIN, ROWS))
    return spread.reshape(SLOTS, ROWS)


def ranks(routes):
    experts = iota((EXPERTS, ROWS), 0)
    member = jnp.zeros((EXPERTS, ROWS), F32)
    for k in range(TOP):
        member = member + jnp.where(routes[k : k + 1, :] == experts, 1.0, 0.0)
    earlier = jnp.where(iota((ROWS, ROWS), 0) < iota((ROWS, ROWS), 1), 1.0, 0.0)
    rank = dot(member.astype(BF16), earlier.astype(BF16))
    return jnp.where(member > 0.0, rank, -1.0)


def pair_gates(routes, gates):
    experts = iota((EXPERTS, ROWS), 0)
    total = jnp.zeros((EXPERTS, ROWS), F32)
    for k in range(TOP):
        total = total + jnp.where(routes[k : k + 1, :] == experts, gates[k : k + 1, :], 0.0)
    return total


def choosers(routes):
    rank = expanded(ranks(routes))
    place = iota((SLOTS, ROWS), 0) % MAIN
    main = rank == place.astype(F32)
    extra = rank == (MAIN + place % EXTRA).astype(F32)
    quarters = [extra & (place // EXTRA == j) for j in range(MAIN // EXTRA)]
    return main, quarters


def one_hot(chosen):
    return jnp.where(chosen, 1.0, 0.0).astype(BF16)


def unpacker():
    row = iota((SLOTS, SLOTS), 0)
    wanted = (row % SPARE) // EXTRA * MAIN + row // SPARE * EXTRA + row % EXTRA
    return one_hot(iota((SLOTS, SLOTS), 1) == wanted)


def packer():
    row = iota((SLOTS, SLOTS), 0)
    wanted = (row % MAIN) // EXTRA * SPARE + row // MAIN * EXTRA + row % EXTRA
    return one_hot(iota((SLOTS, SLOTS), 1) == wanted)


def dispatch_kernel(routes_hbm, tokens_hbm, out_hbm, routes_ref, tokens_ref, out_ref, sems, out_sems):
    routes_copy = pltpu.make_async_copy(routes_hbm, routes_ref, sems.at[0])
    tokens_copy = pltpu.make_async_copy(tokens_hbm, tokens_ref, sems.at[1])
    routes_copy.start()
    tokens_copy.start()
    routes_copy.wait()
    main, quarters = choosers(routes_ref[...])
    main = one_hot(main)
    quarter = WIDTH // 4
    total = jnp.zeros((SLOTS, quarter), F32)
    tokens_copy.wait()
    outgoing = []
    for j in range(5):
        cols = slice(j * quarter, (j + 1) * quarter)
        if j < 4:
            out_ref[:, cols] = dot(main, tokens_ref[:, cols]).astype(BF16)
            total = total + dot(one_hot(quarters[j]), tokens_ref[:, cols])
        else:
            out_ref[:, cols] = total.astype(BF16)
        part = pl.ds(j * quarter, quarter)
        copy = pltpu.make_async_copy(out_ref.at[:, part], out_hbm.at[:, part], out_sems.at[j])
        copy.start()
        outgoing.append(copy)
    for copy in outgoing:
        copy.wait()


def prepare_kernel(down_hbm, head_hbm, tokens_hbm, mixed_ref, base_ref, down_ref, head_ref, tokens_ref, sems):
    copies = [
        pltpu.make_async_copy(source, target, sems.at[i])
        for i, (source, target) in enumerate(
            ((head_hbm, head_ref), (tokens_hbm, tokens_ref), (down_hbm, down_ref))
        )
    ]
    for copy in copies:
        copy.start()
    copies[0].wait()
    copies[1].wait()
    base_ref[...] = dot(tokens_ref[...], head_ref[...])
    copies[2].wait()
    mixed_ref[...] = dot(down_ref[...], head_ref[...]).astype(BF16)


def forward_kernel(
    recv_hbm, w_hbm, mixed_hbm, out_hbm, hidden_hbm, slopes_hbm,
    x_ref, extra_ref, act_ref, w_ref, mixed_ref, hidden_ref, slopes_ref, out_ref, sems, out_sems,
):
    quarter = WIDTH // 4

    def bring(source, target, index):
        copy = pltpu.make_async_copy(source, target, sems.at[index])
        copy.start()
        return copy

    extra_copy = bring(recv_hbm.at[:, pl.ds(WIDTH, quarter)], extra_ref, 0)
    main_copy = bring(recv_hbm.at[:, pl.ds(0, WIDTH)], x_ref.at[pl.ds(0, SLOTS), :], 1)
    weight_copies = []
    for c, (lo, hi) in enumerate(CHUNKS):
        for h in range(2):
            cols = pl.ds(h * HIDDEN + lo, hi - lo)
            weight_copies.append(bring(w_hbm.at[:, cols], w_ref.at[:, cols], 3 + 2 * c + h))
    mixed_copy = bring(mixed_hbm, mixed_ref, 2)
    turned = unpacker()
    extra_copy.wait()
    spread = dot(turned, extra_ref[...]).astype(BF16)
    for j in range(4):
        x_ref[SLOTS:, j * quarter : (j + 1) * quarter] = spread[j * SPARE : (j + 1) * SPARE]
    main_copy.wait()
    outgoing = []

    def send(source, target, lo, wide):
        cols = pl.ds(lo, wide)
        copy = pltpu.make_async_copy(source.at[:, cols], target.at[:, cols], out_sems.at[len(outgoing)])
        copy.start()
        outgoing.append(copy)

    sent = 0
    for c, (lo, hi) in enumerate(CHUNKS):
        slot = c % 2
        wide = hi - lo
        weight_copies[2 * c].wait()
        weight_copies[2 * c + 1].wait()
        act_ref[slot, 0, :, :wide] = dot(x_ref[...], w_ref[:, lo:hi])
        act_ref[slot, 1, :, :wide] = dot(x_ref[...], w_ref[:, HIDDEN + lo : HIDDEN + hi])
        for m in range(0, TOTAL, 64):
            gate = act_ref[slot, 0, m : m + 64, :wide]
            up = act_ref[slot, 1, m : m + 64, :wide]
            sigmoid = 0.5 + 0.5 * jnp.tanh(0.5 * gate)
            silu = gate * sigmoid
            hidden_ref[m : m + 64, lo:hi] = (silu * up).astype(BF16)
            slopes_ref[m : m + 64, HIDDEN + lo : HIDDEN + hi] = silu.astype(BF16)
            slopes_ref[m : m + 64, lo:hi] = (up * sigmoid * (1.0 + gate * (1.0 - sigmoid))).astype(BF16)
        if c % 3 == 2:
            send(hidden_ref, hidden_hbm, sent, hi - sent)
            send(slopes_ref, slopes_hbm, sent, hi - sent)
            send(slopes_ref, slopes_hbm, HIDDEN + sent, hi - sent)
            sent = hi
    mixed_copy.wait()
    projected = dot(hidden_ref[...], mixed_ref[...]).astype(BF16)
    out_ref[:, :EMBED] = projected[:SLOTS]
    send(out_ref, out_hbm, 0, EMBED)
    quarter = EMBED // 4
    stacked = jnp.concatenate(
        [projected[SLOTS:, j * quarter : (j + 1) * quarter] for j in range(4)], axis=0
    )
    out_ref[:, EMBED:] = dot(packer(), stacked).astype(BF16)
    send(out_ref, out_hbm, EMBED, quarter)
    for copy in outgoing:
        copy.wait()


def weighted(chosen, gates):
    return jnp.where(chosen, gates, 0.0)


def split_product(chosen, gates, values):
    whole = weighted(chosen, gates)
    high = whole.astype(BF16)
    low = (whole - high.astype(F32)).astype(BF16)
    return dot_rows(high, values) + dot_rows(low, values)


def embed_kernel(routes_ref, gates_ref, answer_ref, base_ref, embedding_ref, unit_ref):
    main, quarters = choosers(routes_ref[...])
    gates = expanded(pair_gates(routes_ref[...], gates_ref[...]))
    mixture = split_product(main, gates, answer_ref[:, :EMBED])
    extra = jnp.concatenate(
        [split_product(quarters[j], gates, answer_ref[:, EMBED:]) for j in range(4)], axis=1
    )
    embedding = base_ref[...] + mixture + extra
    inverse = lax.rsqrt(jnp.mean(embedding * embedding, axis=1, keepdims=True) + EPSILON)
    embedding_ref[...] = embedding
    unit_ref[...] = (embedding * inverse).astype(BF16)


def loss_kernel(
    routes_ref, gates_ref, matches_ref, partner_ref, embedding_ref, unit_ref, key_ref,
    loss_ref, grad_ref, out_ref,
):
    embedding = embedding_ref[...]
    unit = unit_ref[...]
    keys = key_ref[...]
    coefficient = 1.0 / (EMBED * TEMPER)
    inverse = lax.rsqrt(jnp.mean(embedding * embedding, axis=1, keepdims=True) + EPSILON)
    unit_rows = embedding * inverse
    entry = iota((ROWS, ROWS), 0)

    def scores(rows, columns, matches):
        logits = dot_cols(rows, columns) * coefficient
        totals = jnp.log(jnp.sum(jnp.exp(logits), axis=0, keepdims=True))
        target = matches == entry
        chosen = jnp.sum(jnp.where(target, logits, 0.0), axis=0, keepdims=True)
        weights = jnp.exp(logits - totals) - jnp.where(target, 1.0, 0.0)
        return totals - chosen, weights.astype(BF16)

    loss, own = scores(keys, unit, matches_ref[...])
    loss_ref[...] = loss
    partner = scores(unit, keys, partner_ref[...].astype(jnp.int32))[1]
    upstream = (dot_rows(own, keys) + dot(partner, keys)) * coefficient
    grad = inverse * (upstream - unit_rows * jnp.mean(upstream * unit_rows, axis=1, keepdims=True))
    grad = grad.astype(BF16)
    grad_ref[...] = grad
    main, quarters = choosers(routes_ref[...])
    gates = expanded(pair_gates(routes_ref[...], gates_ref[...]))
    slot_gates = jnp.sum(weighted(main, gates), axis=1, keepdims=True)
    out_ref[:, :EMBED] = (slot_gates * dot(one_hot(main), grad)).astype(BF16)
    quarter = EMBED // 4
    total = jnp.zeros((SLOTS, quarter), F32)
    extra_gates = jnp.zeros((SLOTS, 1), F32)
    for j in range(4):
        total = total + dot(one_hot(quarters[j]), grad[:, j * quarter : (j + 1) * quarter])
        extra_gates = extra_gates + jnp.sum(weighted(quarters[j], gates), axis=1, keepdims=True)
    out_ref[:, EMBED:] = (extra_gates * total).astype(BF16)


def head_kernel(
    arrived_ref, tokens_ref, embed_grad_ref, hidden_hbm, down_hbm, grads_ref, own_hbm, other_hbm,
    hidden_ref, down_ref, own_ref, other_ref, sems, out_sems,
):
    hidden_copy = pltpu.make_async_copy(hidden_hbm, hidden_ref, sems.at[0])
    hidden_copy.start()
    step = WIDTH // 4
    down_copies = []
    for i in range(4):
        cols = pl.ds(i * step, step)
        copy = pltpu.make_async_copy(down_hbm.at[:, cols], down_ref.at[:, cols], sems.at[1 + i])
        copy.start()
        down_copies.append(copy)
    quarter = EMBED // 4
    grads_ref[:SLOTS, :] = arrived_ref[:, :EMBED]
    spread = dot(unpacker(), arrived_ref[:, EMBED:]).astype(BF16)
    for j in range(4):
        grads_ref[SLOTS:, j * quarter : (j + 1) * quarter] = spread[j * SPARE : (j + 1) * SPARE]
    first = lax.axis_index("expert_2") == 0
    hidden_copy.wait()
    inner = dot_rows(hidden_ref[...], grads_ref[...]).astype(BF16)
    for n in range(0, WIDTH, TILE):
        if n % step == 0:
            down_copies[n // step].wait()
        part = dot_rows(down_ref[:, n : n + TILE], inner)
        part = part + dot_rows(tokens_ref[:, n : n + TILE], embed_grad_ref[...])
        for b in range(TILE // 32):
            row = n // 2 + 16 * b
            even, odd = part[32 * b : 32 * b + 16], part[32 * b + 16 : 32 * b + 32]
            own_ref[row : row + 16, :] = jnp.where(first, even, odd)
            other_ref[row : row + 16, :] = jnp.where(first, odd, even).astype(BF16)
    other_copy = pltpu.make_async_copy(other_ref, other_hbm, out_sems.at[0])
    own_copy = pltpu.make_async_copy(own_ref, own_hbm, out_sems.at[1])
    other_copy.start()
    own_copy.start()
    other_copy.wait()
    own_copy.wait()


def joined_kernel(grads_ref, mixed_hbm, slopes_hbm, joined_ref, mixed_ref, slopes_ref, act_ref, sems):
    def bring(source, target, index):
        copy = pltpu.make_async_copy(source, target, sems.at[index])
        copy.start()
        return copy

    mixed_copy = bring(mixed_hbm, mixed_ref, 0)
    slopes_copies = []
    for c, (lo, hi) in enumerate(CHUNKS):
        for h in range(2):
            cols = pl.ds(h * HIDDEN + lo, hi - lo)
            slopes_copies.append(bring(slopes_hbm.at[:, cols], slopes_ref.at[:, cols], 1 + 2 * c + h))
    mixed_copy.wait()
    for c, (lo, hi) in enumerate(CHUNKS):
        slot = c % 2
        wide = hi - lo
        act_ref[slot, :, :wide] = dot_cols(grads_ref[...], mixed_ref[lo:hi, :])
        slopes_copies[2 * c].wait()
        slopes_copies[2 * c + 1].wait()
        for m in range(0, TOTAL, 64):
            hidden_grad = act_ref[slot, m : m + 64, :wide]
            for offset in (0, HIDDEN):
                slope = slopes_ref[m : m + 64, offset + lo : offset + hi].astype(F32)
                joined_ref[m : m + 64, offset + lo : offset + hi] = (hidden_grad * slope).astype(BF16)


def input_kernel(joined_ref, w_hbm, _, out_hbm, w_ref, extra_ref, out_ref, sems, out_sems):
    step = WIDTH // 4
    weight_copies = []
    for n in range(0, WIDTH, TILE):
        rows = pl.ds(n, TILE)
        copy = pltpu.make_async_copy(w_hbm.at[rows, :], w_ref.at[rows, :], sems.at[n // TILE])
        copy.start()
        weight_copies.append(copy)
    outgoing = []

    def send(start, wide, index):
        cols = pl.ds(start, wide)
        copy = pltpu.make_async_copy(out_ref.at[:, cols], out_hbm.at[:, cols], out_sems.at[index])
        copy.start()
        outgoing.append(copy)

    for n in range(0, WIDTH, TILE):
        weight_copies[n // TILE].wait()
        result = dot_cols(joined_ref[...], w_ref[n : n + TILE, :]).astype(BF16)
        out_ref[:, n : n + TILE] = result[:SLOTS]
        j, within = n // step, n % step
        extra_ref[j * SPARE : (j + 1) * SPARE, within : within + TILE] = result[SLOTS:]
        if within:
            send(j * step, step, j)
    out_ref[:, WIDTH:] = dot(packer(), extra_ref[...]).astype(BF16)
    send(WIDTH, step, 4)
    for copy in outgoing:
        copy.wait()


def share_kernel(axis, count, own_hbm, *refs):
    received_hbm, outs = refs[:count], refs[count : count + 4]
    own_ref, received_ref, total_ref, sent_ref, sems, out_sems = refs[count + 4 :]
    copies = [pltpu.make_async_copy(own_hbm, own_ref, sems.at[count])]
    for k in range(count):
        copies.append(pltpu.make_async_copy(received_hbm[k], received_ref.at[k], sems.at[k]))
    for copy in copies:
        copy.start()
    for copy in copies:
        copy.wait()
    place = lax.axis_index(axis)
    outgoing = []
    for k in (2, 1, 3, 0):
        quarter = jnp.bitwise_xor(place, k)
        total = own_ref[quarter]
        for i in range(count):
            total = total + received_ref[i, quarter].astype(F32)
        if k:
            sent_ref[k - 1] = total.astype(BF16)
            copy = pltpu.make_async_copy(sent_ref.at[k - 1], outs[k], out_sems.at[k])
        else:
            total_ref[...] = total
            copy = pltpu.make_async_copy(total_ref, outs[0], out_sems.at[0])
        copy.start()
        outgoing.append(copy)
    for copy in outgoing:
        copy.wait()


def combine_kernel(routes_ref, direct_ref, back_hbm, out_ref, back_ref, sems):
    quarter = WIDTH // 4
    copies = []
    for n, j in enumerate((4, 0, 1, 2, 3)):
        cols = pl.ds(j * quarter, quarter)
        copy = pltpu.make_async_copy(back_hbm.at[:, cols], back_ref.at[:, cols], sems.at[n])
        copy.start()
        copies.append(copy)
    main, quarters = choosers(routes_ref[...])
    main = one_hot(main).T
    quarters = [one_hot(chosen).T for chosen in quarters]
    copies[0].wait()
    for j in range(4):
        cols = slice(j * quarter, (j + 1) * quarter)
        extra = dot(quarters[j], back_ref[:, WIDTH:])
        copies[j + 1].wait()
        total = dot(main, back_ref[:, cols]) + extra
        out_ref[:, cols] = (direct_ref[:, cols] + total).astype(BF16)


def call(kernel, outs, ins, scratch=(), flops=0, moved=0, limit=24):
    def spec(space):
        return pl.BlockSpec(memory_space=space)

    return pl.pallas_call(
        kernel,
        out_shape=tuple(jax.ShapeDtypeStruct(shape, dtype) for shape, dtype, _ in outs),
        in_specs=[spec(space) for _, space in ins],
        out_specs=tuple(spec(space) for _, _, space in outs),
        scratch_shapes=scratch,
        compiler_params=pltpu.CompilerParams(vmem_limit_bytes=int(limit * 1048576)),
        cost_estimate=pl.CostEstimate(flops=flops, bytes_accessed=moved, transcendentals=0),
    )(*[value for value, _ in ins])


def exchanged(value, axes, parts):
    rows, width = value.shape
    blocks = value.reshape(parts, rows // parts, width)
    return lax.all_to_all(blocks, axes, 0, 0, tiled=True).reshape(rows, width)


def body(tokens, routes, gates, gate_up, down_proj, projection, matches):
    vmem, hbm = pltpu.VMEM, pl.ANY
    routes, gates = routes.T, gates.T
    weights_joined, weights_down = gate_up[0], down_proj[0]
    partner = [(i, i ^ EXPERTS // 2) for i in range(EXPERTS)]
    dma = pltpu.SemaphoreType.DMA
    wide_shape, packed_shape = (SLOTS, WIDTH * 5 // 4), (SLOTS, EMBED * 5 // 4)

    (dispatch,) = call(
        dispatch_kernel, [(wide_shape, BF16, hbm)], [(routes, hbm), (tokens, hbm)],
        scratch=[
            pltpu.VMEM((TOP, ROWS), jnp.int32),
            pltpu.VMEM((ROWS, WIDTH), BF16),
            pltpu.VMEM(wide_shape, BF16),
            dma((2,)),
            dma((5,)),
        ],
        flops=2 * SLOTS * ROWS * WIDTH * 2, moved=3 << 20, limit=WHOLE,
    )
    partner_matches = lax.ppermute(matches.astype(BF16), EXPERT, partner)
    received = exchanged(dispatch, EXPERT, EXPERTS)
    mixed, base = call(
        prepare_kernel,
        [((HIDDEN, EMBED), BF16, vmem), ((ROWS, EMBED), F32, vmem)],
        [(weights_down, hbm), (projection, hbm), (tokens, hbm)],
        scratch=[
            pltpu.VMEM((HIDDEN, WIDTH), BF16),
            pltpu.VMEM((WIDTH, EMBED), BF16),
            pltpu.VMEM((ROWS, WIDTH), BF16),
            dma((3,)),
        ],
        flops=2 * (HIDDEN + ROWS) * WIDTH * EMBED, moved=8 << 20, limit=WHOLE,
    )
    received, partner_matches, base = lax.optimization_barrier((received, partner_matches, base))

    packed, hidden, slopes = call(
        forward_kernel,
        [(packed_shape, BF16, hbm), ((TOTAL, HIDDEN), BF16, hbm), ((TOTAL, 2 * HIDDEN), BF16, hbm)],
        [(received, hbm), (weights_joined, hbm), (mixed, hbm)],
        scratch=[
            pltpu.VMEM((TOTAL, WIDTH), BF16),
            pltpu.VMEM((SLOTS, WIDTH // 4), BF16),
            pltpu.VMEM((2, 2, TOTAL, 256), F32),
            pltpu.VMEM((WIDTH, 2 * HIDDEN), BF16),
            pltpu.VMEM((HIDDEN, EMBED), BF16),
            pltpu.VMEM((TOTAL, HIDDEN), BF16),
            pltpu.VMEM((TOTAL, 2 * HIDDEN), BF16),
            pltpu.VMEM(packed_shape, BF16),
            dma((3 + 2 * len(CHUNKS),)),
            dma((8,)),
        ],
        flops=2 * TOTAL * HIDDEN * (2 * WIDTH + EMBED), moved=22 << 20, limit=55,
    )
    answer = exchanged(packed, EXPERT, EXPERTS)
    embedding, unit = call(
        embed_kernel,
        [((ROWS, EMBED), F32, vmem), ((ROWS, EMBED), BF16, vmem)],
        [(routes, vmem), (gates, vmem), (answer, vmem), (base, vmem)],
        flops=4 * SLOTS * ROWS * EMBED * 2, moved=2 << 20,
    )
    keys = lax.ppermute(unit, EXPERT, partner)
    row_loss, embed_grad, slot_grads = call(
        loss_kernel,
        [((1, ROWS), F32, vmem), ((ROWS, EMBED), BF16, vmem), (packed_shape, BF16, vmem)],
        [(routes, vmem), (gates, vmem), (matches, vmem), (partner_matches, vmem),
         (embedding, vmem), (unit, vmem), (keys, vmem)],
        flops=2 * SLOTS * ROWS * EMBED * 2, moved=2 << 20, limit=16,
    )
    arrived = exchanged(slot_grads, EXPERT, EXPERTS)
    half_shape = (WIDTH // 2, EMBED)
    grads, own, other = call(
        head_kernel,
        [((TOTAL, EMBED), BF16, vmem), (half_shape, F32, hbm), (half_shape, BF16, hbm)],
        [(arrived, vmem), (tokens, vmem), (embed_grad, vmem), (hidden, hbm), (weights_down, hbm)],
        scratch=[
            pltpu.VMEM((TOTAL, HIDDEN), BF16),
            pltpu.VMEM((HIDDEN, WIDTH), BF16),
            pltpu.VMEM(half_shape, F32),
            pltpu.VMEM(half_shape, BF16),
            dma((5,)),
            dma((2,)),
        ],
        flops=2 * HIDDEN * EMBED * (TOTAL + WIDTH), moved=12 << 20, limit=59,
    )
    arrivals = [lax.ppermute(other, "expert_2", [(0, 1), (1, 0)])]
    joined_shape = (TOTAL, 2 * HIDDEN)
    (joined_grad,) = call(
        joined_kernel,
        [(joined_shape, BF16, vmem)],
        [(grads, vmem), (mixed, hbm), (slopes, hbm)],
        scratch=[
            pltpu.VMEM((HIDDEN, EMBED), BF16),
            pltpu.VMEM(joined_shape, BF16),
            pltpu.VMEM((2, TOTAL, 256), F32),
            dma((1 + 2 * len(CHUNKS),)),
        ],
        flops=2 * TOTAL * HIDDEN * EMBED, moved=8 << 20, limit=54,
    )
    (input_grads,) = call(
        input_kernel,
        [(wide_shape, BF16, hbm)],
        [(joined_grad, vmem), (weights_joined, hbm), (arrivals[0], hbm)],
        scratch=[
            pltpu.VMEM((WIDTH, 2 * HIDDEN), BF16),
            pltpu.VMEM((SLOTS, WIDTH // 4), BF16),
            pltpu.VMEM(wide_shape, BF16),
            dma((WIDTH // TILE,)),
            dma((5,)),
        ],
        flops=4 * TOTAL * HIDDEN * WIDTH, moved=18 << 20, limit=54,
    )
    back = exchanged(input_grads, EXPERT, EXPERTS)
    direct = dot_cols(embed_grad, projection)
    for axis in ("dp", "expert_0", "expert_1"):
        rows, count = own.shape[0] // 4, len(arrivals)
        own, *sent = call(
            functools.partial(share_kernel, axis, count),
            [((rows, EMBED), F32, hbm)] + [((rows, EMBED), BF16, hbm)] * 3,
            [(own.reshape(4, rows, EMBED), hbm)]
            + [(value.reshape(4, rows, EMBED), hbm) for value in arrivals],
            scratch=[
                pltpu.VMEM((4, rows, EMBED), F32),
                pltpu.VMEM((count, 4, rows, EMBED), BF16),
                pltpu.VMEM((rows, EMBED), F32),
                pltpu.VMEM((3, rows, EMBED), BF16),
                dma((1 + count,)),
                dma((4,)),
            ],
            limit=16,
        )
        arrivals = [
            lax.ppermute(value, axis, [(i, i ^ (k + 1)) for i in range(4)])
            for k, value in enumerate(sent)
        ]
    summed = own
    for value in arrivals:
        summed = summed + value.astype(F32)
    device_count = lax.axis_size("dp") * EXPERTS
    grad_projection = summed * (1.0 / math.sqrt(ROWS * device_count))
    (grad_tokens,) = call(
        combine_kernel, [((ROWS, WIDTH), BF16, vmem)], [(routes, vmem), (direct, vmem), (back, hbm)],
        scratch=[pltpu.VMEM(wide_shape, BF16), dma((5,))],
        flops=2 * SLOTS * ROWS * WIDTH * 2, moved=4 << 20, limit=WHOLE,
    )
    return grad_tokens, grad_projection, row_loss.reshape(ROWS)


def solution(mesh):
    torus = Mesh(
        mesh.devices.reshape(mesh.shape["dp"], 4, 4, 2), ("dp", "expert_0", "expert_1", "expert_2")
    )
    return jax.shard_map(
        body,
        mesh=torus,
        in_specs=(
            P(DP_EXPERT, None),
            P(DP_EXPERT, None),
            P(DP_EXPERT, None),
            P(EXPERT, None, None),
            P(EXPERT, None, None),
            P(),
            P(DP_EXPERT, None),
        ),
        out_specs=(P(DP_EXPERT, None), P(DP_EXPERT, None), P(DP_EXPERT)),
        check_vma=False,
    )
```

```python
import functools
import math

import jax
import jax.numpy as jnp
from jax import lax
from jax.experimental import pallas as pl
from jax.experimental.pallas import tpu as pltpu
from jax.sharding import Mesh
from jax.sharding import PartitionSpec as P

EXPERT = ("expert_0", "expert_1", "expert_2")
DP_EXPERT = ("dp", "expert_0", "expert_1", "expert_2")

TEMPER = 0.1
EPSILON = 1e-06
ROWS = 128
TOP = 4
WIDTH = 2048
HIDDEN = 1408
EMBED = 512
EXPERTS = 32
MAIN = 16
EXTRA = 4
SLOTS = EXPERTS * MAIN
SPARE = EXPERTS * EXTRA
TOTAL = SLOTS + SPARE
CHUNKS = tuple((lo, min(lo + 256, HIDDEN)) for lo in range(0, HIDDEN, 256))
TILE = 256
F32 = jnp.float32
BF16 = jnp.bfloat16
WHOLE = 60


def dot(left, right):
    return jnp.dot(left, right, preferred_element_type=F32)


def dot_rows(left, right):
    return lax.dot_general(left, right, (((0,), (0,)), ((), ())), preferred_element_type=F32)


def dot_cols(left, right):
    return lax.dot_general(left, right, (((1,), (1,)), ((), ())), preferred_element_type=F32)


def iota(shape, dim):
    return lax.broadcasted_iota(jnp.int32, shape, dim)


def expanded(table):
    spread = jnp.broadcast_to(table[:, None, :], (EXPERTS, MAIN, ROWS))
    return spread.reshape(SLOTS, ROWS)


def ranks(routes):
    experts = iota((EXPERTS, ROWS), 0)
    member = jnp.zeros((EXPERTS, ROWS), F32)
    for k in range(TOP):
        member = member + jnp.where(routes[k : k + 1, :] == experts, 1.0, 0.0)
    earlier = jnp.where(iota((ROWS, ROWS), 0) < iota((ROWS, ROWS), 1), 1.0, 0.0)
    rank = dot(member.astype(BF16), earlier.astype(BF16))
    return jnp.where(member > 0.0, rank, -1.0)


def pair_gates(routes, gates):
    experts = iota((EXPERTS, ROWS), 0)
    total = jnp.zeros((EXPERTS, ROWS), F32)
    for k in range(TOP):
        total = total + jnp.where(routes[k : k + 1, :] == experts, gates[k : k + 1, :], 0.0)
    return total


def choosers(routes):
    rank = expanded(ranks(routes))
    place = iota((SLOTS, ROWS), 0) % MAIN
    main = rank == place.astype(F32)
    extra = rank == (MAIN + place % EXTRA).astype(F32)
    quarters = [extra & (place // EXTRA == j) for j in range(MAIN // EXTRA)]
    return main, quarters


def one_hot(chosen):
    return jnp.where(chosen, 1.0, 0.0).astype(BF16)


def unpacker():
    row = iota((SLOTS, SLOTS), 0)
    wanted = (row % SPARE) // EXTRA * MAIN + row // SPARE * EXTRA + row % EXTRA
    return one_hot(iota((SLOTS, SLOTS), 1) == wanted)


def packer():
    row = iota((SLOTS, SLOTS), 0)
    wanted = (row % MAIN) // EXTRA * SPARE + row // MAIN * EXTRA + row % EXTRA
    return one_hot(iota((SLOTS, SLOTS), 1) == wanted)


def dispatch_kernel(routes_hbm, tokens_hbm, out_hbm, routes_ref, tokens_ref, out_ref, sems, out_sems):
    routes_copy = pltpu.make_async_copy(routes_hbm, routes_ref, sems.at[0])
    tokens_copy = pltpu.make_async_copy(tokens_hbm, tokens_ref, sems.at[1])
    routes_copy.start()
    tokens_copy.start()
    routes_copy.wait()
    main, quarters = choosers(routes_ref[...])
    main = one_hot(main)
    quarter = WIDTH // 4
    total = jnp.zeros((SLOTS, quarter), F32)
    tokens_copy.wait()
    outgoing = []
    for j in range(5):
        cols = slice(j * quarter, (j + 1) * quarter)
        if j < 4:
            out_ref[:, cols] = dot(main, tokens_ref[:, cols]).astype(BF16)
            total = total + dot(one_hot(quarters[j]), tokens_ref[:, cols])
        else:
            out_ref[:, cols] = total.astype(BF16)
        part = pl.ds(j * quarter, quarter)
        copy = pltpu.make_async_copy(out_ref.at[:, part], out_hbm.at[:, part], out_sems.at[j])
        copy.start()
        outgoing.append(copy)
    for copy in outgoing:
        copy.wait()


def prepare_kernel(down_hbm, head_hbm, tokens_hbm, mixed_ref, base_ref, down_ref, head_ref, tokens_ref, sems):
    copies = [
        pltpu.make_async_copy(source, target, sems.at[i])
        for i, (source, target) in enumerate(
            ((head_hbm, head_ref), (tokens_hbm, tokens_ref), (down_hbm, down_ref))
        )
    ]
    for copy in copies:
        copy.start()
    copies[0].wait()
    copies[1].wait()
    base_ref[...] = dot(tokens_ref[...], head_ref[...])
    copies[2].wait()
    mixed_ref[...] = dot(down_ref[...], head_ref[...]).astype(BF16)


def forward_kernel(
    recv_ref, w_hbm, mixed_hbm, out_hbm, hidden_hbm, slopes_hbm,
    x_ref, act_ref, w_ref, mixed_ref, hidden_ref, slopes_ref, out_ref, sems, out_sems,
):
    quarter = WIDTH // 4

    def bring(source, target, index):
        copy = pltpu.make_async_copy(source, target, sems.at[index])
        copy.start()
        return copy

    groups = ((0, 1), (1, 3), (3, len(CHUNKS)))
    weight_copies = []
    for g, (begin, end) in enumerate(groups):
        lo, hi = CHUNKS[begin][0], CHUNKS[end - 1][1]
        for h in range(2):
            cols = pl.ds(h * HIDDEN + lo, hi - lo)
            weight_copies.append(bring(w_hbm.at[:, cols], w_ref.at[:, cols], 1 + 2 * g + h))
    mixed_copy = bring(mixed_hbm, mixed_ref, 0)
    x_ref[:SLOTS, :] = recv_ref[:, :WIDTH]
    spread = dot(unpacker(), recv_ref[:, WIDTH:]).astype(BF16)
    for j in range(4):
        x_ref[SLOTS:, j * quarter : (j + 1) * quarter] = spread[j * SPARE : (j + 1) * SPARE]
    outgoing = []

    def send(source, target, lo, wide):
        cols = pl.ds(lo, wide)
        copy = pltpu.make_async_copy(source.at[:, cols], target.at[:, cols], out_sems.at[len(outgoing)])
        copy.start()
        outgoing.append(copy)

    for g, (begin, end) in enumerate(groups):
        weight_copies[2 * g].wait()
        weight_copies[2 * g + 1].wait()
        for c in range(begin, end):
            lo, hi = CHUNKS[c]
            slot = c % 2
            wide = hi - lo
            act_ref[slot, 0, :, :wide] = dot(x_ref[...], w_ref[:, lo:hi])
            act_ref[slot, 1, :, :wide] = dot(x_ref[...], w_ref[:, HIDDEN + lo : HIDDEN + hi])
            for m in range(0, TOTAL, 64):
                rows = slice(m, m + 64)
                gate = act_ref[slot, 0, rows, :wide]
                up = act_ref[slot, 1, rows, :wide]
                sigmoid = 0.5 + 0.5 * jnp.tanh(0.5 * gate)
                silu = gate * sigmoid
                hidden_ref[rows, lo:hi] = (silu * up).astype(BF16)
                slopes_ref[rows, HIDDEN + lo : HIDDEN + hi] = silu.astype(BF16)
                slopes_ref[rows, lo:hi] = (up * sigmoid * (1.0 + gate * (1.0 - sigmoid))).astype(BF16)
        lo, hi = CHUNKS[begin][0], CHUNKS[end - 1][1]
        send(hidden_ref, hidden_hbm, lo, hi - lo)
        send(slopes_ref, slopes_hbm, lo, hi - lo)
        send(slopes_ref, slopes_hbm, HIDDEN + lo, hi - lo)
    mixed_copy.wait()
    projected = dot(hidden_ref[...], mixed_ref[...]).astype(BF16)
    out_ref[:, :EMBED] = projected[:SLOTS]
    quarter = EMBED // 4
    stacked = jnp.concatenate(
        [projected[SLOTS:, j * quarter : (j + 1) * quarter] for j in range(4)], axis=0
    )
    out_ref[:, EMBED:] = dot(packer(), stacked).astype(BF16)
    send(out_ref, out_hbm, 0, EMBED + quarter)
    for copy in outgoing:
        copy.wait()


def fetch_kernel(_, down_hbm, hidden_hbm, down_ref, hidden_ref, sems):
    copies = (
        pltpu.make_async_copy(hidden_hbm, hidden_ref, sems.at[0]),
        pltpu.make_async_copy(down_hbm, down_ref, sems.at[1]),
    )
    for copy in copies:
        copy.start()
    for copy in copies:
        copy.wait()


def weighted(chosen, gates):
    return jnp.where(chosen, gates, 0.0)


def split_product(chosen, gates, values):
    whole = weighted(chosen, gates)
    high = whole.astype(BF16)
    low = (whole - high.astype(F32)).astype(BF16)
    return dot_rows(high, values) + dot_rows(low, values)


def embed_kernel(routes_ref, gates_ref, answer_ref, base_ref, embedding_ref, unit_ref):
    main, quarters = choosers(routes_ref[...])
    gates = expanded(pair_gates(routes_ref[...], gates_ref[...]))
    mixture = split_product(main, gates, answer_ref[:, :EMBED])
    extra = jnp.concatenate(
        [split_product(quarters[j], gates, answer_ref[:, EMBED:]) for j in range(4)], axis=1
    )
    embedding = base_ref[...] + mixture + extra
    inverse = lax.rsqrt(jnp.mean(embedding * embedding, axis=1, keepdims=True) + EPSILON)
    embedding_ref[...] = embedding
    unit_ref[...] = (embedding * inverse).astype(BF16)


def loss_kernel(
    routes_ref, gates_ref, matches_ref, partner_ref, embedding_ref, unit_ref, key_ref, _,
    loss_ref, grad_ref, out_ref,
):
    embedding = embedding_ref[...]
    unit = unit_ref[...]
    keys = key_ref[...]
    coefficient = 1.0 / (EMBED * TEMPER)
    inverse = lax.rsqrt(jnp.mean(embedding * embedding, axis=1, keepdims=True) + EPSILON)
    unit_rows = embedding * inverse
    entry = iota((ROWS, ROWS), 0)

    def scores(rows, columns, matches):
        logits = dot_cols(rows, columns) * coefficient
        totals = jnp.log(jnp.sum(jnp.exp(logits), axis=0, keepdims=True))
        target = matches == entry
        chosen = jnp.sum(jnp.where(target, logits, 0.0), axis=0, keepdims=True)
        weights = jnp.exp(logits - totals) - jnp.where(target, 1.0, 0.0)
        return totals - chosen, weights.astype(BF16)

    loss, own = scores(keys, unit, matches_ref[...])
    loss_ref[...] = loss
    partner = scores(unit, keys, partner_ref[...].astype(jnp.int32))[1]
    upstream = (dot_rows(own, keys) + dot(partner, keys)) * coefficient
    grad = inverse * (upstream - unit_rows * jnp.mean(upstream * unit_rows, axis=1, keepdims=True))
    grad = grad.astype(BF16)
    grad_ref[...] = grad
    main, quarters = choosers(routes_ref[...])
    gates = expanded(pair_gates(routes_ref[...], gates_ref[...]))
    slot_gates = jnp.sum(weighted(main, gates), axis=1, keepdims=True)
    out_ref[:, :EMBED] = (slot_gates * dot(one_hot(main), grad)).astype(BF16)
    quarter = EMBED // 4
    total = jnp.zeros((SLOTS, quarter), F32)
    extra_gates = jnp.zeros((SLOTS, 1), F32)
    for j in range(4):
        total = total + dot(one_hot(quarters[j]), grad[:, j * quarter : (j + 1) * quarter])
        extra_gates = extra_gates + jnp.sum(weighted(quarters[j], gates), axis=1, keepdims=True)
    out_ref[:, EMBED:] = (extra_gates * total).astype(BF16)


def head_kernel(
    arrived_ref, tokens_ref, embed_grad_ref, hidden_ref, down_ref, grads_ref, own_ref, other_ref
):
    quarter = EMBED // 4
    grads_ref[:SLOTS, :] = arrived_ref[:, :EMBED]
    spread = dot(unpacker(), arrived_ref[:, EMBED:]).astype(BF16)
    for j in range(4):
        grads_ref[SLOTS:, j * quarter : (j + 1) * quarter] = spread[j * SPARE : (j + 1) * SPARE]
    first = lax.axis_index("expert_2") == 0
    inner = dot_rows(hidden_ref[...], grads_ref[...]).astype(BF16)
    for n in range(0, WIDTH, TILE):
        part = dot_rows(down_ref[:, n : n + TILE], inner)
        part = part + dot_rows(tokens_ref[:, n : n + TILE], embed_grad_ref[...])
        for b in range(TILE // 32):
            row = n // 2 + 16 * b
            even, odd = part[32 * b : 32 * b + 16], part[32 * b + 16 : 32 * b + 32]
            own_ref[row : row + 16, :] = jnp.where(first, even, odd)
            other_ref[row : row + 16, :] = jnp.where(first, odd, even).astype(BF16)


def joined_kernel(grads_ref, mixed_ref, slopes_ref, joined_ref, act_ref):
    for c, (lo, hi) in enumerate(CHUNKS):
        slot = c % 2
        wide = hi - lo
        act_ref[slot, :, :wide] = dot_cols(grads_ref[...], mixed_ref[lo:hi, :])
        for m in range(0, TOTAL, 64):
            hidden_grad = act_ref[slot, m : m + 64, :wide]
            for offset in (0, HIDDEN):
                slope = slopes_ref[m : m + 64, offset + lo : offset + hi].astype(F32)
                joined_ref[m : m + 64, offset + lo : offset + hi] = (hidden_grad * slope).astype(BF16)


def input_kernel(joined_ref, w_ref, _, out_hbm, extra_ref, out_ref, out_sems):
    step = WIDTH // 4
    outgoing = []

    def send(start, wide, index):
        cols = pl.ds(start, wide)
        copy = pltpu.make_async_copy(out_ref.at[:, cols], out_hbm.at[:, cols], out_sems.at[index])
        copy.start()
        outgoing.append(copy)

    for n in range(0, WIDTH, TILE):
        result = dot_cols(joined_ref[...], w_ref[n : n + TILE, :]).astype(BF16)
        out_ref[:, n : n + TILE] = result[:SLOTS]
        j, within = n // step, n % step
        extra_ref[j * SPARE : (j + 1) * SPARE, within : within + TILE] = result[SLOTS:]
        if n == WIDTH // 2 - TILE:
            send(0, WIDTH // 2, 0)
    out_ref[:, WIDTH:] = dot(packer(), extra_ref[...]).astype(BF16)
    send(WIDTH // 2, WIDTH // 2 + step, 1)
    for copy in outgoing:
        copy.wait()


def share_kernel(axis, count, own_hbm, *refs):
    received_hbm, outs = refs[:count], refs[count : count + 4]
    own_ref, received_ref, total_ref, sent_ref, sems, out_sems = refs[count + 4 :]
    copies = [pltpu.make_async_copy(own_hbm, own_ref, sems.at[count])]
    for k in range(count):
        copies.append(pltpu.make_async_copy(received_hbm[k], received_ref.at[k], sems.at[k]))
    for copy in copies:
        copy.start()
    for copy in copies:
        copy.wait()
    place = lax.axis_index(axis)
    outgoing = []
    for k in (2, 1, 3, 0):
        quarter = jnp.bitwise_xor(place, k)
        total = own_ref[quarter]
        for i in range(count):
            total = total + received_ref[i, quarter].astype(F32)
        if k:
            sent_ref[k - 1] = total.astype(BF16)
            copy = pltpu.make_async_copy(sent_ref.at[k - 1], outs[k], out_sems.at[k])
        else:
            total_ref[...] = total
            copy = pltpu.make_async_copy(total_ref, outs[0], out_sems.at[0])
        copy.start()
        outgoing.append(copy)
    for copy in outgoing:
        copy.wait()


def combine_kernel(routes_ref, direct_ref, back_hbm, out_ref, back_ref, sems):
    quarter = WIDTH // 4
    copies = []
    for n, j in enumerate((4, 0, 1, 2, 3)):
        cols = pl.ds(j * quarter, quarter)
        copy = pltpu.make_async_copy(back_hbm.at[:, cols], back_ref.at[:, cols], sems.at[n])
        copy.start()
        copies.append(copy)
    main, quarters = choosers(routes_ref[...])
    main = one_hot(main).T
    quarters = [one_hot(chosen).T for chosen in quarters]
    copies[0].wait()
    for j in range(4):
        cols = slice(j * quarter, (j + 1) * quarter)
        extra = dot(quarters[j], back_ref[:, WIDTH:])
        copies[j + 1].wait()
        total = dot(main, back_ref[:, cols]) + extra
        out_ref[:, cols] = (direct_ref[:, cols] + total).astype(BF16)


def call(kernel, outs, ins, scratch=(), flops=0, moved=0, limit=24):
    def spec(space):
        return pl.BlockSpec(memory_space=space)

    return pl.pallas_call(
        kernel,
        out_shape=tuple(jax.ShapeDtypeStruct(shape, dtype) for shape, dtype, _ in outs),
        in_specs=[spec(space) for _, space in ins],
        out_specs=tuple(spec(space) for _, _, space in outs),
        scratch_shapes=scratch,
        compiler_params=pltpu.CompilerParams(vmem_limit_bytes=int(limit * 1048576)),
        cost_estimate=pl.CostEstimate(flops=flops, bytes_accessed=moved, transcendentals=0),
    )(*[value for value, _ in ins])


def exchanged(value, axes, parts):
    rows, width = value.shape
    blocks = value.reshape(parts, rows // parts, width)
    return lax.all_to_all(blocks, axes, 0, 0, tiled=True).reshape(rows, width)


def body(tokens, routes, gates, gate_up, down_proj, projection, matches):
    vmem, hbm = pltpu.VMEM, pl.ANY
    routes, gates = routes.T, gates.T
    weights_joined, weights_down = gate_up[0], down_proj[0]
    partner = [(i, i ^ EXPERTS // 2) for i in range(EXPERTS)]
    dma = pltpu.SemaphoreType.DMA
    wide_shape, packed_shape = (SLOTS, WIDTH * 5 // 4), (SLOTS, EMBED * 5 // 4)

    (dispatch,) = call(
        dispatch_kernel, [(wide_shape, BF16, hbm)], [(routes, hbm), (tokens, hbm)],
        scratch=[
            pltpu.VMEM((TOP, ROWS), jnp.int32),
            pltpu.VMEM((ROWS, WIDTH), BF16),
            pltpu.VMEM(wide_shape, BF16),
            dma((2,)),
            dma((5,)),
        ],
        flops=2 * SLOTS * ROWS * WIDTH * 2, moved=3 << 20, limit=WHOLE,
    )
    partner_matches = lax.ppermute(matches.astype(BF16), EXPERT, partner)
    received = exchanged(dispatch, EXPERT, EXPERTS)
    mixed, base = call(
        prepare_kernel,
        [((HIDDEN, EMBED), BF16, vmem), ((ROWS, EMBED), F32, vmem)],
        [(weights_down, hbm), (projection, hbm), (tokens, hbm)],
        scratch=[
            pltpu.VMEM((HIDDEN, WIDTH), BF16),
            pltpu.VMEM((WIDTH, EMBED), BF16),
            pltpu.VMEM((ROWS, WIDTH), BF16),
            dma((3,)),
        ],
        flops=2 * (HIDDEN + ROWS) * WIDTH * EMBED, moved=8 << 20, limit=WHOLE,
    )
    received, partner_matches, base = lax.optimization_barrier((received, partner_matches, base))

    packed, hidden, slopes = call(
        forward_kernel,
        [(packed_shape, BF16, hbm), ((TOTAL, HIDDEN), BF16, hbm), ((TOTAL, 2 * HIDDEN), BF16, hbm)],
        [(received, vmem), (weights_joined, hbm), (mixed, hbm)],
        scratch=[
            pltpu.VMEM((TOTAL, WIDTH), BF16),
            pltpu.VMEM((2, 2, TOTAL, 256), F32),
            pltpu.VMEM((WIDTH, 2 * HIDDEN), BF16),
            pltpu.VMEM((HIDDEN, EMBED), BF16),
            pltpu.VMEM((TOTAL, HIDDEN), BF16),
            pltpu.VMEM((TOTAL, 2 * HIDDEN), BF16),
            pltpu.VMEM(packed_shape, BF16),
            dma((7,)),
            dma((10,)),
        ],
        flops=2 * TOTAL * HIDDEN * (2 * WIDTH + EMBED), moved=22 << 20, limit=56.5,
    )
    answer = exchanged(packed, EXPERT, EXPERTS)
    embedding, unit = call(
        embed_kernel,
        [((ROWS, EMBED), F32, vmem), ((ROWS, EMBED), BF16, vmem)],
        [(routes, vmem), (gates, vmem), (answer, vmem), (base, vmem)],
        flops=4 * SLOTS * ROWS * EMBED * 2, moved=2 << 20,
    )
    keys = lax.ppermute(unit, EXPERT, partner)
    down_near, hidden_near = call(
        fetch_kernel,
        [(weights_down.shape, BF16, vmem), (hidden.shape, BF16, vmem)],
        [(unit, vmem), (weights_down, hbm), (hidden, hbm)],
        scratch=[dma((2,))],
        moved=16 << 20, limit=30,
    )
    row_loss, embed_grad, slot_grads = call(
        loss_kernel,
        [((1, ROWS), F32, vmem), ((ROWS, EMBED), BF16, vmem), (packed_shape, BF16, vmem)],
        [(routes, vmem), (gates, vmem), (matches, vmem), (partner_matches, vmem),
         (embedding, vmem), (unit, vmem), (keys, vmem), (hidden_near, hbm)],
        flops=2 * SLOTS * ROWS * EMBED * 2, moved=2 << 20, limit=16,
    )
    arrived = exchanged(slot_grads, EXPERT, EXPERTS)
    half_shape = (WIDTH // 2, EMBED)
    grads, own, other = call(
        head_kernel,
        [((TOTAL, EMBED), BF16, vmem), (half_shape, F32, vmem), (half_shape, BF16, vmem)],
        [(arrived, vmem), (tokens, vmem), (embed_grad, vmem), (hidden_near, vmem), (down_near, vmem)],
        flops=2 * HIDDEN * EMBED * (TOTAL + WIDTH), moved=12 << 20, limit=16,
    )
    arrivals = [lax.ppermute(other, "expert_2", [(0, 1), (1, 0)])]
    joined_shape = (TOTAL, 2 * HIDDEN)
    (joined_grad,) = call(
        joined_kernel,
        [(joined_shape, BF16, vmem)],
        [(grads, vmem), (mixed, vmem), (slopes, vmem)],
        scratch=[pltpu.VMEM((2, TOTAL, 256), F32)],
        flops=2 * TOTAL * HIDDEN * EMBED, moved=8 << 20, limit=16,
    )
    (input_grads,) = call(
        input_kernel,
        [(wide_shape, BF16, hbm)],
        [(joined_grad, vmem), (weights_joined, vmem), (arrivals[0], hbm)],
        scratch=[
            pltpu.VMEM((SLOTS, WIDTH // 4), BF16),
            pltpu.VMEM(wide_shape, BF16),
            dma((2,)),
        ],
        flops=4 * TOTAL * HIDDEN * WIDTH, moved=18 << 20, limit=34,
    )
    back = exchanged(input_grads, EXPERT, EXPERTS)
    direct = dot_cols(embed_grad, projection)
    rows = own.shape[0] // 4
    own, *sent = call(
        functools.partial(share_kernel, "dp", 1),
        [((rows, EMBED), F32, hbm)] + [((rows, EMBED), BF16, hbm)] * 3,
        [(value.reshape(4, rows, EMBED), hbm) for value in (own, *arrivals)],
        scratch=[
            pltpu.VMEM((4, rows, EMBED), F32),
            pltpu.VMEM((1, 4, rows, EMBED), BF16),
            pltpu.VMEM((rows, EMBED), F32),
            pltpu.VMEM((3, rows, EMBED), BF16),
            dma((2,)),
            dma((4,)),
        ],
        limit=16,
    )
    for k, value in enumerate(sent):
        arrived = lax.ppermute(value, "dp", [(i, i ^ (k + 1)) for i in range(4)])
        own = own + arrived.astype(F32)
    back, sums = lax.optimization_barrier((back, own.astype(BF16)))
    parts = lax.all_to_all(
        sums.reshape(16, 16, EMBED), ("expert_0", "expert_1"), 0, 0, tiled=True
    )
    (grad_tokens,) = call(
        combine_kernel, [((ROWS, WIDTH), BF16, vmem)], [(routes, vmem), (direct, vmem), (back, hbm)],
        scratch=[pltpu.VMEM(wide_shape, BF16), dma((5,))],
        flops=2 * SLOTS * ROWS * WIDTH * 2, moved=4 << 20, limit=WHOLE,
    )
    device_count = lax.axis_size("dp") * EXPERTS
    grad_projection = jnp.sum(parts.astype(F32), axis=0) * (1.0 / math.sqrt(ROWS * device_count))
    return grad_tokens, grad_projection, row_loss.reshape(ROWS)


def solution(mesh):
    torus = Mesh(
        mesh.devices.reshape(mesh.shape["dp"], 4, 4, 2), ("dp", "expert_0", "expert_1", "expert_2")
    )
    return jax.shard_map(
        body,
        mesh=torus,
        in_specs=(
            P(DP_EXPERT, None),
            P(DP_EXPERT, None),
            P(DP_EXPERT, None),
            P(EXPERT, None, None),
            P(EXPERT, None, None),
            P(),
            P(DP_EXPERT, None),
        ),
        out_specs=(P(DP_EXPERT, None), P(DP_EXPERT, None), P(DP_EXPERT)),
        check_vma=False,
    )
```

```python
import functools
import math

import jax
import jax.numpy as jnp
from jax import lax
from jax.experimental import pallas as pl
from jax.experimental.pallas import tpu as pltpu
from jax.sharding import Mesh
from jax.sharding import PartitionSpec as P

EXPERT = ("expert_0", "expert_1", "expert_2")
DP_EXPERT = ("dp", "expert_0", "expert_1", "expert_2")

TEMPER = 0.1
EPSILON = 1e-06
ROWS = 128
TOP = 4
WIDTH = 2048
HIDDEN = 1408
EMBED = 512
EXPERTS = 32
MAIN = 16
EXTRA = 4
SLOTS = EXPERTS * MAIN
SPARE = EXPERTS * EXTRA
TOTAL = SLOTS + SPARE
CHUNKS = tuple((lo, min(lo + 256, HIDDEN)) for lo in range(0, HIDDEN, 256))
TILE = 256
F32 = jnp.float32
BF16 = jnp.bfloat16
WHOLE = 60


def dot(left, right):
    return jnp.dot(left, right, preferred_element_type=F32)


def dot_rows(left, right):
    return lax.dot_general(left, right, (((0,), (0,)), ((), ())), preferred_element_type=F32)


def dot_cols(left, right):
    return lax.dot_general(left, right, (((1,), (1,)), ((), ())), preferred_element_type=F32)


def iota(shape, dim):
    return lax.broadcasted_iota(jnp.int32, shape, dim)


def expanded(table):
    spread = jnp.broadcast_to(table[:, None, :], (EXPERTS, MAIN, ROWS))
    return spread.reshape(SLOTS, ROWS)


def ranks(routes):
    experts = iota((EXPERTS, ROWS), 0)
    member = jnp.zeros((EXPERTS, ROWS), F32)
    for k in range(TOP):
        member = member + jnp.where(routes[k : k + 1, :] == experts, 1.0, 0.0)
    earlier = jnp.where(iota((ROWS, ROWS), 0) < iota((ROWS, ROWS), 1), 1.0, 0.0)
    rank = dot(member.astype(BF16), earlier.astype(BF16))
    return jnp.where(member > 0.0, rank, -1.0)


def pair_gates(routes, gates):
    experts = iota((EXPERTS, ROWS), 0)
    total = jnp.zeros((EXPERTS, ROWS), F32)
    for k in range(TOP):
        total = total + jnp.where(routes[k : k + 1, :] == experts, gates[k : k + 1, :], 0.0)
    return total


def choosers(routes):
    rank = expanded(ranks(routes))
    place = iota((SLOTS, ROWS), 0) % MAIN
    main = rank == place.astype(F32)
    extra = rank == (MAIN + place % EXTRA).astype(F32)
    quarters = [extra & (place // EXTRA == j) for j in range(MAIN // EXTRA)]
    return main, quarters


def one_hot(chosen):
    return jnp.where(chosen, 1.0, 0.0).astype(BF16)


def unpacker():
    row = iota((SLOTS, SLOTS), 0)
    wanted = (row % SPARE) // EXTRA * MAIN + row // SPARE * EXTRA + row % EXTRA
    return one_hot(iota((SLOTS, SLOTS), 1) == wanted)


def packer():
    row = iota((SLOTS, SLOTS), 0)
    wanted = (row % MAIN) // EXTRA * SPARE + row // MAIN * EXTRA + row % EXTRA
    return one_hot(iota((SLOTS, SLOTS), 1) == wanted)


def dispatch_kernel(routes_hbm, tokens_hbm, out_hbm, routes_ref, tokens_ref, out_ref, sems, out_sems):
    routes_copy = pltpu.make_async_copy(routes_hbm, routes_ref, sems.at[0])
    tokens_copy = pltpu.make_async_copy(tokens_hbm, tokens_ref, sems.at[1])
    routes_copy.start()
    tokens_copy.start()
    routes_copy.wait()
    main, quarters = choosers(routes_ref[...])
    main = one_hot(main)
    quarter = WIDTH // 4
    total = jnp.zeros((SLOTS, quarter), F32)
    tokens_copy.wait()
    outgoing = []
    for j in range(5):
        cols = slice(j * quarter, (j + 1) * quarter)
        if j < 4:
            out_ref[:, cols] = dot(main, tokens_ref[:, cols]).astype(BF16)
            total = total + dot(one_hot(quarters[j]), tokens_ref[:, cols])
        else:
            out_ref[:, cols] = total.astype(BF16)
        part = pl.ds(j * quarter, quarter)
        copy = pltpu.make_async_copy(out_ref.at[:, part], out_hbm.at[:, part], out_sems.at[j])
        copy.start()
        outgoing.append(copy)
    for copy in outgoing:
        copy.wait()


def prepare_kernel(down_hbm, head_hbm, tokens_hbm, mixed_ref, base_ref, down_ref, head_ref, tokens_ref, sems):
    copies = [
        pltpu.make_async_copy(source, target, sems.at[i])
        for i, (source, target) in enumerate(
            ((head_hbm, head_ref), (tokens_hbm, tokens_ref), (down_hbm, down_ref))
        )
    ]
    for copy in copies:
        copy.start()
    copies[0].wait()
    copies[1].wait()
    base_ref[...] = dot(tokens_ref[...], head_ref[...])
    copies[2].wait()
    mixed_ref[...] = dot(down_ref[...], head_ref[...]).astype(BF16)


def forward_kernel(
    recv_hbm, w_hbm, mixed_hbm, out_hbm, hidden_hbm, slopes_hbm,
    x_ref, extra_ref, act_ref, w_ref, mixed_ref, hidden_ref, slopes_ref, out_ref, sems, out_sems,
):
    quarter = WIDTH // 4

    def bring(source, target, index):
        copy = pltpu.make_async_copy(source, target, sems.at[index])
        copy.start()
        return copy

    extra_copy = bring(recv_hbm.at[:, pl.ds(WIDTH, quarter)], extra_ref, 7)
    main_copy = bring(recv_hbm.at[:, pl.ds(0, WIDTH)], x_ref.at[pl.ds(0, SLOTS), :], 8)
    groups = ((0, 1), (1, 3), (3, len(CHUNKS)))
    weight_copies = []
    for g, (begin, end) in enumerate(groups):
        lo, hi = CHUNKS[begin][0], CHUNKS[end - 1][1]
        for h in range(2):
            cols = pl.ds(h * HIDDEN + lo, hi - lo)
            weight_copies.append(bring(w_hbm.at[:, cols], w_ref.at[:, cols], 1 + 2 * g + h))
    mixed_copy = bring(mixed_hbm, mixed_ref, 0)
    turned = unpacker()
    extra_copy.wait()
    spread = dot(turned, extra_ref[...]).astype(BF16)
    for j in range(4):
        x_ref[SLOTS:, j * quarter : (j + 1) * quarter] = spread[j * SPARE : (j + 1) * SPARE]
    main_copy.wait()
    outgoing = []

    def send(source, target, lo, wide):
        cols = pl.ds(lo, wide)
        copy = pltpu.make_async_copy(source.at[:, cols], target.at[:, cols], out_sems.at[len(outgoing)])
        copy.start()
        outgoing.append(copy)

    for g, (begin, end) in enumerate(groups):
        weight_copies[2 * g].wait()
        weight_copies[2 * g + 1].wait()
        for c in range(begin, end):
            lo, hi = CHUNKS[c]
            slot = c % 2
            wide = hi - lo
            act_ref[slot, 0, :, :wide] = dot(x_ref[...], w_ref[:, lo:hi])
            act_ref[slot, 1, :, :wide] = dot(x_ref[...], w_ref[:, HIDDEN + lo : HIDDEN + hi])
            for m in range(0, TOTAL, 64):
                rows = slice(m, m + 64)
                gate = act_ref[slot, 0, rows, :wide]
                up = act_ref[slot, 1, rows, :wide]
                sigmoid = 0.5 + 0.5 * jnp.tanh(0.5 * gate)
                silu = gate * sigmoid
                hidden_ref[rows, lo:hi] = (silu * up).astype(BF16)
                slopes_ref[rows, HIDDEN + lo : HIDDEN + hi] = silu.astype(BF16)
                slopes_ref[rows, lo:hi] = (up * sigmoid * (1.0 + gate * (1.0 - sigmoid))).astype(BF16)
        lo, hi = CHUNKS[begin][0], CHUNKS[end - 1][1]
        send(hidden_ref, hidden_hbm, lo, hi - lo)
        send(slopes_ref, slopes_hbm, lo, hi - lo)
        send(slopes_ref, slopes_hbm, HIDDEN + lo, hi - lo)
    mixed_copy.wait()
    projected = dot(hidden_ref[...], mixed_ref[...]).astype(BF16)
    out_ref[:, :EMBED] = projected[:SLOTS]
    quarter = EMBED // 4
    stacked = jnp.concatenate(
        [projected[SLOTS:, j * quarter : (j + 1) * quarter] for j in range(4)], axis=0
    )
    out_ref[:, EMBED:] = dot(packer(), stacked).astype(BF16)
    send(out_ref, out_hbm, 0, EMBED + quarter)
    for copy in outgoing:
        copy.wait()


def fetch_kernel(_, down_hbm, hidden_hbm, down_ref, hidden_ref, sems):
    copies = (
        pltpu.make_async_copy(hidden_hbm, hidden_ref, sems.at[0]),
        pltpu.make_async_copy(down_hbm, down_ref, sems.at[1]),
    )
    for copy in copies:
        copy.start()
    for copy in copies:
        copy.wait()


def weighted(chosen, gates):
    return jnp.where(chosen, gates, 0.0)


def split_product(chosen, gates, values):
    whole = weighted(chosen, gates)
    high = whole.astype(BF16)
    low = (whole - high.astype(F32)).astype(BF16)
    return dot_rows(high, values) + dot_rows(low, values)


def embed_kernel(routes_ref, gates_ref, answer_ref, base_ref, embedding_ref, unit_ref):
    main, quarters = choosers(routes_ref[...])
    gates = expanded(pair_gates(routes_ref[...], gates_ref[...]))
    mixture = split_product(main, gates, answer_ref[:, :EMBED])
    extra = jnp.concatenate(
        [split_product(quarters[j], gates, answer_ref[:, EMBED:]) for j in range(4)], axis=1
    )
    embedding = base_ref[...] + mixture + extra
    inverse = lax.rsqrt(jnp.mean(embedding * embedding, axis=1, keepdims=True) + EPSILON)
    embedding_ref[...] = embedding
    unit_ref[...] = (embedding * inverse).astype(BF16)


def loss_kernel(
    routes_ref, gates_ref, matches_ref, partner_ref, embedding_ref, unit_ref, key_ref, _,
    loss_ref, grad_ref, out_ref,
):
    embedding = embedding_ref[...]
    unit = unit_ref[...]
    keys = key_ref[...]
    coefficient = 1.0 / (EMBED * TEMPER)
    inverse = lax.rsqrt(jnp.mean(embedding * embedding, axis=1, keepdims=True) + EPSILON)
    unit_rows = embedding * inverse
    entry = iota((ROWS, ROWS), 0)

    def scores(rows, columns, matches):
        logits = dot_cols(rows, columns) * coefficient
        totals = jnp.log(jnp.sum(jnp.exp(logits), axis=0, keepdims=True))
        target = matches == entry
        chosen = jnp.sum(jnp.where(target, logits, 0.0), axis=0, keepdims=True)
        weights = jnp.exp(logits - totals) - jnp.where(target, 1.0, 0.0)
        return totals - chosen, weights.astype(BF16)

    loss, own = scores(keys, unit, matches_ref[...])
    loss_ref[...] = loss
    partner = scores(unit, keys, partner_ref[...].astype(jnp.int32))[1]
    upstream = (dot_rows(own, keys) + dot(partner, keys)) * coefficient
    grad = inverse * (upstream - unit_rows * jnp.mean(upstream * unit_rows, axis=1, keepdims=True))
    grad = grad.astype(BF16)
    grad_ref[...] = grad
    main, quarters = choosers(routes_ref[...])
    gates = expanded(pair_gates(routes_ref[...], gates_ref[...]))
    slot_gates = jnp.sum(weighted(main, gates), axis=1, keepdims=True)
    out_ref[:, :EMBED] = (slot_gates * dot(one_hot(main), grad)).astype(BF16)
    quarter = EMBED // 4
    total = jnp.zeros((SLOTS, quarter), F32)
    extra_gates = jnp.zeros((SLOTS, 1), F32)
    for j in range(4):
        total = total + dot(one_hot(quarters[j]), grad[:, j * quarter : (j + 1) * quarter])
        extra_gates = extra_gates + jnp.sum(weighted(quarters[j], gates), axis=1, keepdims=True)
    out_ref[:, EMBED:] = (extra_gates * total).astype(BF16)


def head_kernel(
    arrived_ref, tokens_ref, embed_grad_ref, hidden_ref, down_ref, grads_ref, own_ref, other_ref
):
    quarter = EMBED // 4
    grads_ref[:SLOTS, :] = arrived_ref[:, :EMBED]
    spread = dot(unpacker(), arrived_ref[:, EMBED:]).astype(BF16)
    for j in range(4):
        grads_ref[SLOTS:, j * quarter : (j + 1) * quarter] = spread[j * SPARE : (j + 1) * SPARE]
    first = lax.axis_index("expert_2") == 0
    inner = dot_rows(hidden_ref[...], grads_ref[...]).astype(BF16)
    for n in range(0, WIDTH, TILE):
        part = dot_rows(down_ref[:, n : n + TILE], inner)
        part = part + dot_rows(tokens_ref[:, n : n + TILE], embed_grad_ref[...])
        for b in range(TILE // 32):
            row = n // 2 + 16 * b
            even, odd = part[32 * b : 32 * b + 16], part[32 * b + 16 : 32 * b + 32]
            own_ref[row : row + 16, :] = jnp.where(first, even, odd)
            other_ref[row : row + 16, :] = jnp.where(first, odd, even).astype(BF16)


def joined_kernel(grads_ref, mixed_ref, slopes_ref, joined_ref, act_ref):
    for c, (lo, hi) in enumerate(CHUNKS):
        slot = c % 2
        wide = hi - lo
        act_ref[slot, :, :wide] = dot_cols(grads_ref[...], mixed_ref[lo:hi, :])
        for m in range(0, TOTAL, 64):
            hidden_grad = act_ref[slot, m : m + 64, :wide]
            for offset in (0, HIDDEN):
                slope = slopes_ref[m : m + 64, offset + lo : offset + hi].astype(F32)
                joined_ref[m : m + 64, offset + lo : offset + hi] = (hidden_grad * slope).astype(BF16)


def input_tiles(joined_ref, w_ref, begin, end, out_ref, extra_ref):
    step = WIDTH // 4
    for n in range(begin, end, TILE):
        result = dot_cols(joined_ref[...], w_ref[n : n + TILE, :]).astype(BF16)
        out_ref[:, n - begin : n - begin + TILE] = result[:SLOTS]
        j, within = (n - begin) // step, n % step
        extra_ref[j * SPARE : (j + 1) * SPARE, within : within + TILE] = result[SLOTS:]


def input_kernel(joined_ref, w_ref, out_ref, extra_ref):
    input_tiles(joined_ref, w_ref, 0, WIDTH * 3 // 4, out_ref, extra_ref)


def last_input_kernel(joined_ref, w_ref, first_ref, extra_ref, *refs):
    out_hbm, last_ref, stacked_ref, sems = refs[-4:]
    split = WIDTH * 3 // 4

    def send(source, begin, wide, index):
        copy = pltpu.make_async_copy(source, out_hbm.at[:, pl.ds(begin, wide)], sems.at[index])
        copy.start()
        return copy

    first = send(first_ref, 0, split, 0)
    step = WIDTH // 4
    stacked_ref[: 3 * SPARE, :] = extra_ref[...]
    input_tiles(
        joined_ref, w_ref, split, WIDTH, last_ref.at[:, pl.ds(0, step)],
        stacked_ref.at[pl.ds(3 * SPARE, SPARE), :],
    )
    last_ref[:, step:] = dot(packer(), stacked_ref[...]).astype(BF16)
    last = send(last_ref, split, 2 * step, 1)
    first.wait()
    last.wait()


def share_kernel(axis, count, own_hbm, *refs):
    received_hbm, outs = refs[:count], refs[count : count + 4]
    own_ref, received_ref, total_ref, sent_ref, sems, out_sems = refs[count + 4 :]
    copies = [pltpu.make_async_copy(own_hbm, own_ref, sems.at[count])]
    for k in range(count):
        copies.append(pltpu.make_async_copy(received_hbm[k], received_ref.at[k], sems.at[k]))
    for copy in copies:
        copy.start()
    for copy in copies:
        copy.wait()
    place = lax.axis_index(axis)
    outgoing = []
    for k in (2, 1, 3, 0):
        quarter = jnp.bitwise_xor(place, k)
        total = own_ref[quarter]
        for i in range(count):
            total = total + received_ref[i, quarter].astype(F32)
        if k:
            sent_ref[k - 1] = total.astype(BF16)
            copy = pltpu.make_async_copy(sent_ref.at[k - 1], outs[k], out_sems.at[k])
        else:
            total_ref[...] = total
            copy = pltpu.make_async_copy(total_ref, outs[0], out_sems.at[0])
        copy.start()
        outgoing.append(copy)
    for copy in outgoing:
        copy.wait()


def combine_kernel(routes_ref, direct_ref, back_hbm, out_ref, back_ref, sems):
    quarter = WIDTH // 4
    copies = []
    for n, j in enumerate((4, 0, 1, 2, 3)):
        cols = pl.ds(j * quarter, quarter)
        copy = pltpu.make_async_copy(back_hbm.at[:, cols], back_ref.at[:, cols], sems.at[n])
        copy.start()
        copies.append(copy)
    main, quarters = choosers(routes_ref[...])
    main = one_hot(main).T
    quarters = [one_hot(chosen).T for chosen in quarters]
    copies[0].wait()
    for j in range(4):
        cols = slice(j * quarter, (j + 1) * quarter)
        extra = dot(quarters[j], back_ref[:, WIDTH:])
        copies[j + 1].wait()
        total = dot(main, back_ref[:, cols]) + extra
        out_ref[:, cols] = (direct_ref[:, cols] + total).astype(BF16)


def call(kernel, outs, ins, scratch=(), flops=0, moved=0, limit=24):
    def spec(space):
        return pl.BlockSpec(memory_space=space)

    return pl.pallas_call(
        kernel,
        out_shape=tuple(jax.ShapeDtypeStruct(shape, dtype) for shape, dtype, _ in outs),
        in_specs=[spec(space) for _, space in ins],
        out_specs=tuple(spec(space) for _, _, space in outs),
        scratch_shapes=scratch,
        compiler_params=pltpu.CompilerParams(vmem_limit_bytes=int(limit * 1048576)),
        cost_estimate=pl.CostEstimate(flops=flops, bytes_accessed=moved, transcendentals=0),
    )(*[value for value, _ in ins])


def exchanged(value, axes, parts):
    rows, width = value.shape
    blocks = value.reshape(parts, rows // parts, width)
    return lax.all_to_all(blocks, axes, 0, 0, tiled=True).reshape(rows, width)


def body(tokens, routes, gates, gate_up, down_proj, projection, matches):
    vmem, hbm = pltpu.VMEM, pl.ANY
    routes, gates = routes.T, gates.T
    weights_joined, weights_down = gate_up[0], down_proj[0]
    partner = [(i, i ^ EXPERTS // 2) for i in range(EXPERTS)]
    dma = pltpu.SemaphoreType.DMA
    wide_shape, packed_shape = (SLOTS, WIDTH * 5 // 4), (SLOTS, EMBED * 5 // 4)

    (dispatch,) = call(
        dispatch_kernel, [(wide_shape, BF16, hbm)], [(routes, hbm), (tokens, hbm)],
        scratch=[
            pltpu.VMEM((TOP, ROWS), jnp.int32),
            pltpu.VMEM((ROWS, WIDTH), BF16),
            pltpu.VMEM(wide_shape, BF16),
            dma((2,)),
            dma((5,)),
        ],
        flops=2 * SLOTS * ROWS * WIDTH * 2, moved=3 << 20, limit=WHOLE,
    )
    partner_matches = lax.ppermute(matches.astype(BF16), EXPERT, partner)
    received = exchanged(dispatch, EXPERT, EXPERTS)
    mixed, base = call(
        prepare_kernel,
        [((HIDDEN, EMBED), BF16, vmem), ((ROWS, EMBED), F32, vmem)],
        [(weights_down, hbm), (projection, hbm), (tokens, hbm)],
        scratch=[
            pltpu.VMEM((HIDDEN, WIDTH), BF16),
            pltpu.VMEM((WIDTH, EMBED), BF16),
            pltpu.VMEM((ROWS, WIDTH), BF16),
            dma((3,)),
        ],
        flops=2 * (HIDDEN + ROWS) * WIDTH * EMBED, moved=8 << 20, limit=WHOLE,
    )
    received, partner_matches, base = lax.optimization_barrier((received, partner_matches, base))

    packed, hidden, slopes = call(
        forward_kernel,
        [(packed_shape, BF16, hbm), ((TOTAL, HIDDEN), BF16, hbm), ((TOTAL, 2 * HIDDEN), BF16, hbm)],
        [(received, hbm), (weights_joined, hbm), (mixed, hbm)],
        scratch=[
            pltpu.VMEM((TOTAL, WIDTH), BF16),
            pltpu.VMEM((SLOTS, WIDTH // 4), BF16),
            pltpu.VMEM((2, 2, TOTAL, 256), F32),
            pltpu.VMEM((WIDTH, 2 * HIDDEN), BF16),
            pltpu.VMEM((HIDDEN, EMBED), BF16),
            pltpu.VMEM((TOTAL, HIDDEN), BF16),
            pltpu.VMEM((TOTAL, 2 * HIDDEN), BF16),
            pltpu.VMEM(packed_shape, BF16),
            dma((9,)),
            dma((10,)),
        ],
        flops=2 * TOTAL * HIDDEN * (2 * WIDTH + EMBED), moved=22 << 20, limit=56.5,
    )
    answer = exchanged(packed, EXPERT, EXPERTS)
    embedding, unit = call(
        embed_kernel,
        [((ROWS, EMBED), F32, vmem), ((ROWS, EMBED), BF16, vmem)],
        [(routes, vmem), (gates, vmem), (answer, vmem), (base, vmem)],
        flops=4 * SLOTS * ROWS * EMBED * 2, moved=2 << 20,
    )
    keys = lax.ppermute(unit, EXPERT, partner)
    down_near, hidden_near = call(
        fetch_kernel,
        [(weights_down.shape, BF16, vmem), (hidden.shape, BF16, vmem)],
        [(unit, vmem), (weights_down, hbm), (hidden, hbm)],
        scratch=[dma((2,))],
        moved=16 << 20, limit=30,
    )
    row_loss, embed_grad, slot_grads = call(
        loss_kernel,
        [((1, ROWS), F32, vmem), ((ROWS, EMBED), BF16, vmem), (packed_shape, BF16, vmem)],
        [(routes, vmem), (gates, vmem), (matches, vmem), (partner_matches, vmem),
         (embedding, vmem), (unit, vmem), (keys, vmem), (hidden_near, hbm)],
        flops=2 * SLOTS * ROWS * EMBED * 2, moved=2 << 20, limit=16,
    )
    arrived = exchanged(slot_grads, EXPERT, EXPERTS)
    half_shape = (WIDTH // 2, EMBED)
    grads, own, other = call(
        head_kernel,
        [((TOTAL, EMBED), BF16, vmem), (half_shape, F32, vmem), (half_shape, BF16, vmem)],
        [(arrived, vmem), (tokens, vmem), (embed_grad, vmem), (hidden_near, vmem), (down_near, vmem)],
        flops=2 * HIDDEN * EMBED * (TOTAL + WIDTH), moved=12 << 20, limit=16,
    )
    arrivals = [lax.ppermute(other, "expert_2", [(0, 1), (1, 0)])]
    joined_shape = (TOTAL, 2 * HIDDEN)
    (joined_grad,) = call(
        joined_kernel,
        [(joined_shape, BF16, vmem)],
        [(grads, vmem), (mixed, vmem), (slopes, vmem)],
        scratch=[pltpu.VMEM((2, TOTAL, 256), F32)],
        flops=2 * TOTAL * HIDDEN * EMBED, moved=8 << 20, limit=16,
    )

    def shared(axis, own, arrivals):
        rows, count = own.shape[0] // 4, len(arrivals)
        own, *sent = call(
            functools.partial(share_kernel, axis, count),
            [((rows, EMBED), F32, hbm)] + [((rows, EMBED), BF16, hbm)] * 3,
            [(value.reshape(4, rows, EMBED), hbm) for value in (own, *arrivals)],
            scratch=[
                pltpu.VMEM((4, rows, EMBED), F32),
                pltpu.VMEM((count, 4, rows, EMBED), BF16),
                pltpu.VMEM((rows, EMBED), F32),
                pltpu.VMEM((3, rows, EMBED), BF16),
                dma((1 + count,)),
                dma((4,)),
            ],
            limit=16,
        )
        return own, [
            lax.ppermute(value, axis, [(i, i ^ (k + 1)) for i in range(4)])
            for k, value in enumerate(sent)
        ]

    own, arrivals = shared("dp", own, arrivals)
    split = WIDTH * 3 // 4
    first_grads, extra_grads = call(
        input_kernel,
        [((SLOTS, split), BF16, vmem), ((3 * SPARE, WIDTH // 4), BF16, vmem)],
        [(joined_grad, vmem), (weights_joined, vmem)],
        flops=3 * TOTAL * HIDDEN * WIDTH, moved=14 << 20, limit=34,
    )
    (input_grads,) = call(
        last_input_kernel,
        [(wide_shape, BF16, hbm)],
        [(joined_grad, vmem), (weights_joined, vmem), (first_grads, vmem), (extra_grads, vmem)]
        + [(value, hbm) for value in arrivals],
        scratch=[
            pltpu.VMEM((SLOTS, WIDTH // 2), BF16),
            pltpu.VMEM((SLOTS, WIDTH // 4), BF16),
            dma((2,)),
        ],
        flops=TOTAL * HIDDEN * WIDTH, moved=6 << 20, limit=34,
    )
    back = exchanged(input_grads, EXPERT, EXPERTS)
    direct = dot_cols(embed_grad, projection)
    for axis in ("expert_0", "expert_1"):
        own, arrivals = shared(axis, own, arrivals)
    for value in arrivals:
        own = own + value.astype(F32)
    device_count = lax.axis_size("dp") * EXPERTS
    grad_projection = own * (1.0 / math.sqrt(ROWS * device_count))
    (grad_tokens,) = call(
        combine_kernel, [((ROWS, WIDTH), BF16, vmem)], [(routes, vmem), (direct, vmem), (back, hbm)],
        scratch=[pltpu.VMEM(wide_shape, BF16), dma((5,))],
        flops=2 * SLOTS * ROWS * WIDTH * 2, moved=4 << 20, limit=WHOLE,
    )
    return grad_tokens, grad_projection, row_loss.reshape(ROWS)


def solution(mesh):
    torus = Mesh(
        mesh.devices.reshape(mesh.shape["dp"], 4, 4, 2), ("dp", "expert_0", "expert_1", "expert_2")
    )
    return jax.shard_map(
        body,
        mesh=torus,
        in_specs=(
            P(DP_EXPERT, None),
            P(DP_EXPERT, None),
            P(DP_EXPERT, None),
            P(EXPERT, None, None),
            P(EXPERT, None, None),
            P(),
            P(DP_EXPERT, None),
        ),
        out_specs=(P(DP_EXPERT, None), P(DP_EXPERT, None), P(DP_EXPERT)),
        check_vma=False,
    )
```

```python
import math

import jax
import jax.numpy as jnp
from jax import lax
from jax.experimental import pallas as pl
from jax.experimental.pallas import tpu as pltpu
from jax.sharding import Mesh
from jax.sharding import PartitionSpec as P

EXPERT = ("expert_0", "expert_1", "expert_2")
DP_EXPERT = ("dp", "expert_0", "expert_1", "expert_2")

TEMPER = 0.1
EPSILON = 1e-06
ROWS = 128
TOP = 4
WIDTH = 2048
HIDDEN = 1408
EMBED = 512
EXPERTS = 32
MAIN = 16
EXTRA = 4
SLOTS = EXPERTS * MAIN
SPARE = EXPERTS * EXTRA
TOTAL = SLOTS + SPARE
CHUNKS = tuple((lo, min(lo + 256, HIDDEN)) for lo in range(0, HIDDEN, 256))
TILE = 256
F32 = jnp.float32
BF16 = jnp.bfloat16
WHOLE = 60


def dot(left, right):
    return jnp.dot(left, right, preferred_element_type=F32)


def dot_rows(left, right):
    return lax.dot_general(left, right, (((0,), (0,)), ((), ())), preferred_element_type=F32)


def dot_cols(left, right):
    return lax.dot_general(left, right, (((1,), (1,)), ((), ())), preferred_element_type=F32)


def iota(shape, dim):
    return lax.broadcasted_iota(jnp.int32, shape, dim)


def expanded(table):
    spread = jnp.broadcast_to(table[:, None, :], (EXPERTS, MAIN, ROWS))
    return spread.reshape(SLOTS, ROWS)


def ranks(routes):
    experts = iota((EXPERTS, ROWS), 0)
    member = jnp.zeros((EXPERTS, ROWS), F32)
    for k in range(TOP):
        member = member + jnp.where(routes[k : k + 1, :] == experts, 1.0, 0.0)
    earlier = jnp.where(iota((ROWS, ROWS), 0) < iota((ROWS, ROWS), 1), 1.0, 0.0)
    rank = dot(member.astype(BF16), earlier.astype(BF16))
    return jnp.where(member > 0.0, rank, -1.0)


def pair_gates(routes, gates):
    experts = iota((EXPERTS, ROWS), 0)
    total = jnp.zeros((EXPERTS, ROWS), F32)
    for k in range(TOP):
        total = total + jnp.where(routes[k : k + 1, :] == experts, gates[k : k + 1, :], 0.0)
    return total


def choosers(routes):
    rank = expanded(ranks(routes))
    place = iota((SLOTS, ROWS), 0) % MAIN
    main = rank == place.astype(F32)
    extra = rank == (MAIN + place % EXTRA).astype(F32)
    quarters = [extra & (place // EXTRA == j) for j in range(MAIN // EXTRA)]
    return main, quarters


def one_hot(chosen):
    return jnp.where(chosen, 1.0, 0.0).astype(BF16)


def unpacker():
    row = iota((SLOTS, SLOTS), 0)
    wanted = (row % SPARE) // EXTRA * MAIN + row // SPARE * EXTRA + row % EXTRA
    return one_hot(iota((SLOTS, SLOTS), 1) == wanted)


def packer():
    row = iota((SLOTS, SLOTS), 0)
    wanted = (row % MAIN) // EXTRA * SPARE + row // MAIN * EXTRA + row % EXTRA
    return one_hot(iota((SLOTS, SLOTS), 1) == wanted)


def dispatch_kernel(routes_hbm, tokens_hbm, out_hbm, routes_ref, tokens_ref, out_ref, sems, out_sems):
    routes_copy = pltpu.make_async_copy(routes_hbm, routes_ref, sems.at[0])
    tokens_copy = pltpu.make_async_copy(tokens_hbm, tokens_ref, sems.at[1])
    routes_copy.start()
    tokens_copy.start()
    routes_copy.wait()
    main, quarters = choosers(routes_ref[...])
    main = one_hot(main)
    quarter = WIDTH // 4
    total = jnp.zeros((SLOTS, quarter), F32)
    tokens_copy.wait()
    outgoing = []
    for j in range(5):
        cols = slice(j * quarter, (j + 1) * quarter)
        if j < 4:
            out_ref[:, cols] = dot(main, tokens_ref[:, cols]).astype(BF16)
            total = total + dot(one_hot(quarters[j]), tokens_ref[:, cols])
        else:
            out_ref[:, cols] = total.astype(BF16)
        part = pl.ds(j * quarter, quarter)
        copy = pltpu.make_async_copy(out_ref.at[:, part], out_hbm.at[:, part], out_sems.at[j])
        copy.start()
        outgoing.append(copy)
    for copy in outgoing:
        copy.wait()


def prepare_kernel(down_hbm, head_hbm, tokens_hbm, mixed_ref, base_ref, down_ref, head_ref, tokens_ref, sems):
    copies = [
        pltpu.make_async_copy(source, target, sems.at[i])
        for i, (source, target) in enumerate(
            ((head_hbm, head_ref), (tokens_hbm, tokens_ref), (down_hbm, down_ref))
        )
    ]
    for copy in copies:
        copy.start()
    copies[0].wait()
    copies[1].wait()
    base_ref[...] = dot(tokens_ref[...], head_ref[...])
    copies[2].wait()
    mixed_ref[...] = dot(down_ref[...], head_ref[...]).astype(BF16)


def forward_kernel(
    recv_hbm, w_hbm, mixed_hbm, out_hbm, hidden_hbm, slopes_hbm,
    x_ref, extra_ref, act_ref, w_ref, mixed_ref, hidden_ref, slopes_ref, out_ref, sems, out_sems,
):
    quarter = WIDTH // 4

    def bring(source, target, index):
        copy = pltpu.make_async_copy(source, target, sems.at[index])
        copy.start()
        return copy

    extra_copy = bring(recv_hbm.at[:, pl.ds(WIDTH, quarter)], extra_ref, 7)
    main_copy = bring(recv_hbm.at[:, pl.ds(0, WIDTH)], x_ref.at[pl.ds(0, SLOTS), :], 8)
    groups = ((0, 1), (1, 3), (3, len(CHUNKS)))
    weight_copies = []
    for g, (begin, end) in enumerate(groups):
        lo, hi = CHUNKS[begin][0], CHUNKS[end - 1][1]
        for h in range(2):
            cols = pl.ds(h * HIDDEN + lo, hi - lo)
            weight_copies.append(bring(w_hbm.at[:, cols], w_ref.at[:, cols], 1 + 2 * g + h))
    mixed_copy = bring(mixed_hbm, mixed_ref, 0)
    turned = unpacker()
    extra_copy.wait()
    spread = dot(turned, extra_ref[...]).astype(BF16)
    for j in range(4):
        x_ref[SLOTS:, j * quarter : (j + 1) * quarter] = spread[j * SPARE : (j + 1) * SPARE]
    main_copy.wait()
    outgoing = []

    def send(source, target, lo, wide):
        cols = pl.ds(lo, wide)
        copy = pltpu.make_async_copy(source.at[:, cols], target.at[:, cols], out_sems.at[len(outgoing)])
        copy.start()
        outgoing.append(copy)

    for g, (begin, end) in enumerate(groups):
        weight_copies[2 * g].wait()
        weight_copies[2 * g + 1].wait()
        for c in range(begin, end):
            lo, hi = CHUNKS[c]
            slot = c % 2
            wide = hi - lo
            act_ref[slot, 0, :, :wide] = dot(x_ref[...], w_ref[:, lo:hi])
            act_ref[slot, 1, :, :wide] = dot(x_ref[...], w_ref[:, HIDDEN + lo : HIDDEN + hi])
            for m in range(0, TOTAL, 64):
                rows = slice(m, m + 64)
                gate = act_ref[slot, 0, rows, :wide]
                up = act_ref[slot, 1, rows, :wide]
                sigmoid = 0.5 + 0.5 * jnp.tanh(0.5 * gate)
                silu = gate * sigmoid
                hidden_ref[rows, lo:hi] = (silu * up).astype(BF16)
                slopes_ref[rows, HIDDEN + lo : HIDDEN + hi] = silu.astype(BF16)
                slopes_ref[rows, lo:hi] = (up * sigmoid * (1.0 + gate * (1.0 - sigmoid))).astype(BF16)
        lo, hi = CHUNKS[begin][0], CHUNKS[end - 1][1]
        send(hidden_ref, hidden_hbm, lo, hi - lo)
        send(slopes_ref, slopes_hbm, lo, hi - lo)
        send(slopes_ref, slopes_hbm, HIDDEN + lo, hi - lo)
    mixed_copy.wait()
    projected = dot(hidden_ref[...], mixed_ref[...]).astype(BF16)
    out_ref[:, :EMBED] = projected[:SLOTS]
    quarter = EMBED // 4
    stacked = jnp.concatenate(
        [projected[SLOTS:, j * quarter : (j + 1) * quarter] for j in range(4)], axis=0
    )
    out_ref[:, EMBED:] = dot(packer(), stacked).astype(BF16)
    send(out_ref, out_hbm, 0, EMBED + quarter)
    for copy in outgoing:
        copy.wait()


def weighted(chosen, gates):
    return jnp.where(chosen, gates, 0.0)


def split_product(chosen, gates, values):
    whole = weighted(chosen, gates)
    high = whole.astype(BF16)
    low = (whole - high.astype(F32)).astype(BF16)
    return dot_rows(high, values) + dot_rows(low, values)


def embed_kernel(routes_ref, gates_ref, answer_ref, base_ref, embedding_ref, unit_ref):
    main, quarters = choosers(routes_ref[...])
    gates = expanded(pair_gates(routes_ref[...], gates_ref[...]))
    mixture = split_product(main, gates, answer_ref[:, :EMBED])
    extra = jnp.concatenate(
        [split_product(quarters[j], gates, answer_ref[:, EMBED:]) for j in range(4)], axis=1
    )
    embedding = base_ref[...] + mixture + extra
    inverse = lax.rsqrt(jnp.mean(embedding * embedding, axis=1, keepdims=True) + EPSILON)
    embedding_ref[...] = embedding
    unit_ref[...] = (embedding * inverse).astype(BF16)


def loss_kernel(
    routes_ref, gates_ref, matches_ref, partner_ref, embedding_ref, unit_ref, key_ref,
    loss_ref, grad_ref, out_ref,
):
    embedding = embedding_ref[...]
    unit = unit_ref[...]
    keys = key_ref[...]
    coefficient = 1.0 / (EMBED * TEMPER)
    inverse = lax.rsqrt(jnp.mean(embedding * embedding, axis=1, keepdims=True) + EPSILON)
    unit_rows = embedding * inverse
    entry = iota((ROWS, ROWS), 0)

    def scores(rows, columns, matches):
        logits = dot_cols(rows, columns) * coefficient
        totals = jnp.log(jnp.sum(jnp.exp(logits), axis=0, keepdims=True))
        target = matches == entry
        chosen = jnp.sum(jnp.where(target, logits, 0.0), axis=0, keepdims=True)
        weights = jnp.exp(logits - totals) - jnp.where(target, 1.0, 0.0)
        return totals - chosen, weights.astype(BF16)

    loss, own = scores(keys, unit, matches_ref[...])
    loss_ref[...] = loss
    partner = scores(unit, keys, partner_ref[...].astype(jnp.int32))[1]
    upstream = (dot_rows(own, keys) + dot(partner, keys)) * coefficient
    grad = inverse * (upstream - unit_rows * jnp.mean(upstream * unit_rows, axis=1, keepdims=True))
    grad = grad.astype(BF16)
    grad_ref[...] = grad
    main, quarters = choosers(routes_ref[...])
    gates = expanded(pair_gates(routes_ref[...], gates_ref[...]))
    slot_gates = jnp.sum(weighted(main, gates), axis=1, keepdims=True)
    out_ref[:, :EMBED] = (slot_gates * dot(one_hot(main), grad)).astype(BF16)
    quarter = EMBED // 4
    total = jnp.zeros((SLOTS, quarter), F32)
    extra_gates = jnp.zeros((SLOTS, 1), F32)
    for j in range(4):
        total = total + dot(one_hot(quarters[j]), grad[:, j * quarter : (j + 1) * quarter])
        extra_gates = extra_gates + jnp.sum(weighted(quarters[j], gates), axis=1, keepdims=True)
    out_ref[:, EMBED:] = (extra_gates * total).astype(BF16)


def joined_kernel(arrived_ref, mixed_ref, slopes_ref, joined_ref, grads_ref, act_ref):
    quarter = EMBED // 4
    grads_ref[:SLOTS, :] = arrived_ref[:, :EMBED]
    spread = dot(unpacker(), arrived_ref[:, EMBED:]).astype(BF16)
    for j in range(4):
        grads_ref[SLOTS:, j * quarter : (j + 1) * quarter] = spread[j * SPARE : (j + 1) * SPARE]
    for c, (lo, hi) in enumerate(CHUNKS):
        slot = c % 2
        wide = hi - lo
        act_ref[slot, :, :wide] = dot_cols(grads_ref[...], mixed_ref[lo:hi, :])
        for m in range(0, TOTAL, 64):
            hidden_grad = act_ref[slot, m : m + 64, :wide]
            for offset in (0, HIDDEN):
                slope = slopes_ref[m : m + 64, offset + lo : offset + hi].astype(F32)
                joined_ref[m : m + 64, offset + lo : offset + hi] = (hidden_grad * slope).astype(BF16)


def input_kernel(joined_ref, w_ref, out_hbm, extra_ref, out_ref, out_sems):
    step = WIDTH // 4
    outgoing = []

    def send(start, wide, index):
        cols = pl.ds(start, wide)
        copy = pltpu.make_async_copy(out_ref.at[:, cols], out_hbm.at[:, cols], out_sems.at[index])
        copy.start()
        outgoing.append(copy)

    for n in range(0, WIDTH, TILE):
        result = dot_cols(joined_ref[...], w_ref[n : n + TILE, :]).astype(BF16)
        out_ref[:, n : n + TILE] = result[:SLOTS]
        j, within = n // step, n % step
        extra_ref[j * SPARE : (j + 1) * SPARE, within : within + TILE] = result[SLOTS:]
        if n in (WIDTH // 2 - TILE, WIDTH * 3 // 4 - TILE):
            begin = 0 if len(outgoing) == 0 else WIDTH // 2
            send(begin, n + TILE - begin, len(outgoing))
    out_ref[:, WIDTH:] = dot(packer(), extra_ref[...]).astype(BF16)
    send(WIDTH * 3 // 4, 2 * step, 2)
    for copy in outgoing:
        copy.wait()


def head_kernel(
    grads_ref, tokens_ref, embed_grad_ref, hidden_ref, down_ref, own_ref, other_ref
):
    first = lax.axis_index("expert_2") == 0
    inner = dot_rows(hidden_ref[...], grads_ref[...]).astype(BF16)
    for n in range(0, WIDTH, TILE):
        part = dot_rows(down_ref[:, n : n + TILE], inner)
        part = part + dot_rows(tokens_ref[:, n : n + TILE], embed_grad_ref[...])
        for b in range(TILE // 32):
            row = n // 2 + 16 * b
            even, odd = part[32 * b : 32 * b + 16], part[32 * b + 16 : 32 * b + 32]
            own_ref[row : row + 16, :] = jnp.where(first, even, odd)
            other_ref[row : row + 16, :] = jnp.where(first, odd, even).astype(BF16)


def ring_kernel(own_ref, received_ref, *outs):
    place = lax.axis_index("dp")
    for half, near in enumerate((1, 3)):
        kept_ref, sent_ref = outs[2 * half : 2 * half + 2]
        for i, k in enumerate((0, near ^ 2)):
            quarter = jnp.bitwise_xor(place, k)
            kept_ref[i] = own_ref[quarter, half] + received_ref[quarter, half].astype(F32)
        for i, k in enumerate((near, 2)):
            quarter = jnp.bitwise_xor(place, k)
            total = own_ref[quarter, half] + received_ref[quarter, half].astype(F32)
            sent_ref[i] = total.astype(BF16)


def second_kernel(first_ref, first_in_ref, last_ref, last_in_ref, own_ref, sent_first_ref, sent_last_ref):
    own_ref[0] = first_ref[0] + first_in_ref[0].astype(F32)
    own_ref[1] = last_ref[0] + last_in_ref[0].astype(F32)
    sent_first_ref[...] = (first_ref[1] + first_in_ref[1].astype(F32)).astype(BF16)
    sent_last_ref[...] = (last_ref[1] + last_in_ref[1].astype(F32)).astype(BF16)


def combine_kernel(routes_ref, direct_ref, back_hbm, out_ref, back_ref, sems):
    quarter = WIDTH // 4
    copies = []
    for n, j in enumerate((4, 0, 1, 2, 3)):
        cols = pl.ds(j * quarter, quarter)
        copy = pltpu.make_async_copy(back_hbm.at[:, cols], back_ref.at[:, cols], sems.at[n])
        copy.start()
        copies.append(copy)
    main, quarters = choosers(routes_ref[...])
    main = one_hot(main).T
    quarters = [one_hot(chosen).T for chosen in quarters]
    copies[0].wait()
    for j in range(4):
        cols = slice(j * quarter, (j + 1) * quarter)
        extra = dot(quarters[j], back_ref[:, WIDTH:])
        copies[j + 1].wait()
        total = dot(main, back_ref[:, cols]) + extra
        out_ref[:, cols] = (direct_ref[:, cols] + total).astype(BF16)


def call(kernel, outs, ins, scratch=(), flops=0, moved=0, limit=24):
    def spec(space):
        return pl.BlockSpec(memory_space=space)

    return pl.pallas_call(
        kernel,
        out_shape=tuple(jax.ShapeDtypeStruct(shape, dtype) for shape, dtype, _ in outs),
        in_specs=[spec(space) for _, space in ins],
        out_specs=tuple(spec(space) for _, _, space in outs),
        scratch_shapes=scratch,
        compiler_params=pltpu.CompilerParams(vmem_limit_bytes=int(limit * 1048576)),
        cost_estimate=pl.CostEstimate(flops=flops, bytes_accessed=moved, transcendentals=0),
    )(*[value for value, _ in ins])


def exchanged(value, axes, parts):
    rows, width = value.shape
    blocks = value.reshape(parts, rows // parts, width)
    return lax.all_to_all(blocks, axes, 0, 0, tiled=True).reshape(rows, width)


def body(tokens, routes, gates, gate_up, down_proj, projection, matches):
    vmem, hbm = pltpu.VMEM, pl.ANY
    routes, gates = routes.T, gates.T
    weights_joined, weights_down = gate_up[0], down_proj[0]
    partner = [(i, i ^ EXPERTS // 2) for i in range(EXPERTS)]
    dma = pltpu.SemaphoreType.DMA
    wide_shape, packed_shape = (SLOTS, WIDTH * 5 // 4), (SLOTS, EMBED * 5 // 4)

    (dispatch,) = call(
        dispatch_kernel, [(wide_shape, BF16, hbm)], [(routes, hbm), (tokens, hbm)],
        scratch=[
            pltpu.VMEM((TOP, ROWS), jnp.int32),
            pltpu.VMEM((ROWS, WIDTH), BF16),
            pltpu.VMEM(wide_shape, BF16),
            dma((2,)),
            dma((5,)),
        ],
        flops=2 * SLOTS * ROWS * WIDTH * 2, moved=3 << 20, limit=WHOLE,
    )
    partner_matches = lax.ppermute(matches.astype(BF16), EXPERT, partner)
    received = exchanged(dispatch, EXPERT, EXPERTS)
    mixed, base = call(
        prepare_kernel,
        [((HIDDEN, EMBED), BF16, vmem), ((ROWS, EMBED), F32, vmem)],
        [(weights_down, hbm), (projection, hbm), (tokens, hbm)],
        scratch=[
            pltpu.VMEM((HIDDEN, WIDTH), BF16),
            pltpu.VMEM((WIDTH, EMBED), BF16),
            pltpu.VMEM((ROWS, WIDTH), BF16),
            dma((3,)),
        ],
        flops=2 * (HIDDEN + ROWS) * WIDTH * EMBED, moved=8 << 20, limit=WHOLE,
    )
    received, partner_matches, base = lax.optimization_barrier((received, partner_matches, base))

    packed, hidden, slopes = call(
        forward_kernel,
        [(packed_shape, BF16, hbm), ((TOTAL, HIDDEN), BF16, hbm), ((TOTAL, 2 * HIDDEN), BF16, hbm)],
        [(received, hbm), (weights_joined, hbm), (mixed, hbm)],
        scratch=[
            pltpu.VMEM((TOTAL, WIDTH), BF16),
            pltpu.VMEM((SLOTS, WIDTH // 4), BF16),
            pltpu.VMEM((2, 2, TOTAL, 256), F32),
            pltpu.VMEM((WIDTH, 2 * HIDDEN), BF16),
            pltpu.VMEM((HIDDEN, EMBED), BF16),
            pltpu.VMEM((TOTAL, HIDDEN), BF16),
            pltpu.VMEM((TOTAL, 2 * HIDDEN), BF16),
            pltpu.VMEM(packed_shape, BF16),
            dma((9,)),
            dma((10,)),
        ],
        flops=2 * TOTAL * HIDDEN * (2 * WIDTH + EMBED), moved=22 << 20, limit=56.5,
    )
    answer = exchanged(packed, EXPERT, EXPERTS)
    embedding, unit = call(
        embed_kernel,
        [((ROWS, EMBED), F32, vmem), ((ROWS, EMBED), BF16, vmem)],
        [(routes, vmem), (gates, vmem), (answer, vmem), (base, vmem)],
        flops=4 * SLOTS * ROWS * EMBED * 2, moved=2 << 20,
    )
    keys = lax.ppermute(unit, EXPERT, partner)
    row_loss, embed_grad, slot_grads = call(
        loss_kernel,
        [((1, ROWS), F32, vmem), ((ROWS, EMBED), BF16, vmem), (packed_shape, BF16, vmem)],
        [(routes, vmem), (gates, vmem), (matches, vmem), (partner_matches, vmem),
         (embedding, vmem), (unit, vmem), (keys, vmem)],
        flops=20 * 10**9, moved=2 << 20, limit=16,
    )
    arrived = exchanged(slot_grads, EXPERT, EXPERTS)
    joined_shape = (TOTAL, 2 * HIDDEN)
    joined_grad, grads = call(
        joined_kernel,
        [(joined_shape, BF16, vmem), ((TOTAL, EMBED), BF16, vmem)],
        [(arrived, vmem), (mixed, vmem), (slopes, vmem)],
        scratch=[pltpu.VMEM((2, TOTAL, 256), F32)],
        flops=4 * 10**9, moved=8 << 20, limit=16,
    )
    (input_grads,) = call(
        input_kernel,
        [(wide_shape, BF16, hbm)],
        [(joined_grad, vmem), (weights_joined, vmem)],
        scratch=[
            pltpu.VMEM((SLOTS, WIDTH // 4), BF16),
            pltpu.VMEM(wide_shape, BF16),
            dma((3,)),
        ],
        flops=4 * TOTAL * HIDDEN * WIDTH, moved=18 << 20, limit=34,
    )
    back = exchanged(input_grads, EXPERT, EXPERTS)
    direct = dot_cols(embed_grad, projection)
    half_shape = (WIDTH // 2, EMBED)
    own, other = call(
        head_kernel,
        [(half_shape, F32, vmem), (half_shape, BF16, vmem)],
        [(grads, vmem), (tokens, vmem), (embed_grad, vmem), (hidden, vmem), (weights_down, vmem)],
        limit=16,
    )
    other = lax.ppermute(other, "expert_2", [(0, 1), (1, 0)])
    rows = WIDTH // 16

    def around(value, distance):
        return lax.ppermute(value, "dp", [(i, i ^ distance) for i in range(4)])

    kept_first, sent_first, kept_last, sent_last = call(
        ring_kernel,
        [((2, rows, EMBED), F32, vmem), ((2, rows, EMBED), BF16, vmem)] * 2,
        [(value.reshape(4, 2, rows, EMBED), vmem) for value in (own, other)],
        limit=16,
    )
    own, sent_last, sent_first = call(
        second_kernel,
        [((2, rows, EMBED), F32, vmem)] + [((rows, EMBED), BF16, vmem)] * 2,
        [(kept_first, vmem), (around(sent_first, 1), vmem), (kept_last, vmem), (around(sent_last, 3), vmem)],
        limit=16,
    )
    own = own + jnp.stack([around(sent_last, 3), around(sent_first, 1)]).astype(F32)
    back, sums = lax.optimization_barrier((back, own.astype(BF16).reshape(2 * rows, EMBED)))
    parts = lax.all_to_all(
        sums.reshape(16, 16, EMBED), ("expert_0", "expert_1"), 0, 0, tiled=True
    )
    (grad_tokens,) = call(
        combine_kernel, [((ROWS, WIDTH), BF16, vmem)], [(routes, vmem), (direct, vmem), (back, hbm)],
        scratch=[pltpu.VMEM(wide_shape, BF16), dma((5,))],
        flops=2 * SLOTS * ROWS * WIDTH * 2, moved=4 << 20, limit=WHOLE,
    )
    device_count = lax.axis_size("dp") * EXPERTS
    grad_projection = jnp.sum(parts.astype(F32), axis=0) * (1.0 / math.sqrt(ROWS * device_count))
    return grad_tokens, grad_projection, row_loss.reshape(ROWS)


def solution(mesh):
    torus = Mesh(
        mesh.devices.reshape(mesh.shape["dp"], 4, 4, 2), ("dp", "expert_0", "expert_1", "expert_2")
    )
    return jax.shard_map(
        body,
        mesh=torus,
        in_specs=(
            P(DP_EXPERT, None),
            P(DP_EXPERT, None),
            P(DP_EXPERT, None),
            P(EXPERT, None, None),
            P(EXPERT, None, None),
            P(),
            P(DP_EXPERT, None),
        ),
        out_specs=(P(DP_EXPERT, None), P(DP_EXPERT, None), P(DP_EXPERT)),
        check_vma=False,
    )
```

```python
import math

import jax
import jax.numpy as jnp
from jax import lax
from jax.experimental import pallas as pl
from jax.experimental.pallas import tpu as pltpu
from jax.sharding import Mesh
from jax.sharding import PartitionSpec as P

EXPERT = ("expert_0", "expert_1", "expert_2")
DP_EXPERT = ("dp", "expert_0", "expert_1", "expert_2")

TEMPER = 0.1
EPSILON = 1e-06
ROWS = 128
TOP = 4
WIDTH = 2048
HIDDEN = 1408
EMBED = 512
EXPERTS = 32
MAIN = 16
EXTRA = 4
SLOTS = EXPERTS * MAIN
SPARE = EXPERTS * EXTRA
TOTAL = SLOTS + SPARE
CHUNKS = tuple((lo, min(lo + 256, HIDDEN)) for lo in range(0, HIDDEN, 256))
TILE = 256
F32 = jnp.float32
BF16 = jnp.bfloat16
WHOLE = 60


def dot(left, right):
    return jnp.dot(left, right, preferred_element_type=F32)


def dot_rows(left, right):
    return lax.dot_general(left, right, (((0,), (0,)), ((), ())), preferred_element_type=F32)


def dot_cols(left, right):
    return lax.dot_general(left, right, (((1,), (1,)), ((), ())), preferred_element_type=F32)


def iota(shape, dim):
    return lax.broadcasted_iota(jnp.int32, shape, dim)


def expanded(table):
    spread = jnp.broadcast_to(table[:, None, :], (EXPERTS, MAIN, ROWS))
    return spread.reshape(SLOTS, ROWS)


def ranks(routes):
    experts = iota((EXPERTS, ROWS), 0)
    member = jnp.zeros((EXPERTS, ROWS), F32)
    for k in range(TOP):
        member = member + jnp.where(routes[k : k + 1, :] == experts, 1.0, 0.0)
    earlier = jnp.where(iota((ROWS, ROWS), 0) < iota((ROWS, ROWS), 1), 1.0, 0.0)
    rank = dot(member.astype(BF16), earlier.astype(BF16))
    return jnp.where(member > 0.0, rank, -1.0)


def pair_gates(routes, gates):
    experts = iota((EXPERTS, ROWS), 0)
    total = jnp.zeros((EXPERTS, ROWS), F32)
    for k in range(TOP):
        total = total + jnp.where(routes[k : k + 1, :] == experts, gates[k : k + 1, :], 0.0)
    return total


def choosers(routes):
    rank = expanded(ranks(routes))
    place = iota((SLOTS, ROWS), 0) % MAIN
    main = rank == place.astype(F32)
    extra = rank == (MAIN + place % EXTRA).astype(F32)
    quarters = [extra & (place // EXTRA == j) for j in range(MAIN // EXTRA)]
    return main, quarters


def one_hot(chosen):
    return jnp.where(chosen, 1.0, 0.0).astype(BF16)


def unpacker():
    row = iota((SLOTS, SLOTS), 0)
    wanted = (row % SPARE) // EXTRA * MAIN + row // SPARE * EXTRA + row % EXTRA
    return one_hot(iota((SLOTS, SLOTS), 1) == wanted)


def packer():
    row = iota((SLOTS, SLOTS), 0)
    wanted = (row % MAIN) // EXTRA * SPARE + row // MAIN * EXTRA + row % EXTRA
    return one_hot(iota((SLOTS, SLOTS), 1) == wanted)


def dispatch_kernel(routes_hbm, tokens_hbm, out_hbm, routes_ref, tokens_ref, out_ref, sems, out_sems):
    routes_copy = pltpu.make_async_copy(routes_hbm, routes_ref, sems.at[0])
    tokens_copy = pltpu.make_async_copy(tokens_hbm, tokens_ref, sems.at[1])
    routes_copy.start()
    tokens_copy.start()
    routes_copy.wait()
    main, quarters = choosers(routes_ref[...])
    main = one_hot(main)
    quarter = WIDTH // 4
    total = jnp.zeros((SLOTS, quarter), F32)
    tokens_copy.wait()
    outgoing = []
    for j in range(5):
        cols = slice(j * quarter, (j + 1) * quarter)
        if j < 4:
            out_ref[:, cols] = dot(main, tokens_ref[:, cols]).astype(BF16)
            total = total + dot(one_hot(quarters[j]), tokens_ref[:, cols])
        else:
            out_ref[:, cols] = total.astype(BF16)
        part = pl.ds(j * quarter, quarter)
        copy = pltpu.make_async_copy(out_ref.at[:, part], out_hbm.at[:, part], out_sems.at[j])
        copy.start()
        outgoing.append(copy)
    for copy in outgoing:
        copy.wait()


def prepare_kernel(down_hbm, head_hbm, tokens_hbm, mixed_ref, base_ref, down_ref, head_ref, tokens_ref, sems):
    copies = [
        pltpu.make_async_copy(source, target, sems.at[i])
        for i, (source, target) in enumerate(
            ((head_hbm, head_ref), (tokens_hbm, tokens_ref), (down_hbm, down_ref))
        )
    ]
    for copy in copies:
        copy.start()
    copies[0].wait()
    copies[1].wait()
    base_ref[...] = dot(tokens_ref[...], head_ref[...])
    copies[2].wait()
    mixed_ref[...] = dot(down_ref[...], head_ref[...]).astype(BF16)


def forward_kernel(
    recv_hbm, w_hbm, mixed_hbm, out_hbm, hidden_hbm, slopes_hbm,
    x_ref, extra_ref, act_ref, w_ref, mixed_ref, hidden_ref, slopes_ref, out_ref, sems, out_sems,
):
    quarter = WIDTH // 4

    def bring(source, target, index):
        copy = pltpu.make_async_copy(source, target, sems.at[index])
        copy.start()
        return copy

    extra_copy = bring(recv_hbm.at[:, pl.ds(WIDTH, quarter)], extra_ref, 7)
    main_copy = bring(recv_hbm.at[:, pl.ds(0, WIDTH)], x_ref.at[pl.ds(0, SLOTS), :], 8)
    groups = ((0, 1), (1, 3), (3, len(CHUNKS)))

    def bring_group(g):
        begin, end = groups[g]
        lo, hi = CHUNKS[begin][0], CHUNKS[end - 1][1]
        return [
            bring(
                w_hbm.at[:, pl.ds(h * HIDDEN + lo, hi - lo)],
                w_ref.at[:, pl.ds(h * HIDDEN + lo, hi - lo)],
                1 + 2 * g + h,
            )
            for h in range(2)
        ]

    weight_copies = bring_group(0)
    turned = unpacker()
    extra_copy.wait()
    spread = dot(turned, extra_ref[...]).astype(BF16)
    for j in range(4):
        x_ref[SLOTS:, j * quarter : (j + 1) * quarter] = spread[j * SPARE : (j + 1) * SPARE]
    main_copy.wait()
    weight_copies += bring_group(1)
    outgoing = []

    def send(source, target, lo, wide):
        cols = pl.ds(lo, wide)
        copy = pltpu.make_async_copy(source.at[:, cols], target.at[:, cols], out_sems.at[len(outgoing)])
        copy.start()
        outgoing.append(copy)

    for g, (begin, end) in enumerate(groups):
        weight_copies[2 * g].wait()
        weight_copies[2 * g + 1].wait()
        if g == 0:
            weight_copies += bring_group(2)
            mixed_copy = bring(mixed_hbm, mixed_ref, 0)
        for c in range(begin, end):
            lo, hi = CHUNKS[c]
            slot = c % 2
            wide = hi - lo
            act_ref[slot, 0, :, :wide] = dot(x_ref[...], w_ref[:, lo:hi])
            act_ref[slot, 1, :, :wide] = dot(x_ref[...], w_ref[:, HIDDEN + lo : HIDDEN + hi])
            for m in range(0, TOTAL, 64):
                rows = slice(m, m + 64)
                gate = act_ref[slot, 0, rows, :wide]
                up = act_ref[slot, 1, rows, :wide]
                sigmoid = 0.5 + 0.5 * jnp.tanh(0.5 * gate)
                silu = gate * sigmoid
                hidden_ref[rows, lo:hi] = (silu * up).astype(BF16)
                slopes_ref[rows, HIDDEN + lo : HIDDEN + hi] = silu.astype(BF16)
                slopes_ref[rows, lo:hi] = (up * sigmoid * (1.0 + gate * (1.0 - sigmoid))).astype(BF16)
        lo, hi = CHUNKS[begin][0], CHUNKS[end - 1][1]
        send(hidden_ref, hidden_hbm, lo, hi - lo)
        send(slopes_ref, slopes_hbm, lo, hi - lo)
        send(slopes_ref, slopes_hbm, HIDDEN + lo, hi - lo)
    mixed_copy.wait()
    projected = dot(hidden_ref[...], mixed_ref[...]).astype(BF16)
    out_ref[:, :EMBED] = projected[:SLOTS]
    quarter = EMBED // 4
    stacked = jnp.concatenate(
        [projected[SLOTS:, j * quarter : (j + 1) * quarter] for j in range(4)], axis=0
    )
    out_ref[:, EMBED:] = dot(packer(), stacked).astype(BF16)
    send(out_ref, out_hbm, 0, EMBED + quarter)
    for copy in outgoing:
        copy.wait()


def weighted(chosen, gates):
    return jnp.where(chosen, gates, 0.0)


def split_product(chosen, gates, values):
    whole = weighted(chosen, gates)
    high = whole.astype(BF16)
    low = (whole - high.astype(F32)).astype(BF16)
    return dot_rows(high, values) + dot_rows(low, values)


def embed_kernel(routes_ref, gates_ref, answer_ref, base_ref, embedding_ref, unit_ref):
    main, quarters = choosers(routes_ref[...])
    gates = expanded(pair_gates(routes_ref[...], gates_ref[...]))
    mixture = split_product(main, gates, answer_ref[:, :EMBED])
    extra = jnp.concatenate(
        [split_product(quarters[j], gates, answer_ref[:, EMBED:]) for j in range(4)], axis=1
    )
    embedding = base_ref[...] + mixture + extra
    inverse = lax.rsqrt(jnp.mean(embedding * embedding, axis=1, keepdims=True) + EPSILON)
    embedding_ref[...] = embedding
    unit_ref[...] = (embedding * inverse).astype(BF16)


def loss_kernel(
    routes_ref, gates_ref, matches_ref, partner_ref, embedding_ref, unit_ref, key_ref,
    loss_ref, grad_ref, out_ref,
):
    embedding = embedding_ref[...]
    unit = unit_ref[...]
    keys = key_ref[...]
    coefficient = 1.0 / (EMBED * TEMPER)
    inverse = lax.rsqrt(jnp.mean(embedding * embedding, axis=1, keepdims=True) + EPSILON)
    unit_rows = embedding * inverse
    entry = iota((ROWS, ROWS), 0)

    def scores(rows, columns, matches):
        logits = dot_cols(rows, columns) * coefficient
        totals = jnp.log(jnp.sum(jnp.exp(logits), axis=0, keepdims=True))
        target = matches == entry
        chosen = jnp.sum(jnp.where(target, logits, 0.0), axis=0, keepdims=True)
        weights = jnp.exp(logits - totals) - jnp.where(target, 1.0, 0.0)
        return totals - chosen, weights.astype(BF16)

    loss, own = scores(keys, unit, matches_ref[...])
    loss_ref[...] = loss
    partner = scores(unit, keys, partner_ref[...].astype(jnp.int32))[1]
    upstream = (dot_rows(own, keys) + dot(partner, keys)) * coefficient
    grad = inverse * (upstream - unit_rows * jnp.mean(upstream * unit_rows, axis=1, keepdims=True))
    grad = grad.astype(BF16)
    grad_ref[...] = grad
    main, quarters = choosers(routes_ref[...])
    gates = expanded(pair_gates(routes_ref[...], gates_ref[...]))
    slot_gates = jnp.sum(weighted(main, gates), axis=1, keepdims=True)
    out_ref[:, :EMBED] = (slot_gates * dot(one_hot(main), grad)).astype(BF16)
    quarter = EMBED // 4
    total = jnp.zeros((SLOTS, quarter), F32)
    extra_gates = jnp.zeros((SLOTS, 1), F32)
    for j in range(4):
        total = total + dot(one_hot(quarters[j]), grad[:, j * quarter : (j + 1) * quarter])
        extra_gates = extra_gates + jnp.sum(weighted(quarters[j], gates), axis=1, keepdims=True)
    out_ref[:, EMBED:] = (extra_gates * total).astype(BF16)


def joined_kernel(arrived_ref, mixed_ref, slopes_ref, joined_ref, grads_ref, act_ref):
    quarter = EMBED // 4
    grads_ref[:SLOTS, :] = arrived_ref[:, :EMBED]
    spread = dot(unpacker(), arrived_ref[:, EMBED:]).astype(BF16)
    for j in range(4):
        grads_ref[SLOTS:, j * quarter : (j + 1) * quarter] = spread[j * SPARE : (j + 1) * SPARE]
    for c, (lo, hi) in enumerate(CHUNKS):
        slot = c % 2
        wide = hi - lo
        act_ref[slot, :, :wide] = dot_cols(grads_ref[...], mixed_ref[lo:hi, :])
        for m in range(0, TOTAL, 64):
            hidden_grad = act_ref[slot, m : m + 64, :wide]
            for offset in (0, HIDDEN):
                slope = slopes_ref[m : m + 64, offset + lo : offset + hi].astype(F32)
                joined_ref[m : m + 64, offset + lo : offset + hi] = (hidden_grad * slope).astype(BF16)


def input_kernel(joined_ref, w_ref, out_hbm, extra_ref, out_ref, out_sems):
    step = WIDTH // 4
    outgoing = []

    def send(start, wide, index):
        cols = pl.ds(start, wide)
        copy = pltpu.make_async_copy(out_ref.at[:, cols], out_hbm.at[:, cols], out_sems.at[index])
        copy.start()
        outgoing.append(copy)

    for n in range(0, WIDTH, TILE):
        result = dot_cols(joined_ref[...], w_ref[n : n + TILE, :]).astype(BF16)
        out_ref[:, n : n + TILE] = result[:SLOTS]
        j, within = n // step, n % step
        extra_ref[j * SPARE : (j + 1) * SPARE, within : within + TILE] = result[SLOTS:]
        if n in (WIDTH // 2 - TILE, WIDTH * 3 // 4 - TILE):
            begin = 0 if len(outgoing) == 0 else WIDTH // 2
            send(begin, n + TILE - begin, len(outgoing))
    out_ref[:, WIDTH:] = dot(packer(), extra_ref[...]).astype(BF16)
    send(WIDTH * 3 // 4, 2 * step, 2)
    for copy in outgoing:
        copy.wait()


def head_kernel(
    grads_ref, tokens_ref, embed_grad_ref, hidden_ref, down_ref, own_ref, other_ref
):
    first = lax.axis_index("expert_2") == 0
    inner = dot_rows(hidden_ref[...], grads_ref[...]).astype(BF16)
    for n in range(0, WIDTH, TILE):
        part = dot_rows(down_ref[:, n : n + TILE], inner)
        part = part + dot_rows(tokens_ref[:, n : n + TILE], embed_grad_ref[...])
        for b in range(TILE // 32):
            row = n // 2 + 16 * b
            even, odd = part[32 * b : 32 * b + 16], part[32 * b + 16 : 32 * b + 32]
            own_ref[row : row + 16, :] = jnp.where(first, even, odd)
            other_ref[row : row + 16, :] = jnp.where(first, odd, even).astype(BF16)


def ring_kernel(own_ref, received_ref, *outs):
    place = lax.axis_index("dp")
    for half, near in enumerate((1, 3)):
        kept_ref, sent_ref = outs[2 * half : 2 * half + 2]
        for i, k in enumerate((0, near ^ 2)):
            quarter = jnp.bitwise_xor(place, k)
            kept_ref[i] = own_ref[quarter, half] + received_ref[quarter, half].astype(F32)
        for i, k in enumerate((near, 2)):
            quarter = jnp.bitwise_xor(place, k)
            total = own_ref[quarter, half] + received_ref[quarter, half].astype(F32)
            sent_ref[i] = total.astype(BF16)


def second_kernel(first_ref, first_in_ref, last_ref, last_in_ref, own_ref, sent_first_ref, sent_last_ref):
    own_ref[0] = first_ref[0] + first_in_ref[0].astype(F32)
    own_ref[1] = last_ref[0] + last_in_ref[0].astype(F32)
    sent_first_ref[...] = (first_ref[1] + first_in_ref[1].astype(F32)).astype(BF16)
    sent_last_ref[...] = (last_ref[1] + last_in_ref[1].astype(F32)).astype(BF16)


def combine_kernel(routes_ref, direct_ref, back_hbm, out_ref, back_ref, sems):
    quarter = WIDTH // 4
    copies = []
    for n, j in enumerate((4, 0, 1, 2, 3)):
        cols = pl.ds(j * quarter, quarter)
        copy = pltpu.make_async_copy(back_hbm.at[:, cols], back_ref.at[:, cols], sems.at[n])
        copy.start()
        copies.append(copy)
    main, quarters = choosers(routes_ref[...])
    main = one_hot(main).T
    quarters = [one_hot(chosen).T for chosen in quarters]
    copies[0].wait()
    for j in range(4):
        cols = slice(j * quarter, (j + 1) * quarter)
        extra = dot(quarters[j], back_ref[:, WIDTH:])
        copies[j + 1].wait()
        total = dot(main, back_ref[:, cols]) + extra
        out_ref[:, cols] = (direct_ref[:, cols] + total).astype(BF16)


def call(kernel, outs, ins, scratch=(), flops=0, moved=0, limit=24):
    def spec(space):
        return pl.BlockSpec(memory_space=space)

    return pl.pallas_call(
        kernel,
        out_shape=tuple(jax.ShapeDtypeStruct(shape, dtype) for shape, dtype, _ in outs),
        in_specs=[spec(space) for _, space in ins],
        out_specs=tuple(spec(space) for _, _, space in outs),
        scratch_shapes=scratch,
        compiler_params=pltpu.CompilerParams(vmem_limit_bytes=int(limit * 1048576)),
        cost_estimate=pl.CostEstimate(flops=flops, bytes_accessed=moved, transcendentals=0),
    )(*[value for value, _ in ins])


def exchanged(value, axes, parts):
    rows, width = value.shape
    blocks = value.reshape(parts, rows // parts, width)
    return lax.all_to_all(blocks, axes, 0, 0, tiled=True).reshape(rows, width)


def body(tokens, routes, gates, gate_up, down_proj, projection, matches):
    vmem, hbm = pltpu.VMEM, pl.ANY
    routes, gates = routes.T, gates.T
    weights_joined, weights_down = gate_up[0], down_proj[0]
    partner = [(i, i ^ EXPERTS // 2) for i in range(EXPERTS)]
    dma = pltpu.SemaphoreType.DMA
    wide_shape, packed_shape = (SLOTS, WIDTH * 5 // 4), (SLOTS, EMBED * 5 // 4)

    (dispatch,) = call(
        dispatch_kernel, [(wide_shape, BF16, hbm)], [(routes, hbm), (tokens, hbm)],
        scratch=[
            pltpu.VMEM((TOP, ROWS), jnp.int32),
            pltpu.VMEM((ROWS, WIDTH), BF16),
            pltpu.VMEM(wide_shape, BF16),
            dma((2,)),
            dma((5,)),
        ],
        flops=2 * SLOTS * ROWS * WIDTH * 2, moved=3 << 20, limit=WHOLE,
    )
    partner_matches = lax.ppermute(matches.astype(BF16), EXPERT, partner)
    received = exchanged(dispatch, EXPERT, EXPERTS)
    mixed, base = call(
        prepare_kernel,
        [((HIDDEN, EMBED), BF16, vmem), ((ROWS, EMBED), F32, vmem)],
        [(weights_down, hbm), (projection, hbm), (tokens, hbm)],
        scratch=[
            pltpu.VMEM((HIDDEN, WIDTH), BF16),
            pltpu.VMEM((WIDTH, EMBED), BF16),
            pltpu.VMEM((ROWS, WIDTH), BF16),
            dma((3,)),
        ],
        flops=2 * (HIDDEN + ROWS) * WIDTH * EMBED, moved=8 << 20, limit=WHOLE,
    )
    received, partner_matches, base = lax.optimization_barrier((received, partner_matches, base))

    packed, hidden, slopes = call(
        forward_kernel,
        [(packed_shape, BF16, hbm), ((TOTAL, HIDDEN), BF16, hbm), ((TOTAL, 2 * HIDDEN), BF16, hbm)],
        [(received, hbm), (weights_joined, hbm), (mixed, hbm)],
        scratch=[
            pltpu.VMEM((TOTAL, WIDTH), BF16),
            pltpu.VMEM((SLOTS, WIDTH // 4), BF16),
            pltpu.VMEM((2, 2, TOTAL, 256), F32),
            pltpu.VMEM((WIDTH, 2 * HIDDEN), BF16),
            pltpu.VMEM((HIDDEN, EMBED), BF16),
            pltpu.VMEM((TOTAL, HIDDEN), BF16),
            pltpu.VMEM((TOTAL, 2 * HIDDEN), BF16),
            pltpu.VMEM(packed_shape, BF16),
            dma((9,)),
            dma((10,)),
        ],
        flops=2 * TOTAL * HIDDEN * (2 * WIDTH + EMBED), moved=22 << 20, limit=56.5,
    )
    answer = exchanged(packed, EXPERT, EXPERTS)
    embedding, unit = call(
        embed_kernel,
        [((ROWS, EMBED), F32, vmem), ((ROWS, EMBED), BF16, vmem)],
        [(routes, vmem), (gates, vmem), (answer, vmem), (base, vmem)],
        flops=4 * SLOTS * ROWS * EMBED * 2, moved=2 << 20,
    )
    keys = lax.ppermute(unit, EXPERT, partner)
    row_loss, embed_grad, slot_grads = call(
        loss_kernel,
        [((1, ROWS), F32, vmem), ((ROWS, EMBED), BF16, vmem), (packed_shape, BF16, vmem)],
        [(routes, vmem), (gates, vmem), (matches, vmem), (partner_matches, vmem),
         (embedding, vmem), (unit, vmem), (keys, vmem)],
        flops=20 * 10**9, moved=2 << 20, limit=16,
    )
    arrived = exchanged(slot_grads, EXPERT, EXPERTS)
    joined_shape = (TOTAL, 2 * HIDDEN)
    joined_grad, grads = call(
        joined_kernel,
        [(joined_shape, BF16, vmem), ((TOTAL, EMBED), BF16, vmem)],
        [(arrived, vmem), (mixed, vmem), (slopes, vmem)],
        scratch=[pltpu.VMEM((2, TOTAL, 256), F32)],
        flops=4 * 10**9, moved=8 << 20, limit=16,
    )
    (input_grads,) = call(
        input_kernel,
        [(wide_shape, BF16, hbm)],
        [(joined_grad, vmem), (weights_joined, vmem)],
        scratch=[
            pltpu.VMEM((SLOTS, WIDTH // 4), BF16),
            pltpu.VMEM(wide_shape, BF16),
            dma((3,)),
        ],
        flops=4 * TOTAL * HIDDEN * WIDTH, moved=18 << 20, limit=34,
    )
    back = exchanged(input_grads, EXPERT, EXPERTS)
    direct = dot_cols(embed_grad, projection)
    half_shape = (WIDTH // 2, EMBED)
    own, other = call(
        head_kernel,
        [(half_shape, F32, vmem), (half_shape, BF16, vmem)],
        [(grads, vmem), (tokens, vmem), (embed_grad, vmem), (hidden, vmem), (weights_down, vmem)],
        limit=16,
    )
    other = lax.ppermute(other, "expert_2", [(0, 1), (1, 0)])
    rows = WIDTH // 16

    def around(value, distance):
        return lax.ppermute(value, "dp", [(i, i ^ distance) for i in range(4)])

    kept_first, sent_first, kept_last, sent_last = call(
        ring_kernel,
        [((2, rows, EMBED), F32, vmem), ((2, rows, EMBED), BF16, vmem)] * 2,
        [(value.reshape(4, 2, rows, EMBED), vmem) for value in (own, other)],
        limit=16,
    )
    own, sent_last, sent_first = call(
        second_kernel,
        [((2, rows, EMBED), F32, vmem)] + [((rows, EMBED), BF16, vmem)] * 2,
        [(kept_first, vmem), (around(sent_first, 1), vmem), (kept_last, vmem), (around(sent_last, 3), vmem)],
        limit=16,
    )
    own = own + jnp.stack([around(sent_last, 3), around(sent_first, 1)]).astype(F32)
    back, sums = lax.optimization_barrier((back, own.astype(BF16).reshape(2 * rows, EMBED)))
    parts = lax.all_to_all(
        sums.reshape(16, 16, EMBED), ("expert_0", "expert_1"), 0, 0, tiled=True
    )
    (grad_tokens,) = call(
        combine_kernel, [((ROWS, WIDTH), BF16, vmem)], [(routes, vmem), (direct, vmem), (back, hbm)],
        scratch=[pltpu.VMEM(wide_shape, BF16), dma((5,))],
        flops=2 * SLOTS * ROWS * WIDTH * 2, moved=4 << 20, limit=WHOLE,
    )
    device_count = lax.axis_size("dp") * EXPERTS
    grad_projection = jnp.sum(parts.astype(F32), axis=0) * (1.0 / math.sqrt(ROWS * device_count))
    return grad_tokens, grad_projection, row_loss.reshape(ROWS)


def solution(mesh):
    torus = Mesh(
        mesh.devices.reshape(mesh.shape["dp"], 4, 4, 2), ("dp", "expert_0", "expert_1", "expert_2")
    )
    return jax.shard_map(
        body,
        mesh=torus,
        in_specs=(
            P(DP_EXPERT, None),
            P(DP_EXPERT, None),
            P(DP_EXPERT, None),
            P(EXPERT, None, None),
            P(EXPERT, None, None),
            P(),
            P(DP_EXPERT, None),
        ),
        out_specs=(P(DP_EXPERT, None), P(DP_EXPERT, None), P(DP_EXPERT)),
        check_vma=False,
    )
```

```python
import math

import jax
import jax.numpy as jnp
from jax import lax
from jax.experimental import pallas as pl
from jax.experimental.pallas import tpu as pltpu
from jax.sharding import Mesh
from jax.sharding import PartitionSpec as P

EXPERT = ("expert_0", "expert_1", "expert_2")
DP_EXPERT = ("dp", "expert_0", "expert_1", "expert_2")

TEMPER = 0.1
EPSILON = 1e-06
ROWS = 128
TOP = 4
WIDTH = 2048
HIDDEN = 1408
EMBED = 512
EXPERTS = 32
MAIN = 16
EXTRA = 4
SLOTS = EXPERTS * MAIN
SPARE = EXPERTS * EXTRA
TOTAL = SLOTS + SPARE
CHUNKS = tuple((lo, min(lo + 256, HIDDEN)) for lo in range(0, HIDDEN, 256))
TILE = 256
F32 = jnp.float32
BF16 = jnp.bfloat16
WHOLE = 60


def dot(left, right):
    return jnp.dot(left, right, preferred_element_type=F32)


def dot_rows(left, right):
    return lax.dot_general(left, right, (((0,), (0,)), ((), ())), preferred_element_type=F32)


def dot_cols(left, right):
    return lax.dot_general(left, right, (((1,), (1,)), ((), ())), preferred_element_type=F32)


def iota(shape, dim):
    return lax.broadcasted_iota(jnp.int32, shape, dim)


def expanded(table):
    spread = jnp.broadcast_to(table[:, None, :], (EXPERTS, MAIN, ROWS))
    return spread.reshape(SLOTS, ROWS)


def ranks(routes):
    experts = iota((EXPERTS, ROWS), 0)
    member = jnp.zeros((EXPERTS, ROWS), F32)
    for k in range(TOP):
        member = member + jnp.where(routes[k : k + 1, :] == experts, 1.0, 0.0)
    earlier = jnp.where(iota((ROWS, ROWS), 0) < iota((ROWS, ROWS), 1), 1.0, 0.0)
    rank = dot(member.astype(BF16), earlier.astype(BF16))
    return jnp.where(member > 0.0, rank, -1.0)


def pair_gates(routes, gates):
    experts = iota((EXPERTS, ROWS), 0)
    total = jnp.zeros((EXPERTS, ROWS), F32)
    for k in range(TOP):
        total = total + jnp.where(routes[k : k + 1, :] == experts, gates[k : k + 1, :], 0.0)
    return total


def choosers(routes):
    rank = expanded(ranks(routes))
    place = iota((SLOTS, ROWS), 0) % MAIN
    main = rank == place.astype(F32)
    extra = rank == (MAIN + place % EXTRA).astype(F32)
    quarters = [extra & (place // EXTRA == j) for j in range(MAIN // EXTRA)]
    return main, quarters


def one_hot(chosen):
    return jnp.where(chosen, 1.0, 0.0).astype(BF16)


def unpacker():
    row = iota((SLOTS, SLOTS), 0)
    wanted = (row % SPARE) // EXTRA * MAIN + row // SPARE * EXTRA + row % EXTRA
    return one_hot(iota((SLOTS, SLOTS), 1) == wanted)


def packer():
    row = iota((SLOTS, SLOTS), 0)
    wanted = (row % MAIN) // EXTRA * SPARE + row // MAIN * EXTRA + row % EXTRA
    return one_hot(iota((SLOTS, SLOTS), 1) == wanted)


def dispatch_kernel(routes_hbm, tokens_hbm, out_hbm, routes_ref, tokens_ref, out_ref, sems, out_sems):
    routes_copy = pltpu.make_async_copy(routes_hbm, routes_ref, sems.at[0])
    tokens_copy = pltpu.make_async_copy(tokens_hbm, tokens_ref, sems.at[1])
    routes_copy.start()
    tokens_copy.start()
    routes_copy.wait()
    main, quarters = choosers(routes_ref[...])
    main = one_hot(main)
    quarter = WIDTH // 4
    total = jnp.zeros((SLOTS, quarter), F32)
    tokens_copy.wait()
    outgoing = []
    for j in range(5):
        cols = slice(j * quarter, (j + 1) * quarter)
        if j < 4:
            out_ref[:, cols] = dot(main, tokens_ref[:, cols]).astype(BF16)
            total = total + dot(one_hot(quarters[j]), tokens_ref[:, cols])
        else:
            out_ref[:, cols] = total.astype(BF16)
        part = pl.ds(j * quarter, quarter)
        copy = pltpu.make_async_copy(out_ref.at[:, part], out_hbm.at[:, part], out_sems.at[j])
        copy.start()
        outgoing.append(copy)
    for copy in outgoing:
        copy.wait()


def prepare_kernel(down_hbm, head_hbm, tokens_hbm, mixed_ref, base_ref, down_ref, head_ref, tokens_ref, sems):
    copies = [
        pltpu.make_async_copy(source, target, sems.at[i])
        for i, (source, target) in enumerate(
            ((head_hbm, head_ref), (tokens_hbm, tokens_ref), (down_hbm, down_ref))
        )
    ]
    for copy in copies:
        copy.start()
    copies[0].wait()
    copies[1].wait()
    base_ref[...] = dot(tokens_ref[...], head_ref[...])
    copies[2].wait()
    mixed_ref[...] = dot(down_ref[...], head_ref[...]).astype(BF16)


def forward_kernel(
    recv_hbm, w_hbm, mixed_hbm, out_hbm, hidden_hbm, slopes_hbm,
    x_ref, extra_ref, act_ref, w_ref, mixed_ref, hidden_ref, slopes_ref, out_ref, sems, out_sems,
):
    quarter = WIDTH // 4

    def bring(source, target, index):
        copy = pltpu.make_async_copy(source, target, sems.at[index])
        copy.start()
        return copy

    extra_copy = bring(recv_hbm.at[:, pl.ds(WIDTH, quarter)], extra_ref, 7)
    main_copy = bring(recv_hbm.at[:, pl.ds(0, WIDTH)], x_ref.at[pl.ds(0, SLOTS), :], 8)
    groups = ((0, 1), (1, 3), (3, len(CHUNKS)))
    weight_copies = []
    for g, (begin, end) in enumerate(groups):
        lo, hi = CHUNKS[begin][0], CHUNKS[end - 1][1]
        for h in range(2):
            cols = pl.ds(h * HIDDEN + lo, hi - lo)
            weight_copies.append(bring(w_hbm.at[:, cols], w_ref.at[:, cols], 1 + 2 * g + h))
    mixed_copy = bring(mixed_hbm, mixed_ref, 0)
    turned = unpacker()
    extra_copy.wait()
    spread = dot(turned, extra_ref[...]).astype(BF16)
    for j in range(4):
        x_ref[SLOTS:, j * quarter : (j + 1) * quarter] = spread[j * SPARE : (j + 1) * SPARE]
    main_copy.wait()
    outgoing = []

    def send(source, target, lo, wide):
        cols = pl.ds(lo, wide)
        copy = pltpu.make_async_copy(source.at[:, cols], target.at[:, cols], out_sems.at[len(outgoing)])
        copy.start()
        outgoing.append(copy)

    for g, (begin, end) in enumerate(groups):
        weight_copies[2 * g].wait()
        weight_copies[2 * g + 1].wait()
        for c in range(begin, end):
            lo, hi = CHUNKS[c]
            slot = c % 2
            wide = hi - lo
            act_ref[slot, 0, :, :wide] = dot(x_ref[...], w_ref[:, lo:hi])
            act_ref[slot, 1, :, :wide] = dot(x_ref[...], w_ref[:, HIDDEN + lo : HIDDEN + hi])
            for m in range(0, TOTAL, 64):
                rows = slice(m, m + 64)
                gate = act_ref[slot, 0, rows, :wide]
                up = act_ref[slot, 1, rows, :wide]
                sigmoid = 0.5 + 0.5 * jnp.tanh(0.5 * gate)
                silu = gate * sigmoid
                hidden_ref[rows, lo:hi] = (silu * up).astype(BF16)
                slopes_ref[rows, HIDDEN + lo : HIDDEN + hi] = silu.astype(BF16)
                slopes_ref[rows, lo:hi] = (up * sigmoid * (1.0 + gate * (1.0 - sigmoid))).astype(BF16)
        lo, hi = CHUNKS[begin][0], CHUNKS[end - 1][1]
        send(hidden_ref, hidden_hbm, lo, hi - lo)
        send(slopes_ref, slopes_hbm, lo, hi - lo)
        send(slopes_ref, slopes_hbm, HIDDEN + lo, hi - lo)
    mixed_copy.wait()
    projected = dot(hidden_ref[...], mixed_ref[...]).astype(BF16)
    out_ref[:, :EMBED] = projected[:SLOTS]
    quarter = EMBED // 4
    stacked = jnp.concatenate(
        [projected[SLOTS:, j * quarter : (j + 1) * quarter] for j in range(4)], axis=0
    )
    out_ref[:, EMBED:] = dot(packer(), stacked).astype(BF16)
    send(out_ref, out_hbm, 0, EMBED + quarter)
    for copy in outgoing:
        copy.wait()


def weighted(chosen, gates):
    return jnp.where(chosen, gates, 0.0)


def split_product(chosen, gates, values):
    whole = weighted(chosen, gates)
    high = whole.astype(BF16)
    low = (whole - high.astype(F32)).astype(BF16)
    return dot_rows(high, values) + dot_rows(low, values)


def embed_kernel(routes_ref, gates_ref, answer_ref, base_ref, embedding_ref, unit_ref):
    main, quarters = choosers(routes_ref[...])
    gates = expanded(pair_gates(routes_ref[...], gates_ref[...]))
    mixture = split_product(main, gates, answer_ref[:, :EMBED])
    extra = jnp.concatenate(
        [split_product(quarters[j], gates, answer_ref[:, EMBED:]) for j in range(4)], axis=1
    )
    embedding = base_ref[...] + mixture + extra
    inverse = lax.rsqrt(jnp.mean(embedding * embedding, axis=1, keepdims=True) + EPSILON)
    embedding_ref[...] = embedding
    unit_ref[...] = (embedding * inverse).astype(BF16)


def loss_kernel(
    routes_ref, gates_ref, matches_ref, partner_ref, embedding_ref, unit_ref, key_ref,
    loss_ref, grad_ref, out_ref,
):
    embedding = embedding_ref[...]
    unit = unit_ref[...]
    keys = key_ref[...]
    coefficient = 1.0 / (EMBED * TEMPER)
    inverse = lax.rsqrt(jnp.mean(embedding * embedding, axis=1, keepdims=True) + EPSILON)
    unit_rows = embedding * inverse
    entry = iota((ROWS, ROWS), 0)

    def scores(rows, columns, matches):
        logits = dot_cols(rows, columns) * coefficient
        totals = jnp.log(jnp.sum(jnp.exp(logits), axis=0, keepdims=True))
        target = matches == entry
        chosen = jnp.sum(jnp.where(target, logits, 0.0), axis=0, keepdims=True)
        weights = jnp.exp(logits - totals) - jnp.where(target, 1.0, 0.0)
        return totals - chosen, weights.astype(BF16)

    loss, own = scores(keys, unit, matches_ref[...])
    loss_ref[...] = loss
    partner = scores(unit, keys, partner_ref[...].astype(jnp.int32))[1]
    upstream = (dot_rows(own, keys) + dot(partner, keys)) * coefficient
    grad = inverse * (upstream - unit_rows * jnp.mean(upstream * unit_rows, axis=1, keepdims=True))
    grad = grad.astype(BF16)
    grad_ref[...] = grad
    main, quarters = choosers(routes_ref[...])
    gates = expanded(pair_gates(routes_ref[...], gates_ref[...]))
    slot_gates = jnp.sum(weighted(main, gates), axis=1, keepdims=True)
    out_ref[:, :EMBED] = (slot_gates * dot(one_hot(main), grad)).astype(BF16)
    quarter = EMBED // 4
    total = jnp.zeros((SLOTS, quarter), F32)
    extra_gates = jnp.zeros((SLOTS, 1), F32)
    for j in range(4):
        total = total + dot(one_hot(quarters[j]), grad[:, j * quarter : (j + 1) * quarter])
        extra_gates = extra_gates + jnp.sum(weighted(quarters[j], gates), axis=1, keepdims=True)
    out_ref[:, EMBED:] = (extra_gates * total).astype(BF16)


def joined_kernel(arrived_ref, mixed_ref, slopes_ref, joined_ref, grads_ref, act_ref):
    quarter = EMBED // 4
    grads_ref[:SLOTS, :] = arrived_ref[:, :EMBED]
    spread = dot(unpacker(), arrived_ref[:, EMBED:]).astype(BF16)
    for j in range(4):
        grads_ref[SLOTS:, j * quarter : (j + 1) * quarter] = spread[j * SPARE : (j + 1) * SPARE]
    for c, (lo, hi) in enumerate(CHUNKS):
        slot = c % 2
        wide = hi - lo
        act_ref[slot, :, :wide] = dot_cols(grads_ref[...], mixed_ref[lo:hi, :])
        for m in range(0, TOTAL, 64):
            hidden_grad = act_ref[slot, m : m + 64, :wide]
            for offset in (0, HIDDEN):
                slope = slopes_ref[m : m + 64, offset + lo : offset + hi].astype(F32)
                joined_ref[m : m + 64, offset + lo : offset + hi] = (hidden_grad * slope).astype(BF16)


def input_kernel(joined_ref, w_ref, out_hbm, extra_ref, out_ref, out_sems):
    step = WIDTH // 4
    outgoing = []

    def send(start, wide, index):
        cols = pl.ds(start, wide)
        copy = pltpu.make_async_copy(out_ref.at[:, cols], out_hbm.at[:, cols], out_sems.at[index])
        copy.start()
        outgoing.append(copy)

    for n in range(0, WIDTH, TILE):
        result = dot_cols(joined_ref[...], w_ref[n : n + TILE, :]).astype(BF16)
        out_ref[:, n : n + TILE] = result[:SLOTS]
        j, within = n // step, n % step
        extra_ref[j * SPARE : (j + 1) * SPARE, within : within + TILE] = result[SLOTS:]
        if n in (WIDTH // 2 - TILE, WIDTH * 3 // 4 - TILE):
            begin = 0 if len(outgoing) == 0 else WIDTH // 2
            send(begin, n + TILE - begin, len(outgoing))
    out_ref[:, WIDTH:] = dot(packer(), extra_ref[...]).astype(BF16)
    send(WIDTH * 3 // 4, 2 * step, 2)
    for copy in outgoing:
        copy.wait()


def head_kernel(
    grads_ref, tokens_ref, embed_grad_ref, hidden_ref, down_ref, own_ref, other_ref
):
    first = lax.axis_index("expert_2") == 0
    inner = dot_rows(hidden_ref[...], grads_ref[...]).astype(BF16)
    for n in range(0, WIDTH, TILE):
        part = dot_rows(down_ref[:, n : n + TILE], inner)
        part = part + dot_rows(tokens_ref[:, n : n + TILE], embed_grad_ref[...])
        for b in range(TILE // 32):
            row = n // 2 + 16 * b
            even, odd = part[32 * b : 32 * b + 16], part[32 * b + 16 : 32 * b + 32]
            own_ref[row : row + 16, :] = jnp.where(first, even, odd)
            other_ref[row : row + 16, :] = jnp.where(first, odd, even).astype(BF16)


def ring_kernel(own_ref, received_ref, *outs):
    place = lax.axis_index("dp")
    for half, near in enumerate((1, 3)):
        kept_ref, sent_ref = outs[2 * half : 2 * half + 2]
        for i, k in enumerate((0, near ^ 2)):
            quarter = jnp.bitwise_xor(place, k)
            kept_ref[i] = own_ref[quarter, half] + received_ref[quarter, half].astype(F32)
        for i, k in enumerate((near, 2)):
            quarter = jnp.bitwise_xor(place, k)
            total = own_ref[quarter, half] + received_ref[quarter, half].astype(F32)
            sent_ref[i] = total.astype(BF16)


def second_kernel(first_ref, first_in_ref, last_ref, last_in_ref, own_ref, sent_first_ref, sent_last_ref):
    own_ref[0] = first_ref[0] + first_in_ref[0].astype(F32)
    own_ref[1] = last_ref[0] + last_in_ref[0].astype(F32)
    sent_first_ref[...] = (first_ref[1] + first_in_ref[1].astype(F32)).astype(BF16)
    sent_last_ref[...] = (last_ref[1] + last_in_ref[1].astype(F32)).astype(BF16)


def combine_kernel(routes_ref, direct_ref, back_hbm, out_ref, back_ref, sems):
    quarter = WIDTH // 4
    copies = []
    for n, j in enumerate((4, 0, 1, 2, 3)):
        cols = pl.ds(j * quarter, quarter)
        copy = pltpu.make_async_copy(back_hbm.at[:, cols], back_ref.at[:, cols], sems.at[n])
        copy.start()
        copies.append(copy)
    main, quarters = choosers(routes_ref[...])
    main = one_hot(main).T
    quarters = [one_hot(chosen).T for chosen in quarters]
    copies[0].wait()
    for j in range(4):
        cols = slice(j * quarter, (j + 1) * quarter)
        extra = dot(quarters[j], back_ref[:, WIDTH:])
        copies[j + 1].wait()
        total = dot(main, back_ref[:, cols]) + extra
        out_ref[:, cols] = (direct_ref[:, cols] + total).astype(BF16)


def call(kernel, outs, ins, scratch=(), flops=0, moved=0, limit=24):
    def spec(space):
        return pl.BlockSpec(memory_space=space)

    return pl.pallas_call(
        kernel,
        out_shape=tuple(jax.ShapeDtypeStruct(shape, dtype) for shape, dtype, _ in outs),
        in_specs=[spec(space) for _, space in ins],
        out_specs=tuple(spec(space) for _, _, space in outs),
        scratch_shapes=scratch,
        compiler_params=pltpu.CompilerParams(vmem_limit_bytes=int(limit * 1048576)),
        cost_estimate=pl.CostEstimate(flops=flops, bytes_accessed=moved, transcendentals=0),
    )(*[value for value, _ in ins])


def exchanged(value, axes, parts):
    rows, width = value.shape
    blocks = value.reshape(parts, rows // parts, width)
    return lax.all_to_all(blocks, axes, 0, 0, tiled=True).reshape(rows, width)


def body(tokens, routes, gates, gate_up, down_proj, projection, matches):
    vmem, hbm = pltpu.VMEM, pl.ANY
    routes, gates = routes.T, gates.T
    weights_joined, weights_down = gate_up[0], down_proj[0]
    partner = [(i, i ^ EXPERTS // 2) for i in range(EXPERTS)]
    dma = pltpu.SemaphoreType.DMA
    wide_shape, packed_shape = (SLOTS, WIDTH * 5 // 4), (SLOTS, EMBED * 5 // 4)

    (dispatch,) = call(
        dispatch_kernel, [(wide_shape, BF16, hbm)], [(routes, hbm), (tokens, hbm)],
        scratch=[
            pltpu.VMEM((TOP, ROWS), jnp.int32),
            pltpu.VMEM((ROWS, WIDTH), BF16),
            pltpu.VMEM(wide_shape, BF16),
            dma((2,)),
            dma((5,)),
        ],
        flops=2 * SLOTS * ROWS * WIDTH * 2, moved=3 << 20, limit=WHOLE,
    )
    partner_matches = lax.ppermute(matches.astype(BF16), EXPERT, partner)
    received = exchanged(dispatch, EXPERT, EXPERTS)
    mixed, base = call(
        prepare_kernel,
        [((HIDDEN, EMBED), BF16, vmem), ((ROWS, EMBED), F32, vmem)],
        [(weights_down, hbm), (projection, hbm), (tokens, hbm)],
        scratch=[
            pltpu.VMEM((HIDDEN, WIDTH), BF16),
            pltpu.VMEM((WIDTH, EMBED), BF16),
            pltpu.VMEM((ROWS, WIDTH), BF16),
            dma((3,)),
        ],
        flops=2 * (HIDDEN + ROWS) * WIDTH * EMBED, moved=8 << 20, limit=WHOLE,
    )
    received, partner_matches, base = lax.optimization_barrier((received, partner_matches, base))

    packed, hidden, slopes = call(
        forward_kernel,
        [(packed_shape, BF16, hbm), ((TOTAL, HIDDEN), BF16, hbm), ((TOTAL, 2 * HIDDEN), BF16, hbm)],
        [(received, hbm), (weights_joined, hbm), (mixed, hbm)],
        scratch=[
            pltpu.VMEM((TOTAL, WIDTH), BF16),
            pltpu.VMEM((SLOTS, WIDTH // 4), BF16),
            pltpu.VMEM((2, 2, TOTAL, 256), F32),
            pltpu.VMEM((WIDTH, 2 * HIDDEN), BF16),
            pltpu.VMEM((HIDDEN, EMBED), BF16),
            pltpu.VMEM((TOTAL, HIDDEN), BF16),
            pltpu.VMEM((TOTAL, 2 * HIDDEN), BF16),
            pltpu.VMEM(packed_shape, BF16),
            dma((9,)),
            dma((10,)),
        ],
        flops=2 * TOTAL * HIDDEN * (2 * WIDTH + EMBED), moved=22 << 20, limit=49,
    )
    answer = exchanged(packed, EXPERT, EXPERTS)
    embedding, unit = call(
        embed_kernel,
        [((ROWS, EMBED), F32, vmem), ((ROWS, EMBED), BF16, vmem)],
        [(routes, vmem), (gates, vmem), (answer, vmem), (base, vmem)],
        flops=4 * SLOTS * ROWS * EMBED * 2, moved=2 << 20,
    )
    keys = lax.ppermute(unit, EXPERT, partner)
    row_loss, embed_grad, slot_grads = call(
        loss_kernel,
        [((1, ROWS), F32, vmem), ((ROWS, EMBED), BF16, vmem), (packed_shape, BF16, vmem)],
        [(routes, vmem), (gates, vmem), (matches, vmem), (partner_matches, vmem),
         (embedding, vmem), (unit, vmem), (keys, vmem)],
        flops=20 * 10**9, moved=2 << 20, limit=16,
    )
    arrived = exchanged(slot_grads, EXPERT, EXPERTS)
    joined_shape = (TOTAL, 2 * HIDDEN)
    joined_grad, grads = call(
        joined_kernel,
        [(joined_shape, BF16, vmem), ((TOTAL, EMBED), BF16, vmem)],
        [(arrived, vmem), (mixed, vmem), (slopes, vmem)],
        scratch=[pltpu.VMEM((2, TOTAL, 256), F32)],
        flops=4 * 10**9, moved=8 << 20, limit=16,
    )
    (input_grads,) = call(
        input_kernel,
        [(wide_shape, BF16, hbm)],
        [(joined_grad, vmem), (weights_joined, vmem)],
        scratch=[
            pltpu.VMEM((SLOTS, WIDTH // 4), BF16),
            pltpu.VMEM(wide_shape, BF16),
            dma((3,)),
        ],
        flops=4 * TOTAL * HIDDEN * WIDTH, moved=18 << 20, limit=34,
    )
    back = exchanged(input_grads, EXPERT, EXPERTS)
    direct = dot_cols(embed_grad, projection)
    half_shape = (WIDTH // 2, EMBED)
    own, other = call(
        head_kernel,
        [(half_shape, F32, vmem), (half_shape, BF16, vmem)],
        [(grads, vmem), (tokens, vmem), (embed_grad, vmem), (hidden, vmem), (weights_down, vmem)],
        limit=16,
    )
    other = lax.ppermute(other, "expert_2", [(0, 1), (1, 0)])
    rows = WIDTH // 16

    def around(value, distance):
        return lax.ppermute(value, "dp", [(i, i ^ distance) for i in range(4)])

    kept_first, sent_first, kept_last, sent_last = call(
        ring_kernel,
        [((2, rows, EMBED), F32, vmem), ((2, rows, EMBED), BF16, vmem)] * 2,
        [(value.reshape(4, 2, rows, EMBED), vmem) for value in (own, other)],
        limit=16,
    )
    own, sent_last, sent_first = call(
        second_kernel,
        [((2, rows, EMBED), F32, vmem)] + [((rows, EMBED), BF16, vmem)] * 2,
        [(kept_first, vmem), (around(sent_first, 1), vmem), (kept_last, vmem), (around(sent_last, 3), vmem)],
        limit=16,
    )
    own = own + jnp.stack([around(sent_last, 3), around(sent_first, 1)]).astype(F32)
    back, sums = lax.optimization_barrier((back, own.astype(BF16).reshape(2 * rows, EMBED)))
    parts = lax.all_to_all(
        sums.reshape(16, 16, EMBED), ("expert_0", "expert_1"), 0, 0, tiled=True
    )
    (grad_tokens,) = call(
        combine_kernel, [((ROWS, WIDTH), BF16, vmem)], [(routes, vmem), (direct, vmem), (back, hbm)],
        scratch=[pltpu.VMEM(wide_shape, BF16), dma((5,))],
        flops=2 * SLOTS * ROWS * WIDTH * 2, moved=4 << 20, limit=WHOLE,
    )
    device_count = lax.axis_size("dp") * EXPERTS
    grad_projection = jnp.sum(parts.astype(F32), axis=0) * (1.0 / math.sqrt(ROWS * device_count))
    return grad_tokens, grad_projection, row_loss.reshape(ROWS)


def solution(mesh):
    torus = Mesh(
        mesh.devices.reshape(mesh.shape["dp"], 4, 4, 2), ("dp", "expert_0", "expert_1", "expert_2")
    )
    return jax.shard_map(
        body,
        mesh=torus,
        in_specs=(
            P(DP_EXPERT, None),
            P(DP_EXPERT, None),
            P(DP_EXPERT, None),
            P(EXPERT, None, None),
            P(EXPERT, None, None),
            P(),
            P(DP_EXPERT, None),
        ),
        out_specs=(P(DP_EXPERT, None), P(DP_EXPERT, None), P(DP_EXPERT)),
        check_vma=False,
    )
```
